32 devices in a mesh: seq: 16 (over z, y, x), fsdp: 2 (over core).
Axes of the slice: x: 2, y: 2, z: 4, core: 2. Of those that a mesh axis runs over, the one named last changes fastest.
Arguments:
- tokens: float32 [8192, 2048], P(('seq', 'fsdp')), may hold values from -16 to 16
- cotangent: float32 [8192, 2048], P(('seq', 'fsdp')), may hold values from -6 to 6
- gate_proj: bfloat16 [2048, 2560], P('fsdp'), may hold values from -0.125 to 0.125
- input_proj: bfloat16 [2048, 2560], P('fsdp'), may hold values from -0.125 to 0.125
- output_proj: bfloat16 [2560, 2048], P('fsdp'), may hold values from -0.25 to 0.25
- mlp_gate: bfloat16 [2048, 6144], P('fsdp'), may hold values from -0.125 to 0.125
- mlp_up: bfloat16 [2048, 6144], P('fsdp'), may hold values from -0.125 to 0.125
- mlp_down: bfloat16 [6144, 2048], P('fsdp'), may hold values from -0.15625 to 0.15625
- gain_a: bfloat16 [2048], P('fsdp'), may hold values from 0.5 to 1.5
- gain_b: bfloat16 [2048], P('fsdp'), may hold values from 0.5 to 1.5
- conv_weight: float32 [4, 2560], P(None, 'seq'), may hold values from -3 to 3
- conv_bias: float32 [2560], P('seq'), may hold values from -3 to 3
- gate_weight: float32 [2, 2560], P(None, 'seq'), may hold values from -4 to 4
- gate_bias: float32 [2, 2560], P(None, 'seq'), may hold values from -4 to 4
- decay_logits: float32 [2560], P('seq'), may hold values from 5 to 11.5
- lengths: int32 [2, 8], P('fsdp'), may hold values from 1 to 2048, 4096 in all within a row
- permutation: int32 [2, 4096], P('fsdp'), may hold values from 0 to 4095, each once within a row
Outputs:
- output: float32 [8192, 2048], P(('seq', 'fsdp'))
- token_grad: float32 [8192, 2048], P(('seq', 'fsdp'))
- gate_proj_grad: float32 [2048, 2560], P(('seq', 'fsdp'))
- input_proj_grad: float32 [2048, 2560], P(('seq', 'fsdp'))
- output_proj_grad: float32 [2560, 2048], P(('seq', 'fsdp'))
- mlp_gate_grad: float32 [2048, 6144], P(('seq', 'fsdp'))
- mlp_up_grad: float32 [2048, 6144], P(('seq', 'fsdp'))
- mlp_down_grad: float32 [6144, 2048], P(('seq', 'fsdp'))
- gain_a_grad: float32 [2048], P(('seq', 'fsdp'))
- gain_b_grad: float32 [2048], P(('seq', 'fsdp'))
- conv_weight_grad: float32 [4, 2560], P(None, 'seq')
- conv_bias_grad: float32 [2560], P('seq')
- gate_weight_grad: float32 [2, 2560], P(None, 'seq')
- gate_bias_grad: float32 [2, 2560], P(None, 'seq')
- decay_logits_grad: float32 [2560], P('seq')
- rms_values: float32 [4], replicated
The draws below stay inside these ranges and needn't reach their ends.
Inputs may be any that keep to these rules, and one draw needn't show every extreme that they name: `lengths`: each row sums to 4096, and its largest entry is 2048. `permutation`: each row holds every number from 0 to 4095 once.
All inputs are finite; a program needn't handle non-finite values.
Results may differ from the reference program's by a relative error of at most 0.0095.
Values may be sent and summed in bfloat16 or wider, within the bound.
No kernel may reach another device: no remote copies, remote signals or barrier semaphores. Data moves between devices by JAX's collectives and lax.ppermute only.
A program may use at most 512 MiB of HBM per device.

```python
import math
from functools import partial
import jax
import jax.numpy as jnp
import numpy as np
from jax import lax

D = 2048
R = 2560
FF = 6144
CONV = 4
TOK_DEV = 256
SEQS = 8
TOKG = 4096
TOKENS = 8192
N_SEQ = 16
N_FSDP = 2


def draw_tokens(key, part):
    key = jax.random.fold_in(key, 11)
    rows = jnp.arange(TOKENS, dtype=jnp.float32)[:, None] / TOKENS
    values = jnp.clip(jax.random.normal(key, (TOKENS, D), jnp.float32), -5.0, 5.0)
    scale = 1.0 + 2.0 * rows
    return values * scale


def block_scale(key, dims, cuts, low, largest):
    level = 1.0
    for dim, blocks in cuts:
        heights = jax.random.uniform(jax.random.fold_in(jax.random.fold_in(key, 6), dim), (blocks,), jnp.float32, low / len(cuts), largest / len(cuts))
        level = level * jnp.repeat(jnp.exp(heights), dims[dim] // blocks).reshape((-1,) + (1,) * (len(dims) - 1 - dim))
    return level


def split_up(number_of, total, limit, lean):
    loads = [(1 << 20) // math.isqrt(standing ** lean) + 1 for standing in range(2, number_of + 1)]
    rest, holding = total - limit - (number_of - 1), [1] * (number_of - 1)
    while rest > 0:
        candidates = [i for i in range(number_of - 1) if holding[i] < limit]
        whole, budget = sum([loads[i] for i in candidates]), rest
        for i in candidates:
            extra = min(limit - holding[i], max(1, budget * loads[i] // whole), rest)
            holding[i] = holding[i] + extra
            rest = rest - extra
    return np.array([limit] + holding)


def uneven(rng, count, total, reach, slope):
    if count == 2:
        one = jax.random.randint(rng, (), max(1, total - reach), min(reach, total - 1) + 1)
        return jnp.stack([one, total - one])
    tallies = jnp.asarray(split_up(count, total, reach, slope), jnp.int32)
    couples = (count - 1) // 2
    source_of, receiver = tallies[1:1 + 2 * couples:2], tallies[2:2 + 2 * couples:2]
    margin = jnp.minimum(source_of - 1, reach - receiver)
    shifted = jax.random.randint(jax.random.fold_in(rng, 1), (couples,), 0, 1 << 20) % (margin + 1)
    tallies = tallies.at[1:1 + 2 * couples:2].set(source_of - shifted).at[2:2 + 2 * couples:2].set(receiver + shifted)
    return tallies[jax.random.permutation(jax.random.fold_in(rng, 2), count)]


def noise(rng, extent, deviation, most, pieces=(), kind=jnp.bfloat16):
    array = jax.random.normal(rng, extent, jnp.float32) * deviation
    if len(pieces) > 0:
        array = block_scale(rng, extent, pieces, -0.22, 0.18) * array
    return jnp.clip(array, min=-most, max=most).astype(kind)


def setup_inputs(seed: int = 0) -> dict:
    keys = jax.random.split(jax.random.key(seed), 18)
    tokens = draw_tokens(jax.random.fold_in(keys[17], 71), 0)
    cotangent = noise(keys[1], (TOKENS, D), 1.0, 6.0, ((0, 32),), jnp.float32)
    gate_proj = noise(keys[2], (D, R), D ** -0.5, 0.125, ((0, 2),))
    input_proj = noise(keys[3], (D, R), D ** -0.5, 0.125, ((0, 2),))
    output_proj = noise(keys[4], (R, D), (R // 4) ** -0.5, 0.25, ((0, 2),))
    mlp_gate = noise(keys[5], (D, FF), D ** -0.5, 0.125, ((0, 2),))
    mlp_up = noise(keys[6], (D, FF), D ** -0.5, 0.125, ((0, 2),))
    mlp_down = noise(keys[7], (FF, D), (FF // 4) ** -0.5, 0.15625, ((0, 2),))
    gain_a = jnp.clip(1.0 + 0.1 * jax.random.normal(keys[8], (D,), jnp.float32), 0.5, 1.5).astype(jnp.bfloat16)
    gain_b = jnp.clip(1.0 + 0.1 * jax.random.normal(keys[9], (D,), jnp.float32), 0.5, 1.5).astype(jnp.bfloat16)
    conv_weight = noise(keys[10], (CONV, R), CONV ** -0.5, 3.0, ((1, 16),), jnp.float32)
    conv_bias = noise(keys[11], (R,), 0.5, 3.0, ((0, 16),), jnp.float32)
    gate_weight = noise(keys[12], (2, R), 1.0, 4.0, ((1, 16),), jnp.float32)
    gate_bias = noise(keys[13], (2, R), 1.0, 4.0, ((1, 16),), jnp.float32)
    decay_logits = jnp.clip(5.0 + 6.5 * jax.random.uniform(keys[14], (R,), jnp.float32) ** block_scale(keys[14], (R,), ((0, 16),), -0.2, 0.2), 5.0, 11.5)
    lengths = jax.vmap(lambda own: uneven(own, SEQS, TOKG, TOKG // 2, 2))(jax.random.split(keys[15], N_FSDP)).reshape((N_FSDP, SEQS)).astype(jnp.int32)
    permutation = jax.vmap(lambda own: jax.random.permutation(own, TOKG))(jax.random.split(keys[16], N_FSDP)).reshape((N_FSDP, TOKG)).astype(jnp.int32)
    return dict(tokens=tokens, cotangent=cotangent, gate_proj=gate_proj, input_proj=input_proj, output_proj=output_proj, mlp_gate=mlp_gate, mlp_up=mlp_up, mlp_down=mlp_down, gain_a=gain_a, gain_b=gain_b, conv_weight=conv_weight, conv_bias=conv_bias, gate_weight=gate_weight, gate_bias=gate_bias, decay_logits=decay_logits, lengths=lengths, permutation=permutation)


NORM_EPS = 1e-06
RATE_SCALE = 8.0
CHANNEL_BLOCK = 128

@jax.custom_vjp
def low(v):
    return lax.optimization_barrier(v.astype(jnp.bfloat16)).astype(jnp.float32)

@jax.custom_vjp
def low_back(v):
    return v

def low_keep(v):
    return (low(v), None)

def low_pass(kept, grad):
    return (grad,)

def back_keep(v):
    return (v, None)

def back_low(kept, grad):
    return (low(grad),)
low.defvjp(low_keep, low_pass)
low_back.defvjp(back_keep, back_low)

def gelu_tanh(values):
    return jax.nn.gelu(values, approximate=True)

def rms_norm(values, norm_gain):
    return values * lax.rsqrt(lax.optimization_barrier(jnp.mean(values * values, axis=-1, keepdims=True)) + NORM_EPS) * norm_gain

def matmul(left, right):
    return jnp.dot(left, right, precision=lax.Precision.HIGHEST)

def offsets(lengths, row_total):
    lengths = lengths.astype(jnp.int32)
    seq_ends = jnp.cumsum(lengths).astype(jnp.int32)
    seq_starts = seq_ends - lengths
    position = jnp.arange(row_total, dtype=jnp.int32)
    inside = position[:, None] >= seq_starts[None, :]
    seg_first = lax.optimization_barrier(jnp.max(jnp.where(inside, seq_starts[None, :], 0), axis=1)).astype(jnp.int32)
    return position - seg_first

def inverse_of(order):
    return jnp.zeros_like(order).at[order].set(jnp.arange(order.shape[0], dtype=jnp.int32))

def combine_steps(earlier, later_step):
    return (earlier[0] * later_step[0], later_step[0] * earlier[1] + later_step[1])

def recurrence(inputs, conv_weight, conv_bias, gate_weight, gate_bias, decay_logits, position):
    tap_count = conv_weight.shape[0]
    filtered = conv_bias[None, :] + conv_weight[0][None, :] * inputs
    for offset in range(1, tap_count):
        delayed = jnp.pad(inputs, ((offset, 0), (0, 0)))[:-offset]
        filtered = filtered + conv_weight[offset][None, :] * jnp.where(position[:, None] >= offset, delayed, 0.0)
    recur_gate = jax.nn.sigmoid(gate_weight[0][None, :] * filtered + gate_bias[0][None, :])
    input_gate = jax.nn.sigmoid(gate_weight[1][None, :] * filtered + gate_bias[1][None, :])
    decay_rate = RATE_SCALE * jax.nn.softplus(-decay_logits)[None, :] * recur_gate
    decay = jnp.where(position[:, None] > 0, jnp.exp(-decay_rate), 0.0)
    drive = jnp.sqrt(-jnp.expm1(-2.0 * decay_rate)) * input_gate * filtered
    _, hidden_state = lax.associative_scan(combine_steps, (decay, drive), axis=0)
    return hidden_state

def channel_blocks(values):
    count = R // CHANNEL_BLOCK
    return jnp.moveaxis(values.reshape(values.shape[:-1] + (count, CHANNEL_BLOCK)), -2, 0)

def block_forward(tokens, w_gate, w_input, w_output, w_mlpgate, w_mlpup, w_down, gain_a, gain_b, conv_weight, conv_bias, gate_weight, gate_bias, decay_logits, position, permutation, inverse):
    grouped = tokens.reshape(N_SEQ, N_FSDP, TOK_DEV, D).transpose(1, 0, 2, 3).reshape(N_FSDP * TOKG, D)
    normed_a = low(rms_norm(grouped, gain_a))
    gate_pre = low_back(matmul(normed_a, w_gate))
    input_pre = low(low_back(matmul(normed_a, w_input)))
    input_groups = input_pre.reshape(N_FSDP, TOKG, R)
    params = (channel_blocks(conv_weight), channel_blocks(conv_bias), channel_blocks(gate_weight), channel_blocks(gate_bias), channel_blocks(decay_logits))
    states = []
    for group in range(N_FSDP):
        ordered = jnp.take(input_groups[group], inverse[group], axis=0)
        runner = jax.checkpoint(partial(recurrence, position=position[group]))
        scanned = lax.map(lambda items: runner(items[0], items[1], items[2], items[3], items[4], items[5]), (channel_blocks(ordered),) + params)
        scanned = jnp.moveaxis(scanned, 0, 1).reshape(TOKG, R)
        states.append(jnp.take(scanned, permutation[group], axis=0))
    hidden_state = low_back(low(jnp.concatenate(states, axis=0)))
    gated = low(hidden_state * gelu_tanh(gate_pre))
    branch_a = low_back(matmul(gated, w_output))
    middle = grouped + branch_a
    normed_b = low(rms_norm(middle, gain_b))
    first_pre = low_back(matmul(normed_b, w_mlpgate))
    second_pre = low_back(matmul(normed_b, w_mlpup))
    mixed = low(gelu_tanh(first_pre) * second_pre)
    branch_b = low_back(matmul(mixed, w_down))
    output = middle + branch_b
    sums = jnp.stack([jnp.sum(grouped * grouped), jnp.sum(branch_a * branch_a), jnp.sum(middle * middle), jnp.sum(branch_b * branch_b)])
    ungrouped = output.reshape(N_FSDP, N_SEQ, TOK_DEV, D).transpose(1, 0, 2, 3).reshape(TOKENS, D)
    return (ungrouped, sums)

def reference(tokens, cotangent, gate_proj, input_proj, output_proj, mlp_gate, mlp_up, mlp_down, gain_a, gain_b, conv_weight, conv_bias, gate_weight, gate_bias, decay_logits, lengths, permutation):
    position = jnp.stack([offsets(lengths[group], TOKG) for group in range(N_FSDP)])
    inverse = jnp.stack([inverse_of(permutation[group].astype(jnp.int32)) for group in range(N_FSDP)])
    forward = partial(block_forward, position=position, permutation=permutation.astype(jnp.int32), inverse=inverse)
    output, backward, sums = jax.vjp(forward, tokens, gate_proj.astype(jnp.float32), input_proj.astype(jnp.float32), output_proj.astype(jnp.float32), mlp_gate.astype(jnp.float32), mlp_up.astype(jnp.float32), mlp_down.astype(jnp.float32), gain_a.astype(jnp.float32), gain_b.astype(jnp.float32), conv_weight, conv_bias, gate_weight, gate_bias, decay_logits, has_aux=True)
    grads = backward(cotangent)
    rms_values = jnp.sqrt(sums / (TOKENS * D))
    return (output, grads[0], grads[1], grads[2], grads[3], grads[4], grads[5], grads[6], grads[7], grads[8], grads[9], grads[10], grads[11], grads[12], grads[13], rms_values)
```

```python
from functools import partial

import jax
import jax.numpy as jnp
from jax import lax
from jax.sharding import PartitionSpec as P

NORM_EPS = 1e-06
RATE_SCALE = 8.0


def gelu_tanh(values):
    return jax.nn.gelu(values, approximate=True)


def rms_norm(values, norm_gain):
    return (
        values * lax.rsqrt(jnp.mean(values * values, axis=-1, keepdims=True) + NORM_EPS) * norm_gain
    )


def gated_state(state_in, gate_pre):
    return state_in * gelu_tanh(gate_pre)


def mixing(first_pre, second_pre):
    return gelu_tanh(first_pre) * second_pre


def offsets(lengths, row_total):
    seq_ends = jnp.cumsum(lengths)
    seq_starts = seq_ends - lengths
    position = jnp.arange(row_total, dtype=jnp.int32)
    inside = position[:, None] >= seq_starts[None, :]
    seg_first = jnp.max(jnp.where(inside, seq_starts[None, :], 0), axis=1)
    return position - seg_first


def combine_steps(earlier, later_step):
    return (earlier[0] * later_step[0], later_step[0] * earlier[1] + later_step[1])


def recurrence(inputs, conv_weight, conv_bias, gate_weight, gate_bias, decay_logits, position):
    tap_count = conv_weight.shape[0]
    filtered = conv_bias[:, None] + conv_weight[0][:, None] * inputs
    for offset in range(1, tap_count):
        delayed = jnp.pad(inputs, ((0, 0), (offset, 0)))[:, :-offset]
        filtered = filtered + conv_weight[offset][:, None] * jnp.where(
            position[None, :] >= offset, delayed, 0.0
        )
    recur_gate = jax.nn.sigmoid(gate_weight[0][:, None] * filtered + gate_bias[0][:, None])
    input_gate = jax.nn.sigmoid(gate_weight[1][:, None] * filtered + gate_bias[1][:, None])
    decay_rate = RATE_SCALE * jax.nn.softplus(-decay_logits)[:, None] * recur_gate
    decay = jnp.where(position[None, :] > 0, jnp.exp(-decay_rate), 0.0)
    drive = jnp.sqrt(-jnp.expm1(-2.0 * decay_rate)) * input_gate * filtered
    _, hidden_state = lax.associative_scan(combine_steps, (decay, drive), axis=1)
    return hidden_state


def swap_core(values):
    return lax.ppermute(values, "fsdp", [(0, 1), (1, 0)])


def swap_bit(values, bit):
    count = lax.axis_size("seq")
    return lax.ppermute(values, "seq", [(i, i ^ (1 << bit)) for i in range(count)])


def half(values, index, axis):
    size = values.shape[axis] // 2
    return lax.dynamic_slice_in_dim(values, index * size, size, axis)


def reorder_blocks(values, low_bit, high_bit, axis):
    width = high_bit - low_bit
    size = values.shape[axis] >> width
    pieces = []
    for place in range(1 << width):
        natural = sum(((place >> (width - 1 - k)) & 1) << k for k in range(width))
        pieces.append(lax.slice_in_dim(values, natural * size, (natural + 1) * size, axis=axis))
    return jnp.concatenate(pieces, axis=axis)


def gather_tokens(values, swap, axis):
    return jnp.concatenate([values, swap(values)], axis=axis)


def trade_tokens(values, swap, own_bit, split_axis, token_axis):
    other = swap(half(values, 1 - own_bit, split_axis))
    return jnp.concatenate([half(values, own_bit, split_axis), other], axis=token_axis)


def halve_sum(values, swap, own_bit, axis):
    other = swap(half(values, 1 - own_bit, axis).astype(jnp.bfloat16))
    return half(values, own_bit, axis).astype(jnp.float32) + other.astype(jnp.float32)


def collect(values, swap, own_bit, split_axis, join_axis):
    own = half(values, own_bit, split_axis)
    other = swap(half(values, 1 - own_bit, split_axis).astype(jnp.bfloat16)).astype(own.dtype)
    first = jnp.where(own_bit == 0, own, other)
    second = jnp.where(own_bit == 0, other, own)
    return jnp.concatenate([first, second], axis=join_axis)


def share_sum(values, bit_count):
    values = values + swap_core(values)
    for bit in range(bit_count):
        values = values + swap_bit(values, bit)
    return values


def product(subscripts, left, right):
    return jnp.einsum(subscripts, left, right, preferred_element_type=jnp.float32)


def product_sum(subscripts, left, left_axis, right, swap, own_bit):
    sent = product(subscripts, half(left, 1 - own_bit, left_axis), right).astype(jnp.bfloat16)
    other = swap(sent)
    return product(subscripts, half(left, own_bit, left_axis), right) + other.astype(jnp.float32)


def projection_grad(channel_grad, normed_all, core, bits, swaps):
    taken = trade_tokens(channel_grad, swap_core, core, 0, 1)
    for bit in (0, 1):
        taken = trade_tokens(taken, swaps[bit], bits[bit], 0, 1)
    total = product("rt,td->rd", taken, normed_all).astype(jnp.bfloat16)
    for bit in range(2, len(bits)):
        total = halve_sum(total, swaps[bit], bits[bit], 1)
    total = total.T
    for bit in (1, 0):
        total = collect(total, swaps[bit], bits[bit], 0, 1)
    return collect(total, swap_core, core, 0, 1)


def output_grad(gated, out_grad, core, bits, swaps):
    rows, count = gated.shape
    shape = (2,) * len(bits) + (2, rows // (2 << len(bits)), count)
    bit_axes = tuple(range(len(bits) - 1, -1, -1))
    dims = (len(bits),) + bit_axes + (len(bits) + 1, len(bits) + 2)
    taken = gated.reshape(shape).transpose(dims).reshape(rows, count)
    out_all = out_grad
    for swap, own_bit in ((swap_core, core), (swaps[0], bits[0])):
        taken = trade_tokens(taken, swap, own_bit, 0, 1)
        out_all = gather_tokens(out_all, swap, 0)
    total = product_sum("rt,td->rd", taken, 0, out_all, swaps[1], bits[1])
    for bit in range(2, len(bits)):
        total = halve_sum(total, swaps[bit], bits[bit], 0)
    return total


def hidden_grads(normed, hidden, core, bits, swaps):
    normed_all = reorder_blocks(normed, 1, len(bits), 1)
    for swap in (swap_core, swaps[0]):
        normed_all = gather_tokens(normed_all, swap, 0)
    results = []
    for taken in hidden:
        taken = trade_tokens(taken, swap_core, core, 1, 0)
        taken = trade_tokens(taken, swaps[0], bits[0], 1, 0)
        total = product_sum("td,tf->df", normed_all, 1, taken, swaps[1], bits[1])
        for bit in range(2, len(bits)):
            total = halve_sum(total, swaps[bit], bits[bit], 0)
        total = collect(total, swaps[0], bits[0], 0, 1)
        results.append(collect(total, swap_core, core, 0, 1))
    return results


def down_weight_grad(mixed, down_all, core, bits, swaps):
    taken = reorder_blocks(mixed, 0, len(bits), 1)
    for bit in (0, 1):
        taken = trade_tokens(taken, swaps[bit], bits[bit], 1, 0)
    total = product("tf,td->fd", taken, down_all).astype(jnp.bfloat16)
    rows, count = total.shape
    blocks = 1 << (len(bits) - 2)
    total = total.reshape(blocks, 2, rows // (2 * blocks), count).transpose(1, 0, 2, 3)
    total = total.reshape(rows, count)
    total = halve_sum(total, swap_core, core, 0)
    for bit in range(2, len(bits)):
        total = halve_sum(total, swaps[bit], bits[bit], 0)
    return total


def per_device(
    tokens,
    cotangent,
    gate_proj,
    input_proj,
    output_proj,
    mlp_gate,
    mlp_up,
    mlp_down,
    gain_a,
    gain_b,
    conv_weight,
    conv_bias,
    gate_weight,
    gate_bias,
    decay_logits,
    lengths,
    permutation,
):
    w_gate, w_input, w_output, w_mlpgate, w_mlpup, w_down, full_gain_a, full_gain_b = (
        lax.all_gather(gate_proj, "fsdp", axis=0, tiled=True),
        lax.all_gather(input_proj, "fsdp", axis=0, tiled=True),
        lax.all_gather(output_proj, "fsdp", axis=0, tiled=True),
        lax.all_gather(mlp_gate, "fsdp", axis=0, tiled=True),
        lax.all_gather(mlp_up, "fsdp", axis=0, tiled=True),
        lax.all_gather(mlp_down, "fsdp", axis=0, tiled=True),
        lax.all_gather(gain_a, "fsdp", axis=0, tiled=True),
        lax.all_gather(gain_b, "fsdp", axis=0, tiled=True),
    )
    core = lax.axis_index("fsdp")
    place = lax.axis_index("seq")
    bit_count = lax.axis_size("seq").bit_length() - 1
    bits = [(place >> bit) & 1 for bit in range(bit_count)]
    swaps = [partial(swap_bit, bit=bit) for bit in range(bit_count)]
    order = permutation[0]
    inverse = jnp.zeros_like(order).at[order].set(jnp.arange(order.shape[0], dtype=jnp.int32))
    position = offsets(lengths[0], order.shape[0])
    normed_a, norm_back_a = jax.vjp(rms_norm, tokens, full_gain_a.astype(jnp.float32))
    normed_a_low = normed_a.astype(jnp.bfloat16)
    down_grad = cotangent.astype(jnp.bfloat16)
    down_all = gather_tokens(gather_tokens(down_grad, swaps[0], 0), swaps[1], 0)
    normed_a_all = reorder_blocks(normed_a_low, 2, bit_count, 1)
    for swap in (swap_core, swaps[0], swaps[1]):
        normed_a_all = gather_tokens(normed_a_all, swap, 0)
    gate_pre = jnp.einsum("td,dr->rt", normed_a_low, w_gate, preferred_element_type=jnp.float32)
    input_pre = jnp.einsum("td,dr->rt", normed_a_low, w_input, preferred_element_type=jnp.float32)
    channel_in = lax.all_to_all(
        input_pre.astype(jnp.bfloat16), "seq", split_axis=0, concat_axis=1, tiled=True
    )
    ordered = jnp.take(channel_in, inverse, axis=1).astype(jnp.float32)
    states, scan_back = jax.vjp(
        partial(recurrence, position=position),
        ordered,
        conv_weight,
        conv_bias,
        gate_weight,
        gate_bias,
        decay_logits,
    )
    dealt = jnp.take(states, order, axis=1).astype(jnp.bfloat16)
    state_tokens = lax.all_to_all(dealt, "seq", split_axis=1, concat_axis=0, tiled=True)
    gated, gated_back = jax.vjp(gated_state, state_tokens.astype(jnp.float32), gate_pre)
    gated_low = gated.astype(jnp.bfloat16)
    branch_a = jnp.einsum("rt,rd->td", gated_low, w_output, preferred_element_type=jnp.float32)
    middle = tokens + branch_a
    normed_b, norm_back_b = jax.vjp(rms_norm, middle, full_gain_b.astype(jnp.float32))
    normed_b_low = normed_b.astype(jnp.bfloat16)
    first_pre = jnp.dot(normed_b_low, w_mlpgate, preferred_element_type=jnp.float32)
    second_pre = jnp.dot(normed_b_low, w_mlpup, preferred_element_type=jnp.float32)
    mixed, mix_back = jax.vjp(mixing, first_pre, second_pre)
    mixed_low = mixed.astype(jnp.bfloat16)
    branch_b = jnp.dot(mixed_low, w_down, preferred_element_type=jnp.float32)
    output = middle + branch_b
    sums = jnp.stack(
        (
            jnp.sum(tokens * tokens),
            jnp.sum(branch_a * branch_a),
            jnp.sum(middle * middle),
            jnp.sum(branch_b * branch_b),
        )
    )
    entry_total = tokens.shape[0] * tokens.shape[1] * lax.axis_size("seq") * lax.axis_size("fsdp")
    mixed_grad = jnp.einsum("td,fd->tf", down_grad, w_down, preferred_element_type=jnp.float32)
    first_grad, second_grad = mix_back(mixed_grad)
    first_low = first_grad.astype(jnp.bfloat16)
    second_low = second_grad.astype(jnp.bfloat16)
    normed_b_grad = jnp.einsum(
        "tf,df->td", first_low, w_mlpgate, preferred_element_type=jnp.float32
    ) + jnp.einsum("tf,df->td", second_low, w_mlpup, preferred_element_type=jnp.float32)
    middle_norm_grad, gain_b_grad = norm_back_b(normed_b_grad)
    middle_grad = cotangent + middle_norm_grad
    out_grad_low = middle_grad.astype(jnp.bfloat16)
    gated_grad = jnp.einsum("td,rd->rt", out_grad_low, w_output, preferred_element_type=jnp.float32)
    state_grad, gate_grad = gated_back(gated_grad)
    state_low = state_grad.astype(jnp.bfloat16)
    gate_low = gate_grad.astype(jnp.bfloat16)
    channel_grad = lax.all_to_all(state_low, "seq", split_axis=0, concat_axis=1, tiled=True)
    ordered_grad = jnp.take(channel_grad, inverse, axis=1).astype(jnp.float32)
    gate_proj_grad = projection_grad(gate_low, normed_a_all, core, bits, swaps)
    output_proj_grad = output_grad(gated_low, out_grad_low, core, bits, swaps)
    mlp_gate_grad, mlp_up_grad = hidden_grads(
        normed_b_low, (first_low, second_low), core, bits, swaps
    )
    mlp_down_grad = down_weight_grad(mixed_low, down_all, core, bits, swaps)
    in_grad, conv_w_grad, conv_b_grad, gate_w_grad, gate_b_grad, logit_grad = scan_back(
        ordered_grad
    )
    dealt_grad = jnp.take(in_grad, order, axis=1).astype(jnp.bfloat16)
    input_grad = lax.all_to_all(dealt_grad, "seq", split_axis=1, concat_axis=0, tiled=True)
    conv_w_sum, conv_b_sum, gate_w_sum, gate_b_sum, logit_sum = lax.psum(
        (conv_w_grad, conv_b_grad, gate_w_grad, gate_b_grad, logit_grad), "fsdp"
    )
    normed_a_grad = jnp.einsum(
        "rt,dr->td", gate_low, w_gate, preferred_element_type=jnp.float32
    ) + jnp.einsum("rt,dr->td", input_grad, w_input, preferred_element_type=jnp.float32)
    input_proj_grad = projection_grad(input_grad, normed_a_all, core, bits, swaps)
    token_norm_grad, gain_a_grad = norm_back_a(normed_a_grad)
    token_grad = middle_grad + token_norm_grad
    early = share_sum(jnp.concatenate([gain_b_grad, sums]), bit_count)
    gain_b_sum, sums = early[: gain_b_grad.shape[0]], early[gain_b_grad.shape[0] :]
    rms_values = jnp.sqrt(sums / entry_total)
    gain_a_sum = share_sum(gain_a_grad, bit_count)
    gain_size = gain_a_sum.shape[0] // (lax.axis_size("seq") * lax.axis_size("fsdp"))
    gain_start = (place * lax.axis_size("fsdp") + core) * gain_size
    finals = (
        gate_proj_grad,
        input_proj_grad,
        output_proj_grad,
        mlp_gate_grad,
        mlp_up_grad,
        mlp_down_grad,
        lax.dynamic_slice_in_dim(gain_a_sum, gain_start, gain_size, 0),
        lax.dynamic_slice_in_dim(gain_b_sum, gain_start, gain_size, 0),
    )
    return (
        output,
        token_grad,
        finals[0],
        finals[1],
        finals[2],
        finals[3],
        finals[4],
        finals[5],
        finals[6],
        finals[7],
        conv_w_sum,
        conv_b_sum,
        gate_w_sum,
        gate_b_sum,
        logit_sum,
        rms_values,
    )


def solution(mesh):
    in_specs = (
        P(("seq", "fsdp"), None),
        P(("seq", "fsdp"), None),
        P("fsdp", None),
        P("fsdp", None),
        P("fsdp", None),
        P("fsdp", None),
        P("fsdp", None),
        P("fsdp", None),
        P("fsdp"),
        P("fsdp"),
        P(None, "seq"),
        P("seq"),
        P(None, "seq"),
        P(None, "seq"),
        P("seq"),
        P("fsdp", None),
        P("fsdp", None),
    )
    out_specs = (
        P(("seq", "fsdp"), None),
        P(("seq", "fsdp"), None),
        P(("seq", "fsdp"), None),
        P(("seq", "fsdp"), None),
        P(("seq", "fsdp"), None),
        P(("seq", "fsdp"), None),
        P(("seq", "fsdp"), None),
        P(("seq", "fsdp"), None),
        P(("seq", "fsdp")),
        P(("seq", "fsdp")),
        P(None, "seq"),
        P("seq"),
        P(None, "seq"),
        P(None, "seq"),
        P("seq"),
        P(),
    )
    return jax.shard_map(
        per_device, mesh=mesh, in_specs=in_specs, out_specs=out_specs, check_vma=False
    )
```

```python
from functools import partial

import jax
import jax.numpy as jnp
from jax import lax
from jax.experimental import pallas as pl
from jax.experimental.pallas import tpu as pltpu
from jax.sharding import PartitionSpec as P

NORM_EPS = 1e-06
RATE_SCALE = 8.0
LANES = 640
SUB = 8
TAPS = 4
UNROLL = 4
VMEM_LIMIT = 60 << 20


def gelu_tanh(values):
    return jax.nn.gelu(values, approximate=True)


def rms_norm(values, norm_gain):
    return (
        values * lax.rsqrt(jnp.mean(values * values, axis=-1, keepdims=True) + NORM_EPS) * norm_gain
    )


def gated_state(state_in, gate_pre):
    return state_in * gelu_tanh(gate_pre)


def mixing(first_pre, second_pre):
    return gelu_tanh(first_pre) * second_pre


def one_minus_exp_neg(u):
    series = jnp.ones_like(u)
    for k in range(9, 1, -1):
        series = 1.0 - u * (1.0 / k) * series
    return jnp.where(u < 0.5, u * series, 1.0 - jnp.exp(-u))


def logistic(values):
    return 1.0 / (1.0 + jnp.exp(-values))


def earlier_chunk(values, channels):
    rolled = pltpu.roll(values, 1, 0)
    wrapped = pltpu.roll(rolled, channels, 1) if channels < LANES else rolled
    sub = lax.broadcasted_iota(jnp.int32, values.shape, 0)
    lane = lax.broadcasted_iota(jnp.int32, values.shape, 1)
    shifted = jnp.where(sub == 0, wrapped, rolled)
    return jnp.where((sub == 0) & (lane < channels), 0.0, shifted)


def later_chunk(values, channels):
    rolled = pltpu.roll(values, SUB - 1, 0)
    wrapped = pltpu.roll(rolled, LANES - channels, 1) if channels < LANES else rolled
    sub = lax.broadcasted_iota(jnp.int32, values.shape, 0)
    lane = lax.broadcasted_iota(jnp.int32, values.shape, 1)
    shifted = jnp.where(sub == SUB - 1, wrapped, rolled)
    return jnp.where((sub == SUB - 1) & (lane >= LANES - channels), 0.0, shifted)


def place_rows(slot_ref, source, group, rows):
    here = slot_ref[source] - group * rows
    row = lax.broadcasted_iota(jnp.int32, (rows, here.shape[-1]), 0)
    return jnp.where(row == here, 1.0, 0.0).astype(jnp.bfloat16)


def into_order(data_ref, slot_ref, wide_ref, ordered_ref, first_row):
    sources, channels, _ = data_ref.shape
    rows = wide_ref.shape[1]
    for group in range(LANES // channels):

        def add_source(source, total, group=group):
            return total + lax.dot_general(
                data_ref[source],
                place_rows(slot_ref, source, group, rows),
                (((1,), (1,)), ((), ())),
                preferred_element_type=jnp.float32,
            )

        wide_ref[group * channels : (group + 1) * channels, :] = lax.fori_loop(
            0, sources, add_source, jnp.zeros((channels, rows), jnp.float32)
        )
    for start in range(0, rows, 128):
        ordered_ref[first_row + start : first_row + start + 128, :] = wide_ref[
            :, start : start + 128
        ].T


def out_of_order(ordered_ref, slot_ref, narrow_ref, data_ref):
    sources, channels, tokens = data_ref.shape
    groups, _, rows = narrow_ref.shape
    for start in range(0, rows, 128):
        wide = ordered_ref[start : start + 128, :].T
        for group in range(groups):
            narrow_ref[group, :, start : start + 128] = wide[
                group * channels : (group + 1) * channels, :
            ].astype(jnp.bfloat16)

    def one_source(source, carry):
        total = jnp.zeros((channels, tokens), jnp.float32)
        for group in range(groups):
            total = total + jnp.dot(
                narrow_ref[group],
                place_rows(slot_ref, source, group, rows),
                preferred_element_type=jnp.float32,
            )
        data_ref[source] = total.astype(jnp.bfloat16)
        return carry

    lax.fori_loop(0, sources, one_source, 0)


def forward_kernel(
    data_ref, slot_ref, offset_ref, params_ref,
    states_ref, inputs_ref, filtered_ref, decay_ref, hidden_ref,
    wide_ref, reach_ref, narrow_ref,
):
    channels = data_ref.shape[1]
    rows = hidden_ref.shape[0]
    pad = (TAPS - 1) * SUB
    into_order(data_ref, slot_ref, wide_ref, inputs_ref, pad)
    for tap in range(TAPS - 1):
        inputs_ref[tap * SUB : (tap + 1) * SUB, :] = earlier_chunk(
            inputs_ref[rows + tap * SUB : rows + (tap + 1) * SUB, :], channels
        )
    param = [params_ref[k : k + 1, :] for k in range(TAPS + 6)]
    block = UNROLL * SUB

    def local_steps(step, carry):
        state, reach = carry
        start = pl.multiple_of(step * block, block)
        offset = offset_ref[pl.ds(start, block), :]
        filtered = param[TAPS] + param[0] * inputs_ref[pl.ds(start + pad, block), :]
        for tap in range(1, TAPS):
            delayed = inputs_ref[pl.ds(start + pad - tap * SUB, block), :]
            filtered = filtered + param[tap] * jnp.where(offset >= tap, delayed, 0.0)
        recur_gate = logistic(param[TAPS + 1] * filtered + param[TAPS + 3])
        input_gate = logistic(param[TAPS + 2] * filtered + param[TAPS + 4])
        rate = param[TAPS + 5] * recur_gate
        decay = jnp.where(offset > 0, jnp.exp(-rate), 0.0)
        drive = jnp.sqrt(one_minus_exp_neg(2.0 * rate)) * input_gate * filtered
        filtered_ref[pl.ds(start, block), :] = filtered
        decay_ref[pl.ds(start, block), :] = decay
        for k in range(UNROLL):
            now = decay[k * SUB : (k + 1) * SUB, :]
            state = now * state + drive[k * SUB : (k + 1) * SUB, :]
            reach = now * reach
            hidden_ref[pl.ds(start + k * SUB, SUB), :] = state
            reach_ref[pl.ds(start + k * SUB, SUB), :] = reach
        return state, reach

    zeros = jnp.zeros((SUB, LANES), jnp.float32)
    last, reach = lax.fori_loop(0, rows // block, local_steps, (zeros, zeros + 1.0))
    chunks = SUB * (LANES // channels)
    entry = lax.fori_loop(
        0, chunks - 1, lambda _, entry: earlier_chunk(last + reach * entry, channels), zeros
    )
    entries = jnp.concatenate([entry] * UNROLL, axis=0)

    def carry_over(step, carry):
        start = pl.multiple_of(step * block, block)
        hidden_ref[pl.ds(start, block), :] += reach_ref[pl.ds(start, block), :] * entries
        return carry

    lax.fori_loop(0, rows // block, carry_over, 0)
    out_of_order(hidden_ref, slot_ref, narrow_ref, states_ref)


def backward_kernel(
    data_ref, slot_ref, offset_ref, params_ref, inputs_ref, filtered_ref, decay_ref, hidden_ref,
    grads_ref, sums_ref,
    wide_ref, back_ref, reach_ref, narrow_ref, filtered_grad_ref, later_offset_ref,
):
    channels = data_ref.shape[1]
    rows = hidden_ref.shape[0]
    pad = (TAPS - 1) * SUB
    into_order(data_ref, slot_ref, wide_ref, back_ref, 0)
    param = [params_ref[k : k + 1, :] for k in range(TAPS + 6)]
    block = UNROLL * SUB
    count = rows // block

    def local_steps(step, carry):
        passed, reach = carry
        start = pl.multiple_of((count - 1 - step) * block, block)
        decay = decay_ref[pl.ds(start, block), :]
        given = back_ref[pl.ds(start, block), :]
        for k in range(UNROLL - 1, -1, -1):
            back = given[k * SUB : (k + 1) * SUB, :] + passed
            back_ref[pl.ds(start + k * SUB, SUB), :] = back
            reach_ref[pl.ds(start + k * SUB, SUB), :] = reach
            now = decay[k * SUB : (k + 1) * SUB, :]
            passed = now * back
            reach = now * reach
        return passed, reach

    zeros = jnp.zeros((SUB, LANES), jnp.float32)
    first, reach = lax.fori_loop(0, count, local_steps, (zeros, zeros + 1.0))
    chunks = SUB * (LANES // channels)
    entry = lax.fori_loop(
        0, chunks - 1, lambda _, entry: later_chunk(first + reach * entry, channels), zeros
    )
    entries = jnp.concatenate([entry] * UNROLL, axis=0)
    sums_ref[...] = jnp.zeros_like(sums_ref)
    before_first = earlier_chunk(hidden_ref[rows - SUB : rows, :], channels)

    def add_up(index, values):
        total = values[:SUB, :]
        for k in range(1, UNROLL):
            total = total + values[k * SUB : (k + 1) * SUB, :]
        sums_ref[index] += total

    def through_gates(step, before):
        start = pl.multiple_of(step * block, block)
        offset = offset_ref[pl.ds(start, block), :]
        filtered = filtered_ref[pl.ds(start, block), :]
        hidden = hidden_ref[pl.ds(start, block), :]
        earlier = jnp.concatenate([before, hidden[: block - SUB, :]], axis=0)
        back = back_ref[pl.ds(start, block), :] + reach_ref[pl.ds(start, block), :] * entries
        recur_gate = logistic(param[TAPS + 1] * filtered + param[TAPS + 3])
        input_gate = logistic(param[TAPS + 2] * filtered + param[TAPS + 4])
        rate = param[TAPS + 5] * recur_gate
        decay = decay_ref[pl.ds(start, block), :]
        squared = one_minus_exp_neg(2.0 * rate)
        scale_inv = lax.rsqrt(jnp.maximum(squared, 1e-37))
        scale = squared * scale_inv
        scale_grad = back * input_gate * filtered
        input_gate_grad = back * scale * filtered
        rate_grad = scale_grad * (1.0 - squared) * scale_inv - decay * back * earlier
        recur_pre_grad = rate_grad * param[TAPS + 5] * recur_gate * (1.0 - recur_gate)
        input_pre_grad = input_gate_grad * input_gate * (1.0 - input_gate)
        filtered_grad = (
            back * scale * input_gate
            + recur_pre_grad * param[TAPS + 1]
            + input_pre_grad * param[TAPS + 2]
        )
        filtered_grad_ref[pl.ds(start, block), :] = filtered_grad
        add_up(0, filtered_grad * inputs_ref[pl.ds(start + pad, block), :])
        for tap in range(1, TAPS):
            delayed = inputs_ref[pl.ds(start + pad - tap * SUB, block), :]
            add_up(tap, filtered_grad * jnp.where(offset >= tap, delayed, 0.0))
        add_up(TAPS, filtered_grad)
        add_up(TAPS + 1, recur_pre_grad * filtered)
        add_up(TAPS + 2, input_pre_grad * filtered)
        add_up(TAPS + 3, recur_pre_grad)
        add_up(TAPS + 4, input_pre_grad)
        add_up(TAPS + 5, rate_grad * recur_gate)
        return hidden[block - SUB :, :]

    lax.fori_loop(0, count, through_gates, before_first)
    for tap in range(TAPS - 1):
        rows_here = slice(tap * SUB, (tap + 1) * SUB)
        filtered_grad_ref[rows + tap * SUB : rows + (tap + 1) * SUB, :] = later_chunk(
            filtered_grad_ref[rows_here, :], channels
        )
        later_offset_ref[block + tap * SUB : block + (tap + 1) * SUB, :] = later_chunk(
            offset_ref[rows_here, :], channels
        )
    later_offset_ref[:block, :] = offset_ref[rows - block :, :]

    def through_taps(start, offsets_ref, offset_start):
        total = param[0] * filtered_grad_ref[pl.ds(start, block), :]
        for tap in range(1, TAPS):
            later = filtered_grad_ref[pl.ds(start + tap * SUB, block), :]
            offset = offsets_ref[pl.ds(offset_start + tap * SUB, block), :]
            total = total + param[tap] * jnp.where(offset >= tap, later, 0.0)
        back_ref[pl.ds(start, block), :] = total

    def inner_taps(step, carry):
        start = pl.multiple_of(step * block, block)
        through_taps(start, offset_ref, start)
        return carry

    lax.fori_loop(0, count - 1, inner_taps, 0)
    through_taps(rows - block, later_offset_ref, 0)
    out_of_order(back_ref, slot_ref, narrow_ref, grads_ref)


def shapes_of(data):
    sources, channels, tokens = data.shape
    rows = sources * tokens * channels // LANES
    return sources, channels, tokens, rows


def recurrence_forward(data, slot, offset, params):
    sources, channels, tokens, rows = shapes_of(data)
    whole = jax.ShapeDtypeStruct((rows, LANES), jnp.float32)
    padded = jax.ShapeDtypeStruct((rows + (TAPS - 1) * SUB, LANES), jnp.float32)
    count = sources * tokens
    return pl.pallas_call(
        forward_kernel,
        out_shape=(jax.ShapeDtypeStruct(data.shape, jnp.bfloat16), padded, whole, whole, whole),
        scratch_shapes=[
            pltpu.VMEM((LANES, rows), jnp.float32),
            pltpu.VMEM((rows, LANES), jnp.float32),
            pltpu.VMEM((LANES // channels, channels, rows), jnp.bfloat16),
        ],
        compiler_params=pltpu.CompilerParams(vmem_limit_bytes=VMEM_LIMIT),
        cost_estimate=pl.CostEstimate(
            flops=4 * count * count * channels, bytes_accessed=16 * rows * LANES, transcendentals=0
        ),
        name="recurrence_forward",
    )(data, slot, offset, params)


def recurrence_backward(data, slot, offset, params, inputs, filtered, decay, hidden):
    sources, channels, tokens, rows = shapes_of(data)
    count = sources * tokens
    return pl.pallas_call(
        backward_kernel,
        out_shape=(
            jax.ShapeDtypeStruct(data.shape, jnp.bfloat16),
            jax.ShapeDtypeStruct((TAPS + 6, SUB, LANES), jnp.float32),
        ),
        scratch_shapes=[
            pltpu.VMEM((LANES, rows), jnp.float32),
            pltpu.VMEM((rows, LANES), jnp.float32),
            pltpu.VMEM((rows, LANES), jnp.float32),
            pltpu.VMEM((LANES // channels, channels, rows), jnp.bfloat16),
            pltpu.VMEM((rows + (TAPS - 1) * SUB, LANES), jnp.float32),
            pltpu.VMEM((UNROLL * SUB + (TAPS - 1) * SUB, LANES), jnp.float32),
        ],
        compiler_params=pltpu.CompilerParams(vmem_limit_bytes=VMEM_LIMIT),
        cost_estimate=pl.CostEstimate(
            flops=4 * count * count * channels, bytes_accessed=20 * rows * LANES, transcendentals=0
        ),
        name="recurrence_backward",
    )(data, slot, offset, params, inputs, filtered, decay, hidden)


def arrangement(lengths, permutation, sources, channels):
    total = permutation.shape[0]
    groups = LANES // channels
    rows = total // groups
    steps = rows // SUB
    chunk = permutation // steps
    slot = (chunk // SUB) * rows + (permutation % steps) * SUB + chunk % SUB
    seq_ends = jnp.cumsum(lengths)
    seq_starts = seq_ends - lengths
    position = jnp.arange(total, dtype=jnp.int32)
    inside = position[:, None] >= seq_starts[None, :]
    seg_first = jnp.max(jnp.where(inside, seq_starts[None, :], 0), axis=1)
    offset = jnp.minimum(position - seg_first, TAPS - 1).astype(jnp.float32)
    offset = offset.reshape(groups, SUB, steps).transpose(2, 1, 0).reshape(rows, groups, 1)
    offset = jnp.broadcast_to(offset, (rows, groups, channels)).reshape(rows, LANES)
    return slot.reshape(sources, 1, total // sources), offset


def lane_params(conv_weight, conv_bias, gate_weight, gate_bias, decay_logits):
    stacked = jnp.concatenate(
        [
            conv_weight,
            conv_bias[None],
            gate_weight,
            gate_bias,
            RATE_SCALE * jax.nn.softplus(-decay_logits)[None],
        ]
    )
    return jnp.tile(stacked, (1, LANES // stacked.shape[1]))


def channel_sums(sums, channels, decay_logits):
    sums = jnp.sum(sums, axis=1).reshape(TAPS + 6, LANES // channels, channels).sum(axis=1)
    logit = -RATE_SCALE * jax.nn.sigmoid(-decay_logits)[None] * sums[TAPS + 5 :]
    return jnp.concatenate([sums[: TAPS + 5], logit])


def swap_core(values):
    return lax.ppermute(values, "fsdp", [(0, 1), (1, 0)])


def swap_bit(values, bit):
    count = lax.axis_size("seq")
    return lax.ppermute(values, "seq", [(i, i ^ (1 << bit)) for i in range(count)])


def half(values, index, axis):
    size = values.shape[axis] // 2
    return lax.dynamic_slice_in_dim(values, index * size, size, axis)


def reorder_blocks(values, low_bit, high_bit, axis):
    width = high_bit - low_bit
    size = values.shape[axis] >> width
    pieces = []
    for place in range(1 << width):
        natural = sum(((place >> (width - 1 - k)) & 1) << k for k in range(width))
        pieces.append(lax.slice_in_dim(values, natural * size, (natural + 1) * size, axis=axis))
    return jnp.concatenate(pieces, axis=axis)


def trade_channels(values):
    return lax.all_to_all(values, "seq", split_axis=0, concat_axis=0, tiled=True)


def gather_tokens(values, swap, axis):
    return jnp.concatenate([values, swap(values)], axis=axis)


def trade_tokens(values, swap, own_bit, split_axis, token_axis):
    other = swap(half(values, 1 - own_bit, split_axis))
    return jnp.concatenate([half(values, own_bit, split_axis), other], axis=token_axis)


def halve_sum(values, swap, own_bit, axis):
    other = swap(half(values, 1 - own_bit, axis).astype(jnp.bfloat16))
    return half(values, own_bit, axis).astype(jnp.float32) + other.astype(jnp.float32)


def collect(values, swap, own_bit, split_axis, join_axis):
    own = half(values, own_bit, split_axis)
    other = swap(half(values, 1 - own_bit, split_axis).astype(jnp.bfloat16)).astype(own.dtype)
    first = jnp.where(own_bit == 0, own, other)
    second = jnp.where(own_bit == 0, other, own)
    return jnp.concatenate([first, second], axis=join_axis)


def share_sum(values, bit_count):
    values = values + swap_core(values)
    for bit in range(bit_count):
        values = values + swap_bit(values, bit)
    return values


def product(subscripts, left, right):
    return jnp.einsum(subscripts, left, right, preferred_element_type=jnp.float32)


def product_sum(subscripts, left, left_axis, right, swap, own_bit):
    sent = product(subscripts, half(left, 1 - own_bit, left_axis), right).astype(jnp.bfloat16)
    other = swap(sent)
    return product(subscripts, half(left, own_bit, left_axis), right) + other.astype(jnp.float32)


def projection_grad(channel_grad, normed_all, core, bits, swaps):
    taken = trade_tokens(channel_grad, swap_core, core, 0, 1)
    for bit in (0, 1):
        taken = trade_tokens(taken, swaps[bit], bits[bit], 0, 1)
    total = product("rt,td->rd", taken, normed_all).astype(jnp.bfloat16)
    for bit in range(2, len(bits)):
        total = halve_sum(total, swaps[bit], bits[bit], 1)
    total = total.T
    for bit in (1, 0):
        total = collect(total, swaps[bit], bits[bit], 0, 1)
    return collect(total, swap_core, core, 0, 1)


def output_grad(gated, out_grad, core, bits, swaps):
    rows, count = gated.shape
    shape = (2,) * len(bits) + (2, rows // (2 << len(bits)), count)
    bit_axes = tuple(range(len(bits) - 1, -1, -1))
    dims = (len(bits),) + bit_axes + (len(bits) + 1, len(bits) + 2)
    taken = gated.reshape(shape).transpose(dims).reshape(rows, count)
    out_all = out_grad
    for swap, own_bit in ((swap_core, core), (swaps[0], bits[0])):
        taken = trade_tokens(taken, swap, own_bit, 0, 1)
        out_all = gather_tokens(out_all, swap, 0)
    total = product_sum("rt,td->rd", taken, 0, out_all, swaps[1], bits[1])
    for bit in range(2, len(bits)):
        total = halve_sum(total, swaps[bit], bits[bit], 0)
    return total


def hidden_grads(normed, hidden, core, bits, swaps):
    normed_all = reorder_blocks(normed, 1, len(bits), 1)
    for swap in (swap_core, swaps[0]):
        normed_all = gather_tokens(normed_all, swap, 0)
    results = []
    for taken in hidden:
        taken = trade_tokens(taken, swap_core, core, 1, 0)
        taken = trade_tokens(taken, swaps[0], bits[0], 1, 0)
        total = product_sum("td,tf->df", normed_all, 1, taken, swaps[1], bits[1])
        for bit in range(2, len(bits)):
            total = halve_sum(total, swaps[bit], bits[bit], 0)
        total = collect(total, swaps[0], bits[0], 0, 1)
        results.append(collect(total, swap_core, core, 0, 1))
    return results


def down_weight_grad(mixed, down_all, core, bits, swaps):
    taken = reorder_blocks(mixed, 0, len(bits), 1)
    for bit in (0, 1):
        taken = trade_tokens(taken, swaps[bit], bits[bit], 1, 0)
    total = product("tf,td->fd", taken, down_all).astype(jnp.bfloat16)
    rows, count = total.shape
    blocks = 1 << (len(bits) - 2)
    total = total.reshape(blocks, 2, rows // (2 * blocks), count).transpose(1, 0, 2, 3)
    total = total.reshape(rows, count)
    total = halve_sum(total, swap_core, core, 0)
    for bit in range(2, len(bits)):
        total = halve_sum(total, swaps[bit], bits[bit], 0)
    return total


def per_device(
    tokens,
    cotangent,
    gate_proj,
    input_proj,
    output_proj,
    mlp_gate,
    mlp_up,
    mlp_down,
    gain_a,
    gain_b,
    conv_weight,
    conv_bias,
    gate_weight,
    gate_bias,
    decay_logits,
    lengths,
    permutation,
):
    w_gate, w_input, w_output, w_mlpgate, w_mlpup, w_down, full_gain_a, full_gain_b = (
        lax.all_gather(gate_proj, "fsdp", axis=0, tiled=True),
        lax.all_gather(input_proj, "fsdp", axis=0, tiled=True),
        lax.all_gather(output_proj, "fsdp", axis=0, tiled=True),
        lax.all_gather(mlp_gate, "fsdp", axis=0, tiled=True),
        lax.all_gather(mlp_up, "fsdp", axis=0, tiled=True),
        lax.all_gather(mlp_down, "fsdp", axis=0, tiled=True),
        lax.all_gather(gain_a, "fsdp", axis=0, tiled=True),
        lax.all_gather(gain_b, "fsdp", axis=0, tiled=True),
    )
    core = lax.axis_index("fsdp")
    place = lax.axis_index("seq")
    bit_count = lax.axis_size("seq").bit_length() - 1
    bits = [(place >> bit) & 1 for bit in range(bit_count)]
    swaps = [partial(swap_bit, bit=bit) for bit in range(bit_count)]
    channels = decay_logits.shape[0]
    block_shape = (lax.axis_size("seq"), channels, tokens.shape[0])
    slot, offset = arrangement(lengths[0], permutation[0], block_shape[0], channels)
    params = lane_params(conv_weight, conv_bias, gate_weight, gate_bias, decay_logits)
    normed_a, norm_back_a = jax.vjp(rms_norm, tokens, full_gain_a.astype(jnp.float32))
    normed_a_low = normed_a.astype(jnp.bfloat16)
    down_grad = cotangent.astype(jnp.bfloat16)
    down_all = gather_tokens(gather_tokens(down_grad, swaps[0], 0), swaps[1], 0)
    normed_a_all = reorder_blocks(normed_a_low, 2, bit_count, 1)
    for swap in (swap_core, swaps[0], swaps[1]):
        normed_a_all = gather_tokens(normed_a_all, swap, 0)
    gate_pre = jnp.einsum("td,dr->rt", normed_a_low, w_gate, preferred_element_type=jnp.float32)
    input_pre = jnp.einsum("td,dr->rt", normed_a_low, w_input, preferred_element_type=jnp.float32)
    channel_in = trade_channels(input_pre.astype(jnp.bfloat16))
    states, *kept = recurrence_forward(channel_in.reshape(block_shape), slot, offset, params)
    state_tokens = trade_channels(states.reshape(input_pre.shape))
    gated, gated_back = jax.vjp(gated_state, state_tokens.astype(jnp.float32), gate_pre)
    gated_low = gated.astype(jnp.bfloat16)
    branch_a = jnp.einsum("rt,rd->td", gated_low, w_output, preferred_element_type=jnp.float32)
    middle = tokens + branch_a
    normed_b, norm_back_b = jax.vjp(rms_norm, middle, full_gain_b.astype(jnp.float32))
    normed_b_low = normed_b.astype(jnp.bfloat16)
    first_pre = jnp.dot(normed_b_low, w_mlpgate, preferred_element_type=jnp.float32)
    second_pre = jnp.dot(normed_b_low, w_mlpup, preferred_element_type=jnp.float32)
    mixed, mix_back = jax.vjp(mixing, first_pre, second_pre)
    mixed_low = mixed.astype(jnp.bfloat16)
    branch_b = jnp.dot(mixed_low, w_down, preferred_element_type=jnp.float32)
    output = middle + branch_b
    sums = jnp.stack(
        (
            jnp.sum(tokens * tokens),
            jnp.sum(branch_a * branch_a),
            jnp.sum(middle * middle),
            jnp.sum(branch_b * branch_b),
        )
    )
    entry_total = tokens.shape[0] * tokens.shape[1] * lax.axis_size("seq") * lax.axis_size("fsdp")
    mixed_grad = jnp.einsum("td,fd->tf", down_grad, w_down, preferred_element_type=jnp.float32)
    first_grad, second_grad = mix_back(mixed_grad)
    first_low = first_grad.astype(jnp.bfloat16)
    second_low = second_grad.astype(jnp.bfloat16)
    normed_b_grad = jnp.einsum(
        "tf,df->td", first_low, w_mlpgate, preferred_element_type=jnp.float32
    ) + jnp.einsum("tf,df->td", second_low, w_mlpup, preferred_element_type=jnp.float32)
    middle_norm_grad, gain_b_grad = norm_back_b(normed_b_grad)
    middle_grad = cotangent + middle_norm_grad
    out_grad_low = middle_grad.astype(jnp.bfloat16)
    gated_grad = jnp.einsum("td,rd->rt", out_grad_low, w_output, preferred_element_type=jnp.float32)
    state_grad, gate_grad = gated_back(gated_grad)
    state_low = state_grad.astype(jnp.bfloat16)
    gate_low = gate_grad.astype(jnp.bfloat16)
    channel_grad = trade_channels(state_low)
    gate_proj_grad = projection_grad(gate_low, normed_a_all, core, bits, swaps)
    output_proj_grad = output_grad(gated_low, out_grad_low, core, bits, swaps)
    mlp_gate_grad, mlp_up_grad = hidden_grads(
        normed_b_low, (first_low, second_low), core, bits, swaps
    )
    mlp_down_grad = down_weight_grad(mixed_low, down_all, core, bits, swaps)
    dealt_grad, lane_sums = recurrence_backward(
        channel_grad.reshape(block_shape), slot, offset, params, *kept
    )
    input_grad = trade_channels(dealt_grad.reshape(state_low.shape))
    param_sums = channel_sums(lane_sums, channels, decay_logits)
    param_sums = param_sums + swap_core(param_sums)
    normed_a_grad = jnp.einsum(
        "rt,dr->td", gate_low, w_gate, preferred_element_type=jnp.float32
    ) + jnp.einsum("rt,dr->td", input_grad, w_input, preferred_element_type=jnp.float32)
    input_proj_grad = projection_grad(input_grad, normed_a_all, core, bits, swaps)
    token_norm_grad, gain_a_grad = norm_back_a(normed_a_grad)
    token_grad = middle_grad + token_norm_grad
    early = share_sum(jnp.concatenate([gain_b_grad, sums]), bit_count)
    gain_b_sum, sums = early[: gain_b_grad.shape[0]], early[gain_b_grad.shape[0] :]
    rms_values = jnp.sqrt(sums / entry_total)
    gain_a_sum = share_sum(gain_a_grad, bit_count)
    gain_size = gain_a_sum.shape[0] // (lax.axis_size("seq") * lax.axis_size("fsdp"))
    gain_start = (place * lax.axis_size("fsdp") + core) * gain_size
    finals = (
        gate_proj_grad,
        input_proj_grad,
        output_proj_grad,
        mlp_gate_grad,
        mlp_up_grad,
        mlp_down_grad,
        lax.dynamic_slice_in_dim(gain_a_sum, gain_start, gain_size, 0),
        lax.dynamic_slice_in_dim(gain_b_sum, gain_start, gain_size, 0),
    )
    return (
        output,
        token_grad,
        finals[0],
        finals[1],
        finals[2],
        finals[3],
        finals[4],
        finals[5],
        finals[6],
        finals[7],
        param_sums[:TAPS],
        param_sums[TAPS],
        param_sums[TAPS + 1 : TAPS + 3],
        param_sums[TAPS + 3 : TAPS + 5],
        param_sums[TAPS + 5],
        rms_values,
    )


def solution(mesh):
    in_specs = (
        P(("seq", "fsdp"), None),
        P(("seq", "fsdp"), None),
        P("fsdp", None),
        P("fsdp", None),
        P("fsdp", None),
        P("fsdp", None),
        P("fsdp", None),
        P("fsdp", None),
        P("fsdp"),
        P("fsdp"),
        P(None, "seq"),
        P("seq"),
        P(None, "seq"),
        P(None, "seq"),
        P("seq"),
        P("fsdp", None),
        P("fsdp", None),
    )
    out_specs = (
        P(("seq", "fsdp"), None),
        P(("seq", "fsdp"), None),
        P(("seq", "fsdp"), None),
        P(("seq", "fsdp"), None),
        P(("seq", "fsdp"), None),
        P(("seq", "fsdp"), None),
        P(("seq", "fsdp"), None),
        P(("seq", "fsdp"), None),
        P(("seq", "fsdp")),
        P(("seq", "fsdp")),
        P(None, "seq"),
        P("seq"),
        P(None, "seq"),
        P(None, "seq"),
        P("seq"),
        P(),
    )
    return jax.shard_map(
        per_device, mesh=mesh, in_specs=in_specs, out_specs=out_specs, check_vma=False
    )
```

```python
from functools import partial

import jax
import jax.numpy as jnp
from jax import lax
from jax.experimental import pallas as pl
from jax.experimental.pallas import tpu as pltpu
from jax.sharding import PartitionSpec as P

NORM_EPS = 1e-06
RATE_SCALE = 8.0
LANES = 640
SUB = 8
TAPS = 4
UNROLL = 4
VMEM_LIMIT = 60 << 20


def gelu_tanh(values):
    return jax.nn.gelu(values, approximate=True)


def rms_norm(values, norm_gain):
    return (
        values * lax.rsqrt(jnp.mean(values * values, axis=-1, keepdims=True) + NORM_EPS) * norm_gain
    )


def gated_state(state_in, gate_pre):
    return state_in * gelu_tanh(gate_pre)


def mixing(first_pre, second_pre):
    return gelu_tanh(first_pre) * second_pre


def one_minus_exp_neg(u):
    series = jnp.ones_like(u)
    for k in range(9, 1, -1):
        series = 1.0 - u * (1.0 / k) * series
    return jnp.where(u < 0.5, u * series, 1.0 - jnp.exp(-u))


def logistic(values):
    return 1.0 / (1.0 + jnp.exp(-values))


def earlier_chunk(values, channels):
    rolled = pltpu.roll(values, 1, 0)
    wrapped = pltpu.roll(rolled, channels, 1) if channels < LANES else rolled
    sub = lax.broadcasted_iota(jnp.int32, values.shape, 0)
    lane = lax.broadcasted_iota(jnp.int32, values.shape, 1)
    shifted = jnp.where(sub == 0, wrapped, rolled)
    return jnp.where((sub == 0) & (lane < channels), 0.0, shifted)


def later_chunk(values, channels):
    rolled = pltpu.roll(values, SUB - 1, 0)
    wrapped = pltpu.roll(rolled, LANES - channels, 1) if channels < LANES else rolled
    sub = lax.broadcasted_iota(jnp.int32, values.shape, 0)
    lane = lax.broadcasted_iota(jnp.int32, values.shape, 1)
    shifted = jnp.where(sub == SUB - 1, wrapped, rolled)
    return jnp.where((sub == SUB - 1) & (lane >= LANES - channels), 0.0, shifted)


def place_rows(slot_ref, source, group, rows):
    here = slot_ref[source] - group * rows
    row = lax.broadcasted_iota(jnp.int32, (rows, here.shape[-1]), 0)
    return jnp.where(row == here, 1.0, 0.0).astype(jnp.bfloat16)


def into_order(data_ref, slot_ref, wide_ref, ordered_ref, first_row):
    sources, channels, _ = data_ref.shape
    rows = wide_ref.shape[1]
    for group in range(LANES // channels):

        def add_source(source, total, group=group):
            return total + lax.dot_general(
                data_ref[source],
                place_rows(slot_ref, source, group, rows),
                (((1,), (1,)), ((), ())),
                preferred_element_type=jnp.float32,
            )

        wide_ref[group * channels : (group + 1) * channels, :] = lax.fori_loop(
            0, sources, add_source, jnp.zeros((channels, rows), jnp.float32)
        )
    for start in range(0, rows, 128):
        ordered_ref[first_row + start : first_row + start + 128, :] = wide_ref[
            :, start : start + 128
        ].T


def out_of_order(ordered_ref, slot_ref, narrow_ref, data_ref):
    sources, channels, tokens = data_ref.shape
    groups, _, rows = narrow_ref.shape
    for start in range(0, rows, 128):
        wide = ordered_ref[start : start + 128, :].T
        for group in range(groups):
            narrow_ref[group, :, start : start + 128] = wide[
                group * channels : (group + 1) * channels, :
            ].astype(jnp.bfloat16)

    def one_source(source, carry):
        total = jnp.zeros((channels, tokens), jnp.float32)
        for group in range(groups):
            total = total + jnp.dot(
                narrow_ref[group],
                place_rows(slot_ref, source, group, rows),
                preferred_element_type=jnp.float32,
            )
        data_ref[source] = total.astype(jnp.bfloat16)
        return carry

    lax.fori_loop(0, sources, one_source, 0)


def forward_kernel(
    data_ref, slot_ref, offset_ref, params_ref,
    states_ref, inputs_ref, filtered_ref, decay_ref, hidden_ref,
    wide_ref, reach_ref, narrow_ref,
):
    channels = data_ref.shape[1]
    rows = hidden_ref.shape[0]
    pad = (TAPS - 1) * SUB
    into_order(data_ref, slot_ref, wide_ref, inputs_ref, pad)
    for tap in range(TAPS - 1):
        inputs_ref[tap * SUB : (tap + 1) * SUB, :] = earlier_chunk(
            inputs_ref[rows + tap * SUB : rows + (tap + 1) * SUB, :], channels
        )
    param = [params_ref[k : k + 1, :] for k in range(TAPS + 6)]
    block = UNROLL * SUB

    def local_steps(step, carry):
        state, reach = carry
        start = pl.multiple_of(step * block, block)
        offset = offset_ref[pl.ds(start, block), :]
        filtered = param[TAPS] + param[0] * inputs_ref[pl.ds(start + pad, block), :]
        for tap in range(1, TAPS):
            delayed = inputs_ref[pl.ds(start + pad - tap * SUB, block), :]
            filtered = filtered + param[tap] * jnp.where(offset >= tap, delayed, 0.0)
        recur_gate = logistic(param[TAPS + 1] * filtered + param[TAPS + 3])
        input_gate = logistic(param[TAPS + 2] * filtered + param[TAPS + 4])
        rate = param[TAPS + 5] * recur_gate
        decay = jnp.where(offset > 0, jnp.exp(-rate), 0.0)
        drive = jnp.sqrt(one_minus_exp_neg(2.0 * rate)) * input_gate * filtered
        filtered_ref[pl.ds(start, block), :] = filtered
        decay_ref[pl.ds(start, block), :] = decay
        for k in range(UNROLL):
            now = decay[k * SUB : (k + 1) * SUB, :]
            state = now * state + drive[k * SUB : (k + 1) * SUB, :]
            reach = now * reach
            hidden_ref[pl.ds(start + k * SUB, SUB), :] = state
            reach_ref[pl.ds(start + k * SUB, SUB), :] = reach
        return state, reach

    zeros = jnp.zeros((SUB, LANES), jnp.float32)
    last, reach = lax.fori_loop(0, rows // block, local_steps, (zeros, zeros + 1.0))
    chunks = SUB * (LANES // channels)
    entry = lax.fori_loop(
        0, chunks - 1, lambda _, entry: earlier_chunk(last + reach * entry, channels), zeros
    )
    entries = jnp.concatenate([entry] * UNROLL, axis=0)

    def carry_over(step, carry):
        start = pl.multiple_of(step * block, block)
        hidden_ref[pl.ds(start, block), :] += reach_ref[pl.ds(start, block), :] * entries
        return carry

    lax.fori_loop(0, rows // block, carry_over, 0)
    out_of_order(hidden_ref, slot_ref, narrow_ref, states_ref)


def backward_kernel(
    data_ref, slot_ref, offset_ref, params_ref, inputs_ref, filtered_ref, decay_ref, hidden_ref,
    grads_ref, sums_ref,
    wide_ref, back_ref, reach_ref, narrow_ref, filtered_grad_ref, later_offset_ref,
):
    channels = data_ref.shape[1]
    rows = hidden_ref.shape[0]
    pad = (TAPS - 1) * SUB
    into_order(data_ref, slot_ref, wide_ref, back_ref, 0)
    param = [params_ref[k : k + 1, :] for k in range(TAPS + 6)]
    block = UNROLL * SUB
    count = rows // block

    def local_steps(step, carry):
        passed, reach = carry
        start = pl.multiple_of((count - 1 - step) * block, block)
        decay = decay_ref[pl.ds(start, block), :]
        given = back_ref[pl.ds(start, block), :]
        for k in range(UNROLL - 1, -1, -1):
            back = given[k * SUB : (k + 1) * SUB, :] + passed
            back_ref[pl.ds(start + k * SUB, SUB), :] = back
            reach_ref[pl.ds(start + k * SUB, SUB), :] = reach
            now = decay[k * SUB : (k + 1) * SUB, :]
            passed = now * back
            reach = now * reach
        return passed, reach

    zeros = jnp.zeros((SUB, LANES), jnp.float32)
    first, reach = lax.fori_loop(0, count, local_steps, (zeros, zeros + 1.0))
    chunks = SUB * (LANES // channels)
    entry = lax.fori_loop(
        0, chunks - 1, lambda _, entry: later_chunk(first + reach * entry, channels), zeros
    )
    entries = jnp.concatenate([entry] * UNROLL, axis=0)
    sums_ref[...] = jnp.zeros_like(sums_ref)
    before_first = earlier_chunk(hidden_ref[rows - SUB : rows, :], channels)

    def add_up(index, values):
        total = values[:SUB, :]
        for k in range(1, UNROLL):
            total = total + values[k * SUB : (k + 1) * SUB, :]
        sums_ref[index] += total

    def through_gates(step, before):
        start = pl.multiple_of(step * block, block)
        offset = offset_ref[pl.ds(start, block), :]
        filtered = filtered_ref[pl.ds(start, block), :]
        hidden = hidden_ref[pl.ds(start, block), :]
        earlier = jnp.concatenate([before, hidden[: block - SUB, :]], axis=0)
        back = back_ref[pl.ds(start, block), :] + reach_ref[pl.ds(start, block), :] * entries
        recur_gate = logistic(param[TAPS + 1] * filtered + param[TAPS + 3])
        input_gate = logistic(param[TAPS + 2] * filtered + param[TAPS + 4])
        rate = param[TAPS + 5] * recur_gate
        decay = decay_ref[pl.ds(start, block), :]
        squared = one_minus_exp_neg(2.0 * rate)
        scale_inv = lax.rsqrt(jnp.maximum(squared, 1e-37))
        scale = squared * scale_inv
        scale_grad = back * input_gate * filtered
        input_gate_grad = back * scale * filtered
        rate_grad = scale_grad * (1.0 - squared) * scale_inv - decay * back * earlier
        recur_pre_grad = rate_grad * param[TAPS + 5] * recur_gate * (1.0 - recur_gate)
        input_pre_grad = input_gate_grad * input_gate * (1.0 - input_gate)
        filtered_grad = (
            back * scale * input_gate
            + recur_pre_grad * param[TAPS + 1]
            + input_pre_grad * param[TAPS + 2]
        )
        filtered_grad_ref[pl.ds(start, block), :] = filtered_grad
        add_up(0, filtered_grad * inputs_ref[pl.ds(start + pad, block), :])
        for tap in range(1, TAPS):
            delayed = inputs_ref[pl.ds(start + pad - tap * SUB, block), :]
            add_up(tap, filtered_grad * jnp.where(offset >= tap, delayed, 0.0))
        add_up(TAPS, filtered_grad)
        add_up(TAPS + 1, recur_pre_grad * filtered)
        add_up(TAPS + 2, input_pre_grad * filtered)
        add_up(TAPS + 3, recur_pre_grad)
        add_up(TAPS + 4, input_pre_grad)
        add_up(TAPS + 5, rate_grad * recur_gate)
        return hidden[block - SUB :, :]

    lax.fori_loop(0, count, through_gates, before_first)
    for tap in range(TAPS - 1):
        rows_here = slice(tap * SUB, (tap + 1) * SUB)
        filtered_grad_ref[rows + tap * SUB : rows + (tap + 1) * SUB, :] = later_chunk(
            filtered_grad_ref[rows_here, :], channels
        )
        later_offset_ref[block + tap * SUB : block + (tap + 1) * SUB, :] = later_chunk(
            offset_ref[rows_here, :], channels
        )
    later_offset_ref[:block, :] = offset_ref[rows - block :, :]

    def through_taps(start, offsets_ref, offset_start):
        total = param[0] * filtered_grad_ref[pl.ds(start, block), :]
        for tap in range(1, TAPS):
            later = filtered_grad_ref[pl.ds(start + tap * SUB, block), :]
            offset = offsets_ref[pl.ds(offset_start + tap * SUB, block), :]
            total = total + param[tap] * jnp.where(offset >= tap, later, 0.0)
        back_ref[pl.ds(start, block), :] = total

    def inner_taps(step, carry):
        start = pl.multiple_of(step * block, block)
        through_taps(start, offset_ref, start)
        return carry

    lax.fori_loop(0, count - 1, inner_taps, 0)
    through_taps(rows - block, later_offset_ref, 0)
    out_of_order(back_ref, slot_ref, narrow_ref, grads_ref)


def shapes_of(data):
    sources, channels, tokens = data.shape
    rows = sources * tokens * channels // LANES
    return sources, channels, tokens, rows


def recurrence_forward(data, slot, offset, params):
    sources, channels, tokens, rows = shapes_of(data)
    whole = jax.ShapeDtypeStruct((rows, LANES), jnp.float32)
    padded = jax.ShapeDtypeStruct((rows + (TAPS - 1) * SUB, LANES), jnp.float32)
    count = sources * tokens
    return pl.pallas_call(
        forward_kernel,
        out_shape=(jax.ShapeDtypeStruct(data.shape, jnp.bfloat16), padded, whole, whole, whole),
        scratch_shapes=[
            pltpu.VMEM((LANES, rows), jnp.float32),
            pltpu.VMEM((rows, LANES), jnp.float32),
            pltpu.VMEM((LANES // channels, channels, rows), jnp.bfloat16),
        ],
        compiler_params=pltpu.CompilerParams(vmem_limit_bytes=VMEM_LIMIT),
        cost_estimate=pl.CostEstimate(
            flops=0, bytes_accessed=0, transcendentals=0
        ),
        name="recurrence_forward",
    )(data, slot, offset, params)


def recurrence_backward(data, slot, offset, params, inputs, filtered, decay, hidden):
    sources, channels, tokens, rows = shapes_of(data)
    count = sources * tokens
    return pl.pallas_call(
        backward_kernel,
        out_shape=(
            jax.ShapeDtypeStruct(data.shape, jnp.bfloat16),
            jax.ShapeDtypeStruct((TAPS + 6, SUB, LANES), jnp.float32),
        ),
        scratch_shapes=[
            pltpu.VMEM((LANES, rows), jnp.float32),
            pltpu.VMEM((rows, LANES), jnp.float32),
            pltpu.VMEM((rows, LANES), jnp.float32),
            pltpu.VMEM((LANES // channels, channels, rows), jnp.bfloat16),
            pltpu.VMEM((rows + (TAPS - 1) * SUB, LANES), jnp.float32),
            pltpu.VMEM((UNROLL * SUB + (TAPS - 1) * SUB, LANES), jnp.float32),
        ],
        compiler_params=pltpu.CompilerParams(vmem_limit_bytes=VMEM_LIMIT),
        cost_estimate=pl.CostEstimate(
            flops=0, bytes_accessed=0, transcendentals=0
        ),
        name="recurrence_backward",
    )(data, slot, offset, params, inputs, filtered, decay, hidden)


def arrangement(lengths, permutation, sources, channels):
    total = permutation.shape[0]
    groups = LANES // channels
    rows = total // groups
    steps = rows // SUB
    chunk = permutation // steps
    slot = (chunk // SUB) * rows + (permutation % steps) * SUB + chunk % SUB
    seq_ends = jnp.cumsum(lengths)
    seq_starts = seq_ends - lengths
    position = jnp.arange(total, dtype=jnp.int32)
    inside = position[:, None] >= seq_starts[None, :]
    seg_first = jnp.max(jnp.where(inside, seq_starts[None, :], 0), axis=1)
    offset = jnp.minimum(position - seg_first, TAPS - 1).astype(jnp.float32)
    offset = offset.reshape(groups, SUB, steps).transpose(2, 1, 0).reshape(rows, groups, 1)
    offset = jnp.broadcast_to(offset, (rows, groups, channels)).reshape(rows, LANES)
    return slot.reshape(sources, 1, total // sources), offset


def lane_params(conv_weight, conv_bias, gate_weight, gate_bias, decay_logits):
    stacked = jnp.concatenate(
        [
            conv_weight,
            conv_bias[None],
            gate_weight,
            gate_bias,
            RATE_SCALE * jax.nn.softplus(-decay_logits)[None],
        ]
    )
    return jnp.tile(stacked, (1, LANES // stacked.shape[1]))


def channel_sums(sums, channels, decay_logits):
    sums = jnp.sum(sums, axis=1).reshape(TAPS + 6, LANES // channels, channels).sum(axis=1)
    logit = -RATE_SCALE * jax.nn.sigmoid(-decay_logits)[None] * sums[TAPS + 5 :]
    return jnp.concatenate([sums[: TAPS + 5], logit])


def swap_core(values):
    return lax.ppermute(values, "fsdp", [(0, 1), (1, 0)])


def swap_bit(values, bit):
    count = lax.axis_size("seq")
    return lax.ppermute(values, "seq", [(i, i ^ (1 << bit)) for i in range(count)])


def half(values, index, axis):
    size = values.shape[axis] // 2
    return lax.dynamic_slice_in_dim(values, index * size, size, axis)


def reorder_blocks(values, low_bit, high_bit, axis):
    width = high_bit - low_bit
    size = values.shape[axis] >> width
    pieces = []
    for place in range(1 << width):
        natural = sum(((place >> (width - 1 - k)) & 1) << k for k in range(width))
        pieces.append(lax.slice_in_dim(values, natural * size, (natural + 1) * size, axis=axis))
    return jnp.concatenate(pieces, axis=axis)


def trade_channels(values):
    return lax.all_to_all(values, "seq", split_axis=0, concat_axis=0, tiled=True)


def after(values, *earlier):
    return lax.optimization_barrier((values,) + earlier)[0]


def product(subscripts, left, right):
    return jnp.einsum(subscripts, left, right, preferred_element_type=jnp.float32)


class Links:
    def __init__(self, place, core):
        count = lax.axis_size("seq").bit_length() - 1
        self.core = core
        self.bits = [(place >> bit) & 1 for bit in range(count)]

    def own(self, link):
        return self.core if link == "core" else self.bits[link]

    def swap(self, link, values, *earlier):
        if earlier:
            values = after(values, *earlier)
        return swap_core(values) if link == "core" else swap_bit(values, link)


class Chain:
    def __init__(self, links, terms, sums, collects=(), turn=False, rider=None):
        self.links, self.terms, self.rider = links, list(terms), rider
        self.sums, self.collects, self.turn = list(sums), list(collects), turn
        self.send()

    def total(self):
        return sum(term.astype(jnp.float32) for term in self.terms)

    def send(self):
        if self.sums:
            self.link, self.axis = self.sums[0]
        elif self.collects:
            total = self.total()
            self.terms = [total.T if self.turn else total]
            self.turn = False
            self.link, self.axis = self.collects[0], 0
        else:
            return
        own_bit = self.links.own(self.link)
        sent = sum(half(term, 1 - own_bit, self.axis).astype(jnp.float32) for term in self.terms)
        self.sent = sent.astype(jnp.bfloat16)
        self.other = self.links.swap(self.link, self.sent)
        self.terms = [half(term, own_bit, self.axis) for term in self.terms]
        if self.rider is not None:
            self.rider_other = self.links.swap(self.link, self.rider)

    def advance(self, token):
        other = after(self.other, token)
        if self.rider is not None:
            self.rider = self.rider + after(self.rider_other, token)
        if self.sums:
            self.terms.append(other)
            self.sums.pop(0)
        else:
            own, other = self.terms[0], other.astype(jnp.float32)
            first = self.links.own(self.link) == 0
            low, high = jnp.where(first, own, other), jnp.where(first, other, own)
            self.terms = [jnp.concatenate([low, high], axis=1)]
            self.collects.pop(0)
        if not self.sums and not self.collects:
            return token
        self.send()
        return self.sent


def pick(values, *index):
    for place in index:
        values = lax.dynamic_index_in_dim(values, place, 0, keepdims=False)
    return values


def largest_tile(size, most, step):
    return max(tile for tile in range(step, most + 1, step) if size % tile == 0)


def grad_kernel(count, picked, select_ref, *refs):
    rights = jnp.concatenate([ref[...] for ref in refs[count : 2 * count]], axis=0)
    if picked is None:
        lefts = jnp.concatenate([ref[...] for ref in refs[:count]], axis=1)
        total = jnp.dot(lefts, rights, preferred_element_type=jnp.float32)
    else:
        lefts = jnp.concatenate([ref[...] for ref in refs[:count]], axis=0)
        scalar, groups = picked
        width = lefts.shape[1] // (2 * groups)
        chosen = select_ref[scalar[1]] == 0
        parts = [
            jnp.where(
                chosen,
                lefts[:, 2 * k * width : (2 * k + 1) * width],
                lefts[:, (2 * k + 1) * width : (2 * k + 2) * width],
            )
            for k in range(groups)
        ]
        lefts = jnp.concatenate(parts, axis=1) if groups > 1 else parts[0]
        total = lax.dot_general(
            lefts, rights, (((0,), (0,)), ((), ())), preferred_element_type=jnp.float32
        )
    for ref in refs[2 * count : -1]:
        total = total + ref[...].astype(jnp.float32)
    refs[-1][...] = total.astype(jnp.bfloat16)


CORE, OTHER_CORE, X, OTHER_X, Y, OTHER_Y = (("scalar", k) for k in range(6))


def grad_product(select, pieces, rows, row_half=None, added=None, picked=None, order=None):
    cols = pieces[0][2].shape[-1]
    tile_rows = largest_tile(rows, 512, 16) if picked is None else rows // len(order)
    tile_cols = largest_tile(cols, 1024, 256)

    def entry(index, select_ref):
        return select_ref[index[1]] if isinstance(index, tuple) else index

    def left_spec(left, lead):
        if picked is not None:

            def column_place(m, n, select_ref):
                block = sum(((m >> (width - 1 - k)) & 1) << k for k in range(width))
                return tuple(entry(i, select_ref) for i in lead) + (0, block)

            width = len(order).bit_length() - 1
            return pl.BlockSpec((None,) * len(lead) + (left.shape[-2], 2 * tile_rows), column_place)

        def place(m, n, select_ref):
            start = 0 if row_half is None else entry(row_half, select_ref) * (rows // tile_rows)
            return tuple(entry(i, select_ref) for i in lead) + (start + m, 0)

        return pl.BlockSpec((None,) * len(lead) + (tile_rows, left.shape[-1]), place)

    def right_spec(right, lead):
        def place(m, n, select_ref):
            return tuple(entry(i, select_ref) for i in lead) + (0, n)

        return pl.BlockSpec((None,) * len(lead) + (right.shape[-2], tile_cols), place)

    out_spec = pl.BlockSpec((tile_rows, tile_cols), lambda m, n, select_ref: (m, n))
    in_specs = [left_spec(left, lead) for left, lead, _, _ in pieces]
    in_specs += [right_spec(right, lead) for _, _, right, lead in pieces]
    operands = [left for left, _, _, _ in pieces] + [right for _, _, right, _ in pieces]
    if added is not None:
        in_specs.append(out_spec)
        operands.append(added)
    return pl.pallas_call(
        partial(grad_kernel, len(pieces), picked),
        out_shape=jax.ShapeDtypeStruct((rows, cols), jnp.bfloat16),
        grid_spec=pltpu.PrefetchScalarGridSpec(
            num_scalar_prefetch=1,
            grid=(rows // tile_rows, cols // tile_cols),
            in_specs=in_specs,
            out_specs=out_spec,
        ),
        compiler_params=pltpu.CompilerParams(vmem_limit_bytes=VMEM_LIMIT),
        cost_estimate=pl.CostEstimate(flops=0, bytes_accessed=0, transcendentals=0),
        name="weight_grad",
    )(select, *operands)


GELU_SCALE = 0.7978845608028654
GELU_CUBE = 0.044715
HIDDEN_TILE = 768


def mlp_kernel(
    core_ref, normed_ref, down_grad_ref, gate_ref, up_ref, down_ref,
    branch_ref, normed_grad_ref, mixed_ref, sent_gate_ref, sent_up_ref, kept_gate_ref, kept_up_ref,
):
    step = pl.program_id(0)
    by_columns = (((1,), (1,)), ((), ()))
    normed = normed_ref[...]
    first = jnp.dot(normed, gate_ref[...], preferred_element_type=jnp.float32)
    second = jnp.dot(normed, up_ref[...], preferred_element_type=jnp.float32)
    mixed_grad = lax.dot_general(
        down_grad_ref[...], down_ref[...], by_columns, preferred_element_type=jnp.float32
    )
    square = first * first
    bend = jnp.tanh(GELU_SCALE * first * (1.0 + GELU_CUBE * square))
    rise = 0.5 + 0.5 * bend
    gelu = first * rise
    slope = rise + 0.5 * GELU_SCALE * first * (1.0 - bend * bend) * (
        1.0 + 3.0 * GELU_CUBE * square
    )
    mixed = gelu * second
    first_low = (mixed_grad * slope * second).astype(jnp.bfloat16)
    second_low = (mixed_grad * gelu).astype(jnp.bfloat16)
    mixed_ref[...] = mixed.T.astype(jnp.bfloat16)

    @pl.when(step < pl.num_programs(0) // 2)
    def _():
        sent_gate_ref[...] = first_low
        sent_up_ref[...] = second_low

    @pl.when(step >= pl.num_programs(0) // 2)
    def _():
        kept_gate_ref[...] = first_low
        kept_up_ref[...] = second_low

    @pl.when(step == 0)
    def _():
        branch_ref[...] = jnp.zeros_like(branch_ref)
        normed_grad_ref[...] = jnp.zeros_like(normed_grad_ref)

    branch_ref[...] += jnp.dot(
        mixed.astype(jnp.bfloat16), down_ref[...], preferred_element_type=jnp.float32
    )
    normed_grad_ref[...] += lax.dot_general(
        first_low, gate_ref[...], by_columns, preferred_element_type=jnp.float32
    ) + lax.dot_general(second_low, up_ref[...], by_columns, preferred_element_type=jnp.float32)


def mlp_both_ways(core, normed, down_grad, w_gate, w_up, w_down):
    count, width = normed.shape
    hidden = w_gate.shape[1]
    steps = hidden // HIDDEN_TILE
    quarter = hidden // 4
    tiles = steps // 4

    def tile(t, core_ref):
        chosen = jnp.where(t < steps // 2, 1 - core_ref[0], core_ref[0])
        return chosen * (steps // 2) + t % (steps // 2)

    whole = pl.BlockSpec((count, width), lambda t, core_ref: (0, 0))
    column = pl.BlockSpec((width, HIDDEN_TILE), lambda t, core_ref: (0, tile(t, core_ref)))
    row = pl.BlockSpec((HIDDEN_TILE, width), lambda t, core_ref: (tile(t, core_ref), 0))
    turned = pl.BlockSpec((HIDDEN_TILE, count), lambda t, core_ref: (tile(t, core_ref), 0))

    def sent_place(t, core_ref):
        t = jnp.minimum(t, steps // 2 - 1)
        return (t // tiles, 0, t % tiles)

    def kept_place(t, core_ref):
        t = jnp.maximum(t - steps // 2, 0)
        return (t // tiles, 0, t % tiles)

    sent = pl.BlockSpec((None, count, HIDDEN_TILE), sent_place)
    kept = pl.BlockSpec((None, count, HIDDEN_TILE), kept_place)
    traded = jax.ShapeDtypeStruct((2, count, quarter), jnp.bfloat16)
    summed = jax.ShapeDtypeStruct((count, width), jnp.float32)
    return pl.pallas_call(
        mlp_kernel,
        out_shape=(summed, summed, jax.ShapeDtypeStruct((hidden, count), jnp.bfloat16))
        + (traded,) * 4,
        grid_spec=pltpu.PrefetchScalarGridSpec(
            num_scalar_prefetch=1,
            grid=(steps,),
            in_specs=[whole, whole, column, column, row],
            out_specs=[whole, whole, turned, sent, sent, kept, kept],
        ),
        compiler_params=pltpu.CompilerParams(vmem_limit_bytes=VMEM_LIMIT),
        cost_estimate=pl.CostEstimate(flops=0, bytes_accessed=0, transcendentals=0),
        name="mlp_both_ways",
    )(core.astype(jnp.int32).reshape(1), normed, down_grad, w_gate, w_up, w_down)


class Traded:
    def __init__(self, links, channel_grad):
        channels, count = channel_grad.shape
        self.links = links
        self.mine = channel_grad.reshape(2, 2, channels // 4, count)
        self.by_core = links.swap("core", pick(self.mine, 1 - links.core))

    def trade_x(self, token):
        core, other = self.links.core, 1 - self.links.bits[0]
        self.by_core = after(self.by_core, token)
        sent = jnp.stack([pick(self.mine, core, other), pick(self.by_core, other)])
        self.by_x = self.links.swap(0, sent)
        return sent

    def grad(self, select, normed_pieces):
        lefts = [(self.mine, (CORE, X)), (self.by_core, (X,)), (self.by_x, (0,)), (self.by_x, (1,))]
        pieces = [left + right for left, right in zip(lefts, normed_pieces)]
        return grad_product(select, pieces, self.mine.shape[2])


def per_device(
    tokens,
    cotangent,
    gate_proj,
    input_proj,
    output_proj,
    mlp_gate,
    mlp_up,
    mlp_down,
    gain_a,
    gain_b,
    conv_weight,
    conv_bias,
    gate_weight,
    gate_bias,
    decay_logits,
    lengths,
    permutation,
):
    w_gate, w_input, w_output, w_mlpgate, w_mlpup, w_down = (
        lax.all_gather(gate_proj, "fsdp", axis=0, tiled=True),
        lax.all_gather(input_proj, "fsdp", axis=0, tiled=True),
        lax.all_gather(output_proj, "fsdp", axis=0, tiled=True),
        lax.all_gather(mlp_gate, "fsdp", axis=0, tiled=True),
        lax.all_gather(mlp_up, "fsdp", axis=0, tiled=True),
        lax.all_gather(mlp_down, "fsdp", axis=0, tiled=True),
    )
    core = lax.axis_index("fsdp")
    place = lax.axis_index("seq")
    links = Links(place, core)
    x, y = links.bits[0], links.bits[1]
    bit_count = len(links.bits)
    select = jnp.stack([core, 1 - core, x, 1 - x, y, 1 - y]).astype(jnp.int32)
    channels = decay_logits.shape[0]
    count, width = tokens.shape
    block_shape = (lax.axis_size("seq"), channels, count)
    slot, offset = arrangement(lengths[0], permutation[0], block_shape[0], channels)
    params = lane_params(conv_weight, conv_bias, gate_weight, gate_bias, decay_logits)
    gains = jnp.stack([gain_a, gain_b])
    other_gains = links.swap("core", gains)
    full_gain_a, full_gain_b = jnp.where(
        core == 0,
        jnp.concatenate([gains, other_gains], axis=1),
        jnp.concatenate([other_gains, gains], axis=1),
    )
    other_input = links.swap("core", input_proj)
    normed_a, norm_back_a = jax.vjp(rms_norm, tokens, full_gain_a.astype(jnp.float32))
    normed_a_low = normed_a.astype(jnp.bfloat16)
    down_grad = cotangent.astype(jnp.bfloat16)
    input_pre = product("td,dr->rt", half(normed_a_low, core, 1), input_proj)
    input_pre = input_pre + product("td,dr->rt", half(normed_a_low, 1 - core, 1), other_input)
    channel_in = trade_channels(input_pre.astype(jnp.bfloat16))
    gate_pre = product("td,dr->rt", normed_a_low, w_gate)
    normed_order = reorder_blocks(normed_a_low, 1, bit_count, 1)
    normed_core = links.swap("core", normed_order)
    normed_two = jnp.stack([normed_order, normed_core])
    channel_in, gate_pre = lax.optimization_barrier((channel_in, gate_pre))
    down_y = links.swap(1, down_grad, channel_in)
    normed_x = links.swap(0, normed_two, channel_in)
    states, *kept = recurrence_forward(channel_in.reshape(block_shape), slot, offset, params)
    states = after(states, normed_x, down_y)
    state_tokens = trade_channels(states.reshape(input_pre.shape))
    down_x = links.swap(0, jnp.stack([down_grad, down_y]), state_tokens)
    down_pieces = [(down_grad, ()), (down_y, ()), (down_x, (0,)), (down_x, (1,))]
    normed_pieces = [(normed_order, ()), (normed_core, ()), (normed_x, (0,)), (normed_x, (1,))]
    gated, gated_back = jax.vjp(gated_state, state_tokens.astype(jnp.float32), gate_pre)
    gated_low = gated.astype(jnp.bfloat16)
    branch_a = product("rt,rd->td", gated_low, w_output)
    middle = tokens + branch_a
    normed_b, norm_back_b = jax.vjp(rms_norm, middle, full_gain_b.astype(jnp.float32))
    normed_b_low = normed_b.astype(jnp.bfloat16)
    rows_total = gated_low.shape[0]
    shape = (2,) * bit_count + (2, rows_total // (2 << bit_count), count)
    rest = tuple(range(bit_count - 3, -1, -1))
    dims = (bit_count, bit_count - 2, bit_count - 1) + rest + (bit_count + 1, bit_count + 2)
    normed_b_core = links.swap("core", normed_b_low)
    normed_b_two = jnp.stack([normed_b_low, normed_b_core])
    left_pieces, fars = [], []
    for bit in (0, 1):
        far = links.swap(bit, normed_b_two)
        fars.append(far)
        left_pieces.append([(normed_b_low, ()), (normed_b_core, ()), (far, (0,)), (far, (1,))])
    branch_b, normed_b_grad, mixed, *traded = mlp_both_ways(
        core, normed_b_low, down_grad, w_mlpgate, w_mlpup, w_down
    )
    normed_b_grad = after(normed_b_grad, down_x, *fars)
    output = middle + branch_b
    sums = jnp.stack(
        (
            jnp.sum(tokens * tokens),
            jnp.sum(branch_a * branch_a),
            jnp.sum(middle * middle),
            jnp.sum(branch_b * branch_b),
        )
    )
    entry_total = tokens.shape[0] * tokens.shape[1] * lax.axis_size("seq") * lax.axis_size("fsdp")
    middle_norm_grad, gain_b_grad = norm_back_b(normed_b_grad)
    middle_grad = cotangent + middle_norm_grad
    out_grad_low = middle_grad.astype(jnp.bfloat16)
    gated_grad = product("td,rd->rt", out_grad_low, w_output)
    state_grad, gate_grad = gated_back(gated_grad)
    state_low = state_grad.astype(jnp.bfloat16)
    gate_low = gate_grad.astype(jnp.bfloat16)
    channel_grad = trade_channels(state_low)

    hidden_pieces, fars = [], []
    for index, bit in ((0, 0), (1, 1)):
        sent, mine = traded[index], traded[index + 2]
        other = 1 - links.bits[bit]
        by_core = links.swap("core", sent)
        both = after(jnp.stack([pick(mine, other), pick(by_core, other)]), state_low)
        far = links.swap(bit, both)
        fars.append(far)
        near = (X, Y)[bit]
        rights = [(mine, (near,)), (by_core, (near,)), (far, (0,)), (far, (1,))]
        hidden_pieces.append([left + right for left, right in zip(left_pieces[index], rights)])

    gated_mine = after(gated_low, state_low).reshape(shape).transpose(dims)
    gated_mine = gated_mine.reshape(2, 2, rows_total // 4, count)
    gated_core = links.swap("core", pick(gated_mine, 1 - core))
    out_core = links.swap("core", out_grad_low)
    shape = (2,) * bit_count + (2, mixed.shape[0] // (2 << bit_count), count)
    dims = (bit_count - 2, bit_count - 1, bit_count) + rest + (bit_count + 1, bit_count + 2)
    mixed_mine = after(mixed, state_low).reshape(shape).transpose(dims)
    mixed_mine = mixed_mine.reshape(2, 2, 2, mixed.shape[0] // 8, count)
    mixed_y = links.swap(1, pick(mixed_mine, 1 - y))
    out_two = after(jnp.stack([out_grad_low, out_core]), state_low)
    out_y = links.swap(1, out_two)
    gated_two = jnp.stack([pick(gated_mine, core, 1 - y), pick(gated_core, 1 - y)])
    gated_y = links.swap(1, gated_two)

    dealt_grad, lane_sums = recurrence_backward(
        channel_grad.reshape(block_shape), slot, offset, params, *kept
    )
    dealt_grad = after(dealt_grad, mixed_y, *fars)
    input_grad = trade_channels(dealt_grad.reshape(state_low.shape))

    order = range(1 << (bit_count - 2))
    aligned = (width >> bit_count) % 128 == 0
    if not aligned:
        for index, pieces in enumerate(hidden_pieces):
            for k, (left, lead, right, right_lead) in enumerate(pieces):
                split = left.reshape(left.shape[:-1] + (2,) * bit_count + (width >> bit_count,))
                first = left.ndim - 1
                axes = [first + bit_count - 1 - (1 - index)] + [first + axis for axis in rest]
                axes += [first + bit_count - 1 - index, first + bit_count]
                split = split.transpose(tuple(range(first)) + tuple(axes)).reshape(left.shape)
                pieces[k] = (jnp.swapaxes(split, -1, -2), lead, right, right_lead)

    def hidden_product(index, half_rows, token, added=None):
        chosen = after(select, token)
        if not aligned:
            return grad_product(chosen, hidden_pieces[index], width // 2, half_rows, added)
        picked = (half_rows, 1 + index)
        return grad_product(
            chosen, hidden_pieces[index], width // 2, None, added, picked, order
        )

    rest_bits = range(2, bit_count)
    gate_sent = hidden_product(0, OTHER_Y, dealt_grad)
    gate_received = links.swap(1, gate_sent)
    up_sent = hidden_product(1, OTHER_X, gate_sent)
    up_received = links.swap(0, up_sent)
    mixed_two = jnp.stack([pick(mixed_mine, y, 1 - x), pick(after(mixed_y, up_sent), 1 - x)])
    mixed_x = links.swap(0, mixed_two)
    out_y, gated_y = after((out_y, gated_y), up_sent)
    gate_traded = Traded(links, after(gate_low, up_sent))
    token = gate_traded.trade_x(mixed_two)
    input_grad = after(input_grad, token, out_y, gated_y)
    input_traded = Traded(links, input_grad)
    normed_a_grad = product("rt,dr->td", gate_low, w_gate)
    normed_a_grad = normed_a_grad + product("rt,dr->td", input_grad, w_input)
    token_norm_grad, gain_a_grad = norm_back_a(normed_a_grad)
    token_grad = middle_grad + token_norm_grad
    small = jnp.concatenate([gain_a_grad, gain_b_grad, sums])

    out_pieces = [
        (gated_mine, (CORE, Y), out_grad_low, ()),
        (gated_core, (Y,), out_core, ()),
        (gated_y, (0,), out_y, (0,)),
        (gated_y, (1,), out_y, (1,)),
    ]
    out_sent = grad_product(after(select, token_grad), out_pieces, rows_total // 8, OTHER_X)
    out_received = links.swap(0, out_sent)
    token = input_traded.trade_x(out_sent)
    hidden_sums = [(bit, 0) for bit in rest_bits]
    projection_sums = [(bit, 1) for bit in range(1, bit_count)]
    gate_total = hidden_product(0, Y, token, gate_received)
    gate_chain = Chain(links, [gate_total], hidden_sums, (0, "core"))
    gate_proj_total = gate_traded.grad(after(select, gate_total), normed_pieces)
    gate_proj = Chain(links, [gate_proj_total], projection_sums, (0, "core"), True)
    up_total = hidden_product(1, X, gate_proj_total, up_received)
    up_chain = Chain(links, [up_total], hidden_sums, (1, "core"))
    input_total = input_traded.grad(after(select, up_total), normed_pieces)
    input_chain = Chain(links, [input_total], projection_sums, (0, "core"), True, small)

    def down_product(chosen, token, added=None):
        lefts = [(mixed_mine, (Y, X, chosen)), (mixed_y, (X, chosen))]
        lefts += [(mixed_x, (k, chosen)) for k in range(2)]
        pieces = [left + right for left, right in zip(lefts, down_pieces)]
        return grad_product(after(select, token), pieces, mixed.shape[0] // 8, None, added)

    down_sent = down_product(OTHER_CORE, input_total)
    down_received = links.swap("core", down_sent)
    token = gate_chain.advance(down_sent)
    token = gate_proj.advance(token)
    down_total = down_product(CORE, token, down_received)
    down_chain = Chain(links, [down_total], hidden_sums)
    out_total = grad_product(after(select, down_total), out_pieces, rows_total // 8, X, out_received)
    out_chain = Chain(links, [out_total], hidden_sums)
    token = up_chain.advance(out_total)
    chains = [input_chain, gate_proj, gate_chain, out_chain, up_chain, down_chain]
    while any(chain.sums or chain.collects for chain in chains):
        for chain in chains:
            if chain.sums or chain.collects:
                token = chain.advance(token)
    param_sums = channel_sums(lane_sums, channels, decay_logits)
    param_sums = param_sums + links.swap("core", after(param_sums, up_sent))
    totals = input_chain.rider
    gain_size = width // (lax.axis_size("seq") * lax.axis_size("fsdp"))
    gain_start = (place * lax.axis_size("fsdp") + core) * gain_size
    return (
        output,
        token_grad,
        gate_proj.total(),
        input_chain.total(),
        out_chain.total(),
        gate_chain.total(),
        up_chain.total(),
        down_chain.total(),
        lax.dynamic_slice_in_dim(totals, gain_start, gain_size, 0),
        lax.dynamic_slice_in_dim(totals, width + gain_start, gain_size, 0),
        param_sums[:TAPS],
        param_sums[TAPS],
        param_sums[TAPS + 1 : TAPS + 3],
        param_sums[TAPS + 3 : TAPS + 5],
        param_sums[TAPS + 5],
        jnp.sqrt(totals[2 * width :] / entry_total),
    )


def solution(mesh):
    in_specs = (
        P(("seq", "fsdp"), None),
        P(("seq", "fsdp"), None),
        P("fsdp", None),
        P("fsdp", None),
        P("fsdp", None),
        P("fsdp", None),
        P("fsdp", None),
        P("fsdp", None),
        P("fsdp"),
        P("fsdp"),
        P(None, "seq"),
        P("seq"),
        P(None, "seq"),
        P(None, "seq"),
        P("seq"),
        P("fsdp", None),
        P("fsdp", None),
    )
    out_specs = (
        P(("seq", "fsdp"), None),
        P(("seq", "fsdp"), None),
        P(("seq", "fsdp"), None),
        P(("seq", "fsdp"), None),
        P(("seq", "fsdp"), None),
        P(("seq", "fsdp"), None),
        P(("seq", "fsdp"), None),
        P(("seq", "fsdp"), None),
        P(("seq", "fsdp")),
        P(("seq", "fsdp")),
        P(None, "seq"),
        P("seq"),
        P(None, "seq"),
        P(None, "seq"),
        P("seq"),
        P(),
    )
    return jax.shard_map(
        per_device, mesh=mesh, in_specs=in_specs, out_specs=out_specs, check_vma=False
    )
```

```python
from functools import partial

import jax
import jax.numpy as jnp
from jax import lax
from jax.experimental import pallas as pl
from jax.experimental.pallas import tpu as pltpu
from jax.sharding import PartitionSpec as P

NORM_EPS = 1e-06
RATE_SCALE = 8.0
LANES = 640
SUB = 8
TAPS = 4
UNROLL = 4
VMEM_LIMIT = 60 << 20


def gelu_tanh(values):
    return jax.nn.gelu(values, approximate=True)


def rms_norm(values, norm_gain):
    return (
        values * lax.rsqrt(jnp.mean(values * values, axis=-1, keepdims=True) + NORM_EPS) * norm_gain
    )


def gated_state(state_in, gate_pre):
    return state_in * gelu_tanh(gate_pre)


def mixing(first_pre, second_pre):
    return gelu_tanh(first_pre) * second_pre


def one_minus_exp_neg(u):
    series = jnp.ones_like(u)
    for k in range(9, 1, -1):
        series = 1.0 - u * (1.0 / k) * series
    return jnp.where(u < 0.5, u * series, 1.0 - jnp.exp(-u))


def logistic(values):
    return 1.0 / (1.0 + jnp.exp(-values))


def earlier_chunk(values, channels):
    rolled = pltpu.roll(values, 1, 0)
    wrapped = pltpu.roll(rolled, channels, 1) if channels < LANES else rolled
    sub = lax.broadcasted_iota(jnp.int32, values.shape, 0)
    lane = lax.broadcasted_iota(jnp.int32, values.shape, 1)
    shifted = jnp.where(sub == 0, wrapped, rolled)
    return jnp.where((sub == 0) & (lane < channels), 0.0, shifted)


def later_chunk(values, channels):
    rolled = pltpu.roll(values, SUB - 1, 0)
    wrapped = pltpu.roll(rolled, LANES - channels, 1) if channels < LANES else rolled
    sub = lax.broadcasted_iota(jnp.int32, values.shape, 0)
    lane = lax.broadcasted_iota(jnp.int32, values.shape, 1)
    shifted = jnp.where(sub == SUB - 1, wrapped, rolled)
    return jnp.where((sub == SUB - 1) & (lane >= LANES - channels), 0.0, shifted)


def place_rows(slot_ref, source, group, rows):
    here = slot_ref[source] - group * rows
    row = lax.broadcasted_iota(jnp.int32, (rows, here.shape[-1]), 0)
    return jnp.where(row == here, 1.0, 0.0).astype(jnp.bfloat16)


def into_order(data_ref, slot_ref, wide_ref, ordered_ref, first_row):
    sources, channels, _ = data_ref.shape
    rows = wide_ref.shape[1]
    for group in range(LANES // channels):

        def add_source(source, total, group=group):
            return total + lax.dot_general(
                data_ref[source],
                place_rows(slot_ref, source, group, rows),
                (((1,), (1,)), ((), ())),
                preferred_element_type=jnp.float32,
            )

        wide_ref[group * channels : (group + 1) * channels, :] = lax.fori_loop(
            0, sources, add_source, jnp.zeros((channels, rows), jnp.float32)
        )
    for start in range(0, rows, 128):
        ordered_ref[first_row + start : first_row + start + 128, :] = wide_ref[
            :, start : start + 128
        ].T


def out_of_order(ordered_ref, slot_ref, narrow_ref, data_ref):
    sources, channels, tokens = data_ref.shape
    groups, _, rows = narrow_ref.shape
    for start in range(0, rows, 128):
        wide = ordered_ref[start : start + 128, :].T
        for group in range(groups):
            narrow_ref[group, :, start : start + 128] = wide[
                group * channels : (group + 1) * channels, :
            ].astype(jnp.bfloat16)

    def one_source(source, carry):
        total = jnp.zeros((channels, tokens), jnp.float32)
        for group in range(groups):
            total = total + jnp.dot(
                narrow_ref[group],
                place_rows(slot_ref, source, group, rows),
                preferred_element_type=jnp.float32,
            )
        data_ref[source] = total.astype(jnp.bfloat16)
        return carry

    lax.fori_loop(0, sources, one_source, 0)


def forward_kernel(
    data_ref, slot_ref, offset_ref, params_ref,
    states_ref, inputs_ref, filtered_ref, decay_ref, hidden_ref,
    wide_ref, reach_ref, narrow_ref,
):
    channels = data_ref.shape[1]
    rows = hidden_ref.shape[0]
    pad = (TAPS - 1) * SUB
    into_order(data_ref, slot_ref, wide_ref, inputs_ref, pad)
    for tap in range(TAPS - 1):
        inputs_ref[tap * SUB : (tap + 1) * SUB, :] = earlier_chunk(
            inputs_ref[rows + tap * SUB : rows + (tap + 1) * SUB, :], channels
        )
    param = [params_ref[k : k + 1, :] for k in range(TAPS + 6)]
    block = UNROLL * SUB

    def local_steps(step, carry):
        state, reach = carry
        start = pl.multiple_of(step * block, block)
        offset = offset_ref[pl.ds(start, block), :]
        filtered = param[TAPS] + param[0] * inputs_ref[pl.ds(start + pad, block), :]
        for tap in range(1, TAPS):
            delayed = inputs_ref[pl.ds(start + pad - tap * SUB, block), :]
            filtered = filtered + param[tap] * jnp.where(offset >= tap, delayed, 0.0)
        recur_gate = logistic(param[TAPS + 1] * filtered + param[TAPS + 3])
        input_gate = logistic(param[TAPS + 2] * filtered + param[TAPS + 4])
        rate = param[TAPS + 5] * recur_gate
        decay = jnp.where(offset > 0, jnp.exp(-rate), 0.0)
        drive = jnp.sqrt(one_minus_exp_neg(2.0 * rate)) * input_gate * filtered
        filtered_ref[pl.ds(start, block), :] = filtered
        decay_ref[pl.ds(start, block), :] = decay
        for k in range(UNROLL):
            now = decay[k * SUB : (k + 1) * SUB, :]
            state = now * state + drive[k * SUB : (k + 1) * SUB, :]
            reach = now * reach
            hidden_ref[pl.ds(start + k * SUB, SUB), :] = state
            reach_ref[pl.ds(start + k * SUB, SUB), :] = reach
        return state, reach

    zeros = jnp.zeros((SUB, LANES), jnp.float32)
    last, reach = lax.fori_loop(0, rows // block, local_steps, (zeros, zeros + 1.0))
    chunks = SUB * (LANES // channels)
    entry = lax.fori_loop(
        0, chunks - 1, lambda _, entry: earlier_chunk(last + reach * entry, channels), zeros
    )
    entries = jnp.concatenate([entry] * UNROLL, axis=0)

    def carry_over(step, carry):
        start = pl.multiple_of(step * block, block)
        hidden_ref[pl.ds(start, block), :] += reach_ref[pl.ds(start, block), :] * entries
        return carry

    lax.fori_loop(0, rows // block, carry_over, 0)
    out_of_order(hidden_ref, slot_ref, narrow_ref, states_ref)


def backward_kernel(
    data_ref, slot_ref, offset_ref, params_ref, inputs_ref, filtered_ref, decay_ref, hidden_ref,
    grads_ref, sums_ref,
    wide_ref, back_ref, reach_ref, narrow_ref, filtered_grad_ref, later_offset_ref,
):
    channels = data_ref.shape[1]
    rows = hidden_ref.shape[0]
    pad = (TAPS - 1) * SUB
    into_order(data_ref, slot_ref, wide_ref, back_ref, 0)
    param = [params_ref[k : k + 1, :] for k in range(TAPS + 6)]
    block = UNROLL * SUB
    count = rows // block

    def local_steps(step, carry):
        passed, reach = carry
        start = pl.multiple_of((count - 1 - step) * block, block)
        decay = decay_ref[pl.ds(start, block), :]
        given = back_ref[pl.ds(start, block), :]
        for k in range(UNROLL - 1, -1, -1):
            back = given[k * SUB : (k + 1) * SUB, :] + passed
            back_ref[pl.ds(start + k * SUB, SUB), :] = back
            reach_ref[pl.ds(start + k * SUB, SUB), :] = reach
            now = decay[k * SUB : (k + 1) * SUB, :]
            passed = now * back
            reach = now * reach
        return passed, reach

    zeros = jnp.zeros((SUB, LANES), jnp.float32)
    first, reach = lax.fori_loop(0, count, local_steps, (zeros, zeros + 1.0))
    chunks = SUB * (LANES // channels)
    entry = lax.fori_loop(
        0, chunks - 1, lambda _, entry: later_chunk(first + reach * entry, channels), zeros
    )
    entries = jnp.concatenate([entry] * UNROLL, axis=0)
    sums_ref[...] = jnp.zeros_like(sums_ref)
    before_first = earlier_chunk(hidden_ref[rows - SUB : rows, :], channels)

    def add_up(index, values):
        total = values[:SUB, :]
        for k in range(1, UNROLL):
            total = total + values[k * SUB : (k + 1) * SUB, :]
        sums_ref[index] += total

    def through_gates(step, before):
        start = pl.multiple_of(step * block, block)
        offset = offset_ref[pl.ds(start, block), :]
        filtered = filtered_ref[pl.ds(start, block), :]
        hidden = hidden_ref[pl.ds(start, block), :]
        earlier = jnp.concatenate([before, hidden[: block - SUB, :]], axis=0)
        back = back_ref[pl.ds(start, block), :] + reach_ref[pl.ds(start, block), :] * entries
        recur_gate = logistic(param[TAPS + 1] * filtered + param[TAPS + 3])
        input_gate = logistic(param[TAPS + 2] * filtered + param[TAPS + 4])
        rate = param[TAPS + 5] * recur_gate
        decay = decay_ref[pl.ds(start, block), :]
        squared = one_minus_exp_neg(2.0 * rate)
        scale_inv = lax.rsqrt(jnp.maximum(squared, 1e-37))
        scale = squared * scale_inv
        scale_grad = back * input_gate * filtered
        input_gate_grad = back * scale * filtered
        rate_grad = scale_grad * (1.0 - squared) * scale_inv - decay * back * earlier
        recur_pre_grad = rate_grad * param[TAPS + 5] * recur_gate * (1.0 - recur_gate)
        input_pre_grad = input_gate_grad * input_gate * (1.0 - input_gate)
        filtered_grad = (
            back * scale * input_gate
            + recur_pre_grad * param[TAPS + 1]
            + input_pre_grad * param[TAPS + 2]
        )
        filtered_grad_ref[pl.ds(start, block), :] = filtered_grad
        add_up(0, filtered_grad * inputs_ref[pl.ds(start + pad, block), :])
        for tap in range(1, TAPS):
            delayed = inputs_ref[pl.ds(start + pad - tap * SUB, block), :]
            add_up(tap, filtered_grad * jnp.where(offset >= tap, delayed, 0.0))
        add_up(TAPS, filtered_grad)
        add_up(TAPS + 1, recur_pre_grad * filtered)
        add_up(TAPS + 2, input_pre_grad * filtered)
        add_up(TAPS + 3, recur_pre_grad)
        add_up(TAPS + 4, input_pre_grad)
        add_up(TAPS + 5, rate_grad * recur_gate)
        return hidden[block - SUB :, :]

    lax.fori_loop(0, count, through_gates, before_first)
    for tap in range(TAPS - 1):
        rows_here = slice(tap * SUB, (tap + 1) * SUB)
        filtered_grad_ref[rows + tap * SUB : rows + (tap + 1) * SUB, :] = later_chunk(
            filtered_grad_ref[rows_here, :], channels
        )
        later_offset_ref[block + tap * SUB : block + (tap + 1) * SUB, :] = later_chunk(
            offset_ref[rows_here, :], channels
        )
    later_offset_ref[:block, :] = offset_ref[rows - block :, :]

    def through_taps(start, offsets_ref, offset_start):
        total = param[0] * filtered_grad_ref[pl.ds(start, block), :]
        for tap in range(1, TAPS):
            later = filtered_grad_ref[pl.ds(start + tap * SUB, block), :]
            offset = offsets_ref[pl.ds(offset_start + tap * SUB, block), :]
            total = total + param[tap] * jnp.where(offset >= tap, later, 0.0)
        back_ref[pl.ds(start, block), :] = total

    def inner_taps(step, carry):
        start = pl.multiple_of(step * block, block)
        through_taps(start, offset_ref, start)
        return carry

    lax.fori_loop(0, count - 1, inner_taps, 0)
    through_taps(rows - block, later_offset_ref, 0)
    out_of_order(back_ref, slot_ref, narrow_ref, grads_ref)


def shapes_of(data):
    sources, channels, tokens = data.shape
    rows = sources * tokens * channels // LANES
    return sources, channels, tokens, rows


def recurrence_forward(data, slot, offset, params):
    sources, channels, tokens, rows = shapes_of(data)
    whole = jax.ShapeDtypeStruct((rows, LANES), jnp.float32)
    padded = jax.ShapeDtypeStruct((rows + (TAPS - 1) * SUB, LANES), jnp.float32)
    count = sources * tokens
    return pl.pallas_call(
        forward_kernel,
        out_shape=(jax.ShapeDtypeStruct(data.shape, jnp.bfloat16), padded, whole, whole, whole),
        scratch_shapes=[
            pltpu.VMEM((LANES, rows), jnp.float32),
            pltpu.VMEM((rows, LANES), jnp.float32),
            pltpu.VMEM((LANES // channels, channels, rows), jnp.bfloat16),
        ],
        compiler_params=pltpu.CompilerParams(vmem_limit_bytes=VMEM_LIMIT),
        cost_estimate=pl.CostEstimate(
            flops=0, bytes_accessed=0, transcendentals=0
        ),
        name="recurrence_forward",
    )(data, slot, offset, params)


def recurrence_backward(data, slot, offset, params, inputs, filtered, decay, hidden):
    sources, channels, tokens, rows = shapes_of(data)
    count = sources * tokens
    return pl.pallas_call(
        backward_kernel,
        out_shape=(
            jax.ShapeDtypeStruct(data.shape, jnp.bfloat16),
            jax.ShapeDtypeStruct((TAPS + 6, SUB, LANES), jnp.float32),
        ),
        scratch_shapes=[
            pltpu.VMEM((LANES, rows), jnp.float32),
            pltpu.VMEM((rows, LANES), jnp.float32),
            pltpu.VMEM((rows, LANES), jnp.float32),
            pltpu.VMEM((LANES // channels, channels, rows), jnp.bfloat16),
            pltpu.VMEM((rows + (TAPS - 1) * SUB, LANES), jnp.float32),
            pltpu.VMEM((UNROLL * SUB + (TAPS - 1) * SUB, LANES), jnp.float32),
        ],
        compiler_params=pltpu.CompilerParams(vmem_limit_bytes=VMEM_LIMIT),
        cost_estimate=pl.CostEstimate(
            flops=0, bytes_accessed=0, transcendentals=0
        ),
        name="recurrence_backward",
    )(data, slot, offset, params, inputs, filtered, decay, hidden)


def arrangement(lengths, permutation, sources, channels):
    total = permutation.shape[0]
    groups = LANES // channels
    rows = total // groups
    steps = rows // SUB
    chunk = permutation // steps
    slot = (chunk // SUB) * rows + (permutation % steps) * SUB + chunk % SUB
    seq_ends = jnp.cumsum(lengths)
    seq_starts = seq_ends - lengths
    position = jnp.arange(total, dtype=jnp.int32)
    inside = position[:, None] >= seq_starts[None, :]
    seg_first = jnp.max(jnp.where(inside, seq_starts[None, :], 0), axis=1)
    offset = jnp.minimum(position - seg_first, TAPS - 1).astype(jnp.float32)
    offset = offset.reshape(groups, SUB, steps).transpose(2, 1, 0).reshape(rows, groups, 1)
    offset = jnp.broadcast_to(offset, (rows, groups, channels)).reshape(rows, LANES)
    return slot.reshape(sources, 1, total // sources), offset


def lane_params(conv_weight, conv_bias, gate_weight, gate_bias, decay_logits):
    stacked = jnp.concatenate(
        [
            conv_weight,
            conv_bias[None],
            gate_weight,
            gate_bias,
            RATE_SCALE * jax.nn.softplus(-decay_logits)[None],
        ]
    )
    return jnp.tile(stacked, (1, LANES // stacked.shape[1]))


def channel_sums(sums, channels, decay_logits):
    sums = jnp.sum(sums, axis=1).reshape(TAPS + 6, LANES // channels, channels).sum(axis=1)
    logit = -RATE_SCALE * jax.nn.sigmoid(-decay_logits)[None] * sums[TAPS + 5 :]
    return jnp.concatenate([sums[: TAPS + 5], logit])


def swap_core(values):
    return lax.ppermute(values, "fsdp", [(0, 1), (1, 0)])


def swap_bit(values, bit):
    count = lax.axis_size("seq")
    return lax.ppermute(values, "seq", [(i, i ^ (1 << bit)) for i in range(count)])


def half(values, index, axis):
    size = values.shape[axis] // 2
    return lax.dynamic_slice_in_dim(values, index * size, size, axis)


def reorder_blocks(values, low_bit, high_bit, axis):
    width = high_bit - low_bit
    size = values.shape[axis] >> width
    pieces = []
    for place in range(1 << width):
        natural = sum(((place >> (width - 1 - k)) & 1) << k for k in range(width))
        pieces.append(lax.slice_in_dim(values, natural * size, (natural + 1) * size, axis=axis))
    return jnp.concatenate(pieces, axis=axis)


def trade_channels(values):
    return lax.all_to_all(values, "seq", split_axis=0, concat_axis=0, tiled=True)


def after(values, *earlier):
    return lax.optimization_barrier((values,) + earlier)[0]


def product(subscripts, left, right):
    return jnp.einsum(subscripts, left, right, preferred_element_type=jnp.float32)


class Links:
    def __init__(self, place, core):
        count = lax.axis_size("seq").bit_length() - 1
        self.core = core
        self.bits = [(place >> bit) & 1 for bit in range(count)]

    def own(self, link):
        return self.core if link == "core" else self.bits[link]

    def swap(self, link, values, *earlier):
        if earlier:
            values = after(values, *earlier)
        return swap_core(values) if link == "core" else swap_bit(values, link)


class Chain:
    def __init__(self, links, terms, sums, collects=(), turn=False, rider=None):
        self.links, self.terms, self.rider = links, list(terms), rider
        self.sums, self.collects, self.turn = list(sums), list(collects), turn
        self.send()

    def total(self):
        return sum(term.astype(jnp.float32) for term in self.terms)

    def send(self):
        if self.sums:
            self.link, self.axis = self.sums[0]
        elif self.collects:
            total = self.total()
            self.terms = [total.T if self.turn else total]
            self.turn = False
            self.link, self.axis = self.collects[0], 0
        else:
            return
        own_bit = self.links.own(self.link)
        sent = sum(half(term, 1 - own_bit, self.axis).astype(jnp.float32) for term in self.terms)
        self.sent = sent.astype(jnp.bfloat16)
        self.other = self.links.swap(self.link, self.sent)
        self.terms = [half(term, own_bit, self.axis) for term in self.terms]
        if self.rider is not None:
            self.rider_other = self.links.swap(self.link, self.rider)

    def advance(self, token):
        other = after(self.other, token)
        if self.rider is not None:
            self.rider = self.rider + after(self.rider_other, token)
        if self.sums:
            self.terms.append(other)
            self.sums.pop(0)
        else:
            own, other = self.terms[0], other.astype(jnp.float32)
            first = self.links.own(self.link) == 0
            low, high = jnp.where(first, own, other), jnp.where(first, other, own)
            self.terms = [jnp.concatenate([low, high], axis=1)]
            self.collects.pop(0)
        if not self.sums and not self.collects:
            return token
        self.send()
        return self.sent


def both_cores(values, *earlier):
    return lax.all_gather(after(values, *earlier) if earlier else values, "fsdp")


def pick(values, *index):
    for place in index:
        values = lax.dynamic_index_in_dim(values, place, 0, keepdims=False)
    return values


def largest_tile(size, most, step):
    return max(tile for tile in range(step, most + 1, step) if size % tile == 0)


def grad_kernel(count, turned, select_ref, *refs):
    per_piece = turned or 1
    lefts = [ref[...] for ref in refs[: count * per_piece]]
    rights = [ref[...] for ref in refs[count * per_piece : count * (per_piece + 1)]]
    rights = jnp.concatenate(rights, axis=0)
    if turned:
        if per_piece > 1:
            lefts = [
                jnp.concatenate(lefts[k * per_piece : (k + 1) * per_piece], axis=1)
                for k in range(count)
            ]
        total = lax.dot_general(
            jnp.concatenate(lefts, axis=0),
            rights,
            (((0,), (0,)), ((), ())),
            preferred_element_type=jnp.float32,
        )
    else:
        total = jnp.dot(
            jnp.concatenate(lefts, axis=1), rights, preferred_element_type=jnp.float32
        )
    for ref in refs[count * (per_piece + 1) : -1]:
        total = total + ref[...].astype(jnp.float32)
    refs[-1][...] = total.astype(jnp.bfloat16)


(CORE, OTHER_CORE), (X, OTHER_X), (Y, OTHER_Y), (LOW, OTHER_LOW), (TOP, OTHER_TOP) = (
    (("scalar", 2 * k), ("scalar", 2 * k + 1)) for k in range(5)
)


def grad_product(select, pieces, rows, row_half=None, added=None, columns=None):
    cols = pieces[0][2].shape[-1]
    tile_rows = largest_tile(rows, 512, 16) if columns is None else rows // columns[0]
    tile_cols = largest_tile(cols, 1024 if columns is None else 1536, 256)

    def entry(index, select_ref):
        return select_ref[index[1]] if isinstance(index, tuple) else index

    def left_spec(left, lead):
        def place(m, n, select_ref):
            start = 0 if row_half is None else entry(row_half, select_ref) * (rows // tile_rows)
            return tuple(entry(i, select_ref) for i in lead) + (start + m, 0)

        return pl.BlockSpec((None,) * len(lead) + (tile_rows, left.shape[-1]), place)

    def column_spec(left, lead, which):
        def place(m, n, select_ref):
            block = columns[2](m, partial(entry, select_ref=select_ref))[which]
            return tuple(entry(i, select_ref) for i in lead) + (0, block)

        return pl.BlockSpec((None,) * len(lead) + (left.shape[-2], columns[1]), place)

    def right_spec(right, lead):
        def place(m, n, select_ref):
            return tuple(entry(i, select_ref) for i in lead) + (0, n)

        return pl.BlockSpec((None,) * len(lead) + (right.shape[-2], tile_cols), place)

    out_spec = pl.BlockSpec((tile_rows, tile_cols), lambda m, n, select_ref: (m, n))
    turned = 0 if columns is None else tile_rows // columns[1]
    if turned:
        in_specs = [column_spec(p[0], p[1], which) for p in pieces for which in range(turned)]
        operands = [p[0] for p in pieces for _ in range(turned)]
    else:
        in_specs = [left_spec(left, lead) for left, lead, _, _ in pieces]
        operands = [left for left, _, _, _ in pieces]
    in_specs += [right_spec(right, lead) for _, _, right, lead in pieces]
    operands += [right for _, _, right, _ in pieces]
    if added is not None:
        in_specs.append(out_spec)
        operands.append(added)
    return pl.pallas_call(
        partial(grad_kernel, len(pieces), turned),
        out_shape=jax.ShapeDtypeStruct((rows, cols), jnp.bfloat16),
        grid_spec=pltpu.PrefetchScalarGridSpec(
            num_scalar_prefetch=1,
            grid=(rows // tile_rows, cols // tile_cols),
            in_specs=in_specs,
            out_specs=out_spec,
        ),
        compiler_params=pltpu.CompilerParams(vmem_limit_bytes=VMEM_LIMIT),
        cost_estimate=pl.CostEstimate(flops=0, bytes_accessed=0, transcendentals=0),
        name="weight_grad",
    )(select, *operands)


GELU_SCALE = 0.7978845608028654
GELU_CUBE = 0.044715
HIDDEN_TILE = 768


def mlp_kernel(
    bits_ref, normed_ref, down_grad_ref, gate_ref, up_ref, down_ref,
    branch_ref, normed_grad_ref, mixed_ref, sent_gate_ref, sent_up_ref, kept_gate_ref, kept_up_ref,
):
    step = pl.program_id(0)
    by_columns = (((1,), (1,)), ((), ()))
    normed = normed_ref[...]
    first = jnp.dot(normed, gate_ref[...], preferred_element_type=jnp.float32)
    second = jnp.dot(normed, up_ref[...], preferred_element_type=jnp.float32)
    mixed_grad = lax.dot_general(
        down_grad_ref[...], down_ref[...], by_columns, preferred_element_type=jnp.float32
    )
    square = first * first
    bend = jnp.tanh(GELU_SCALE * first * (1.0 + GELU_CUBE * square))
    rise = 0.5 + 0.5 * bend
    gelu = first * rise
    slope = rise + 0.5 * GELU_SCALE * first * (1.0 - bend * bend) * (
        1.0 + 3.0 * GELU_CUBE * square
    )
    mixed = gelu * second
    first_low = (mixed_grad * slope * second).astype(jnp.bfloat16)
    second_low = (mixed_grad * gelu).astype(jnp.bfloat16)
    mixed_ref[...] = mixed.T.astype(jnp.bfloat16)

    side = (step // (pl.num_programs(0) // 4)) % 2
    for which, low, sent_ref, kept_ref in (
        (0, first_low, sent_gate_ref, kept_gate_ref),
        (1, second_low, sent_up_ref, kept_up_ref),
    ):

        @pl.when(side != bits_ref[which])
        def _(low=low, sent_ref=sent_ref):
            sent_ref[...] = low

        @pl.when(side == bits_ref[which])
        def _(low=low, kept_ref=kept_ref):
            kept_ref[...] = low

    @pl.when(step == 0)
    def _():
        branch_ref[...] = jnp.zeros_like(branch_ref)
        normed_grad_ref[...] = jnp.zeros_like(normed_grad_ref)

    branch_ref[...] += jnp.dot(
        mixed.astype(jnp.bfloat16), down_ref[...], preferred_element_type=jnp.float32
    )
    normed_grad_ref[...] += lax.dot_general(
        first_low, gate_ref[...], by_columns, preferred_element_type=jnp.float32
    ) + lax.dot_general(second_low, up_ref[...], by_columns, preferred_element_type=jnp.float32)


def mlp_both_ways(bits, normed, down_grad, w_gate, w_up, w_down):
    count, width = normed.shape
    hidden = w_gate.shape[1]
    steps = hidden // HIDDEN_TILE
    tiles = steps // 4

    whole = pl.BlockSpec((count, width), lambda t, bits_ref: (0, 0))
    column = pl.BlockSpec((width, HIDDEN_TILE), lambda t, bits_ref: (0, t))
    row = pl.BlockSpec((HIDDEN_TILE, width), lambda t, bits_ref: (t, 0))
    turned = pl.BlockSpec((HIDDEN_TILE, count), lambda t, bits_ref: (t, 0))

    def traded(which, kept):
        def place(t, bits_ref):
            wanted = bits_ref[which] if kept else 1 - bits_ref[which]
            side = (t // tiles) % 2
            resting = jnp.where(wanted == 0, tiles - 1, 0)
            return (t // (2 * tiles), 0, jnp.where(side == wanted, t % tiles, resting))

        return pl.BlockSpec((None, count, HIDDEN_TILE), place)

    summed = jax.ShapeDtypeStruct((count, width), jnp.float32)
    return pl.pallas_call(
        mlp_kernel,
        out_shape=(summed, summed, jax.ShapeDtypeStruct((hidden, count), jnp.bfloat16))
        + (jax.ShapeDtypeStruct((2, count, hidden // 4), jnp.bfloat16),) * 4,
        grid_spec=pltpu.PrefetchScalarGridSpec(
            num_scalar_prefetch=1,
            grid=(steps,),
            in_specs=[whole, whole, column, column, row],
            out_specs=[whole, whole, turned]
            + [traded(which, kept) for kept in (False, True) for which in (0, 1)],
        ),
        compiler_params=pltpu.CompilerParams(vmem_limit_bytes=VMEM_LIMIT),
        cost_estimate=pl.CostEstimate(flops=0, bytes_accessed=0, transcendentals=0),
        name="mlp_both_ways",
    )(jnp.stack(bits).astype(jnp.int32), normed, down_grad, w_gate, w_up, w_down)


MIDDLE_TILE = 512


def middle_kernel(
    normed_grad_ref, middle_ref, cotangent_ref, gain_ref, output_ref, gate_ref, state_ref, pre_ref,
    middle_grad_ref, out_grad_ref, gain_grad_ref, state_grad_ref, gate_grad_ref, back_ref,
):
    by_columns = (((1,), (1,)), ((), ()))

    @pl.when(pl.program_id(0) == 0)
    def _():
        middle = middle_ref[...]
        normed_grad = normed_grad_ref[...]
        inverse = lax.rsqrt(jnp.mean(middle * middle, axis=1, keepdims=True) + NORM_EPS)
        scaled = normed_grad * gain_ref[...]
        lean = jnp.mean(scaled * middle, axis=1, keepdims=True)
        total = cotangent_ref[...] + inverse * scaled - middle * (inverse * inverse * inverse * lean)
        middle_grad_ref[...] = total
        out_grad_ref[...] = total.astype(jnp.bfloat16)
        gain_grad_ref[...] = jnp.sum(normed_grad * middle * inverse, axis=0, keepdims=True)
        back_ref[...] = jnp.zeros_like(back_ref)

    grad = lax.dot_general(
        output_ref[...], out_grad_ref[...], by_columns, preferred_element_type=jnp.float32
    )
    pre = pre_ref[...]
    square = pre * pre
    bend = jnp.tanh(GELU_SCALE * pre * (1.0 + GELU_CUBE * square))
    rise = 0.5 + 0.5 * bend
    slope = rise + 0.5 * GELU_SCALE * pre * (1.0 - bend * bend) * (1.0 + 3.0 * GELU_CUBE * square)
    state_grad_ref[...] = (grad * pre * rise).astype(jnp.bfloat16)
    gate_grad = (grad * state_ref[...].astype(jnp.float32) * slope).astype(jnp.bfloat16)
    gate_grad_ref[...] = gate_grad
    back_ref[...] += lax.dot_general(
        gate_grad, gate_ref[...], (((0,), (1,)), ((), ())), preferred_element_type=jnp.float32
    )


def middle_backward(normed_grad, middle, cotangent, gain, w_output, w_gate, states, gate_pre):
    count, width = middle.shape
    channels = w_output.shape[0]
    whole = pl.BlockSpec((count, width), lambda t: (0, 0))
    line = pl.BlockSpec((1, width), lambda t: (0, 0))
    row = pl.BlockSpec((MIDDLE_TILE, width), lambda t: (t, 0))
    column = pl.BlockSpec((width, MIDDLE_TILE), lambda t: (0, t))
    turned = pl.BlockSpec((MIDDLE_TILE, count), lambda t: (t, 0))
    wide = jax.ShapeDtypeStruct((count, width), jnp.float32)
    low = jax.ShapeDtypeStruct((channels, count), jnp.bfloat16)
    return pl.pallas_call(
        middle_kernel,
        out_shape=(
            wide,
            jax.ShapeDtypeStruct((count, width), jnp.bfloat16),
            jax.ShapeDtypeStruct((1, width), jnp.float32),
            low,
            low,
            wide,
        ),
        grid=(channels // MIDDLE_TILE,),
        in_specs=[whole, whole, whole, line, row, column, turned, turned],
        out_specs=[whole, whole, line, turned, turned, whole],
        compiler_params=pltpu.CompilerParams(vmem_limit_bytes=VMEM_LIMIT),
        cost_estimate=pl.CostEstimate(flops=0, bytes_accessed=0, transcendentals=0),
        name="middle_backward",
    )(normed_grad, middle, cotangent, gain, w_output, w_gate, states, gate_pre)


class Traded:
    def __init__(self, links, channel_grad):
        channels, count = channel_grad.shape
        self.links = links
        self.mine = channel_grad.reshape(2, 2, channels // 4, count)
        self.by_core = links.swap("core", pick(self.mine, 1 - links.core))

    def trade_x(self, token):
        core, other = self.links.core, 1 - self.links.bits[0]
        self.by_core = after(self.by_core, token)
        sent = jnp.stack([pick(self.mine, core, other), pick(self.by_core, other)])
        self.by_x = self.links.swap(0, sent)
        return sent

    def grad(self, select, normed_pieces):
        lefts = [(self.mine, (CORE, X)), (self.by_core, (X,)), (self.by_x, (0,)), (self.by_x, (1,))]
        pieces = [left + right for left, right in zip(lefts, normed_pieces)]
        return grad_product(select, pieces, self.mine.shape[2])


def per_device(
    tokens,
    cotangent,
    gate_proj,
    input_proj,
    output_proj,
    mlp_gate,
    mlp_up,
    mlp_down,
    gain_a,
    gain_b,
    conv_weight,
    conv_bias,
    gate_weight,
    gate_bias,
    decay_logits,
    lengths,
    permutation,
):
    w_gate, w_input, w_output, w_mlpgate, w_mlpup, w_down = (
        lax.all_gather(gate_proj, "fsdp", axis=0, tiled=True),
        lax.all_gather(input_proj, "fsdp", axis=0, tiled=True),
        lax.all_gather(output_proj, "fsdp", axis=0, tiled=True),
        lax.all_gather(mlp_gate, "fsdp", axis=0, tiled=True),
        lax.all_gather(mlp_up, "fsdp", axis=0, tiled=True),
        lax.all_gather(mlp_down, "fsdp", axis=0, tiled=True),
    )
    core = lax.axis_index("fsdp")
    place = lax.axis_index("seq")
    links = Links(place, core)
    x, y = links.bits[0], links.bits[1]
    bit_count = len(links.bits)
    top = bit_count - 1
    low = links.bits[2]
    own_bits = (core, x, y, low, links.bits[top])
    select = jnp.stack([value for bit in own_bits for value in (bit, 1 - bit)]).astype(jnp.int32)
    channels = decay_logits.shape[0]
    count, width = tokens.shape
    block_shape = (lax.axis_size("seq"), channels, count)
    slot, offset = arrangement(lengths[0], permutation[0], block_shape[0], channels)
    params = lane_params(conv_weight, conv_bias, gate_weight, gate_bias, decay_logits)
    gains = jnp.stack([gain_a, gain_b])
    other_gains = links.swap("core", gains)
    full_gain_a, full_gain_b = jnp.where(
        core == 0,
        jnp.concatenate([gains, other_gains], axis=1),
        jnp.concatenate([other_gains, gains], axis=1),
    )
    other_input = links.swap("core", input_proj)
    normed_a, norm_back_a = jax.vjp(rms_norm, tokens, full_gain_a.astype(jnp.float32))
    normed_a_low = normed_a.astype(jnp.bfloat16)
    down_grad = cotangent.astype(jnp.bfloat16)
    input_pre = product("td,dr->rt", half(normed_a_low, core, 1), input_proj)
    input_pre = input_pre + product("td,dr->rt", half(normed_a_low, 1 - core, 1), other_input)
    channel_in = trade_channels(input_pre.astype(jnp.bfloat16))
    gate_pre = product("td,dr->rt", normed_a_low, w_gate)
    normed_order = reorder_blocks(normed_a_low, 1, bit_count, 1)
    normed_core = both_cores(normed_order, channel_in)
    channel_in, gate_pre = lax.optimization_barrier((channel_in, gate_pre))
    down_y = links.swap(1, down_grad, channel_in)
    down_top = links.swap(top, down_grad, channel_in)
    normed_x = links.swap(0, normed_order, channel_in)
    states, *kept = recurrence_forward(channel_in.reshape(block_shape), slot, offset, params)
    states = after(states, normed_x, down_y, down_top)
    state_tokens = trade_channels(states.reshape(input_pre.shape))
    normed_both = both_cores(normed_x, states)
    normed_pieces = [(normed_order, ()), (normed_core, (OTHER_CORE,))]
    normed_pieces += [(normed_x, ()), (normed_both, (OTHER_CORE,))]
    gated_low = gated_state(state_tokens.astype(jnp.float32), gate_pre).astype(jnp.bfloat16)
    branch_a = product("rt,rd->td", gated_low, w_output)
    middle = tokens + branch_a
    gain_b_wide = full_gain_b.astype(jnp.float32)
    normed_b_low = rms_norm(middle, gain_b_wide).astype(jnp.bfloat16)
    rows_total = gated_low.shape[0]
    shape = (2,) * bit_count + (2, rows_total // (2 << bit_count), count)
    rest = tuple(range(bit_count - 3, -1, -1))
    out_order = (2, 0, 1, *range(3, bit_count))
    dims = (bit_count, *(top - bit for bit in out_order), bit_count + 1, bit_count + 2)
    shape_out, dims_out = shape, dims
    fars = [links.swap(bit, normed_b_low) for bit in (0, 2)]
    down_both = links.swap(top, after(down_y, normed_b_low))
    down_pieces = [(piece, ()) for piece in (down_grad, down_y, down_top, down_both)]
    mlp_parts = mlp_both_ways((x, low), normed_b_low, down_grad, w_mlpgate, w_mlpup, w_down)
    arrived = lax.optimization_barrier((*mlp_parts, down_both, *fars))
    branch_b, normed_b_grad, mixed, sent_gate, sent_up, kept_gate, kept_up = arrived[:7]
    fars = arrived[8:]
    hidden_far = [links.swap(0, sent_gate), links.swap(2, sent_up)]
    shape = (2,) * bit_count + (2, mixed.shape[0] // (2 << bit_count), count)
    axes = [top - bit for bit in (1, top)] + [bit_count] + [top - bit for bit in (0, *range(2, top))]
    mixed_mine = mixed.reshape(shape).transpose(axes + [bit_count + 1, bit_count + 2])
    mixed_mine = mixed_mine.reshape(2, 2, 2, mixed.shape[0] // 8, count)
    mixed_y = links.swap(1, pick(mixed_mine, 1 - y))
    output = middle + branch_b
    sums = jnp.stack(
        (
            jnp.sum(tokens * tokens),
            jnp.sum(branch_a * branch_a),
            jnp.sum(middle * middle),
            jnp.sum(branch_b * branch_b),
        )
    )
    entry_total = tokens.shape[0] * tokens.shape[1] * lax.axis_size("seq") * lax.axis_size("fsdp")
    middle_grad, out_grad_low, gain_b_grad, state_low, gate_low, gate_part = middle_backward(
        normed_b_grad,
        middle,
        cotangent,
        gain_b_wide[None],
        w_output,
        w_gate,
        state_tokens,
        gate_pre,
    )
    arrived = lax.optimization_barrier((state_low, gate_low, out_grad_low, *hidden_far, mixed_y))
    state_low, gate_low, out_grad_low, *hidden_far, mixed_y = arrived
    gain_b_grad = gain_b_grad[0]
    channel_grad = trade_channels(state_low)

    normed_b_core = both_cores(normed_b_low)
    hidden_pieces = []
    for index in (0, 1):
        mine, far = (kept_gate, kept_up)[index], hidden_far[index]
        far_core = both_cores(fars[index])
        both = jnp.stack([pick(mine, 1 - core), pick(after(far, state_low), 1 - core)])
        by_core = links.swap("core", both)
        hidden_pieces.append(
            [
                (normed_b_low, (), mine, (CORE,)),
                (fars[index], (), far, (CORE,)),
                (normed_b_core, (OTHER_CORE,), by_core, (0,)),
                (far_core, (OTHER_CORE,), by_core, (1,)),
            ]
        )
    aligned = (width >> bit_count) % 128 == 0
    hidden_orders = ((1, (*range(2, bit_count),), 0), (0, (1, *range(3, bit_count)), 2))
    if not aligned:
        for pieces, (summed, between, traded_bit) in zip(hidden_pieces, hidden_orders):
            for k, (left, lead, right, right_lead) in enumerate(pieces):
                split = left.reshape(left.shape[:-1] + (2,) * bit_count + (width >> bit_count,))
                first = left.ndim - 1
                axes = [first + top - bit for bit in (summed, *between, traded_bit)]
                axes = tuple(range(first)) + tuple(axes) + (first + bit_count,)
                split = split.transpose(axes).reshape(left.shape)
                pieces[k] = (jnp.swapaxes(split, -1, -2), lead, right, right_lead)

    def hidden_product(index, half_rows, token, added=None):
        chosen = after(select, token)
        if not aligned:
            return grad_product(chosen, hidden_pieces[index], width // 2, half_rows, added)
        summed, between, traded_bit = hidden_orders[index]

        def blocks(m, entry):
            place = entry(half_rows) << summed
            for k, bit in enumerate(reversed(between)):
                place = place + (((m >> k) & 1) << bit)
            return [place >> 1] if traded_bit == 0 else [place, place + (1 << traded_bit)]

        columns = (1 << len(between), width >> (bit_count - (traded_bit == 0)), blocks)
        return grad_product(chosen, hidden_pieces[index], width // 2, None, added, columns)

    rest_bits = range(2, bit_count)
    mixed_two = jnp.stack(
        [pick(mixed_mine, y, 1 - own_bits[4]), pick(mixed_y, 1 - own_bits[4])]
    )
    gate_traded = Traded(links, gate_low)
    gate_traded.trade_x(state_low)
    gated_mine = after(gated_low, state_low).reshape(shape_out).transpose(dims_out)
    gated_mine = gated_mine.reshape(2, 2, rows_total // 4, count)
    gated_core = links.swap("core", pick(gated_mine, 1 - core))
    gated_two = jnp.stack([pick(gated_mine, core, 1 - low), pick(gated_core, 1 - low)])
    channel_grad = after(channel_grad, mixed_two, gated_two, gate_traded.by_x)
    gate_sent = hidden_product(0, OTHER_Y, channel_grad)
    gate_received = links.swap(1, gate_sent)
    up_sent = hidden_product(1, OTHER_X, gate_sent)
    up_received = links.swap(0, up_sent)
    mixed_far = links.swap(top, mixed_two, channel_grad)
    out_far = links.swap(2, out_grad_low, channel_grad)
    gated_far = links.swap(2, gated_two, channel_grad)
    channel_grad = after(channel_grad, up_sent)

    dealt_grad, lane_sums = recurrence_backward(
        channel_grad.reshape(block_shape), slot, offset, params, *kept
    )
    dealt_grad = after(dealt_grad, gate_received, up_received, mixed_far, out_far, gated_far)
    input_grad = trade_channels(dealt_grad.reshape(state_low.shape))
    def down_product(chosen, token, added=None):
        lefts = [(mixed_mine, (Y, TOP, chosen)), (mixed_y, (TOP, chosen))]
        lefts += [(mixed_far, (k, chosen)) for k in range(2)]
        pieces = [left + right for left, right in zip(lefts, down_pieces)]
        return grad_product(after(select, token), pieces, mixed.shape[0] // 8, None, added)

    hidden_sums = [(bit, 0) for bit in rest_bits]
    projection_sums = [(bit, 1) for bit in range(1, bit_count)]
    gate_total = hidden_product(0, Y, dealt_grad, gate_received)
    gate_chain = Chain(links, [gate_total], hidden_sums, (0, "core"))
    up_total = hidden_product(1, X, gate_total, up_received)
    up_sums = [(bit, 0) for bit in (1, *range(3, bit_count))]
    up_chain = Chain(links, [up_total], up_sums, (2, "core"))
    down_sent = down_product(OTHER_CORE, up_total)
    down_received = links.swap("core", down_sent)
    input_grad = after(input_grad, down_sent)
    input_traded = Traded(links, input_grad)
    token = input_traded.trade_x(input_grad)
    gate_proj_total = gate_traded.grad(after(select, token), normed_pieces)
    out_core = both_cores(out_grad_low, dealt_grad)
    out_both = both_cores(out_far, dealt_grad)
    out_pieces = [
        (gated_mine, (CORE, LOW), out_grad_low, ()),
        (gated_core, (LOW,), out_core, (OTHER_CORE,)),
        (gated_far, (0,), out_far, ()),
        (gated_far, (1,), out_both, (OTHER_CORE,)),
    ]
    out_token = after(select, gate_proj_total)
    out_sent = grad_product(out_token, out_pieces, rows_total // 8, OTHER_X)
    out_received = links.swap(0, out_sent)
    down_total = down_product(CORE, out_sent, down_received)
    input_total = input_traded.grad(after(select, down_total), normed_pieces)
    input_chain = Chain(links, [input_total], projection_sums, (0, "core"), True)
    token = gate_chain.advance(input_chain.sent)
    token = up_chain.advance(token)
    down_total = after(down_total, token)
    down_chain = Chain(links, [down_total], [(bit, 0) for bit in (0, *range(2, top))])
    input_grad = after(input_grad, down_chain.sent)
    normed_a_grad = gate_part + product("rt,dr->td", input_grad, w_input)
    token_norm_grad, gain_a_grad = norm_back_a(normed_a_grad)
    token_grad = middle_grad + token_norm_grad
    small = jnp.concatenate([gain_a_grad, gain_b_grad, sums])
    token = input_chain.advance(token_grad)
    gate_proj_total = after(gate_proj_total, token)
    gate_proj = Chain(links, [gate_proj_total], projection_sums, (0, "core"), True, small)
    out_token = after(select, gate_proj.sent)
    out_total = grad_product(out_token, out_pieces, rows_total // 8, X, out_received)
    out_chain = Chain(links, [out_total], up_sums)
    token = input_chain.advance(out_total)
    token = gate_chain.advance(token)
    token = down_chain.advance(token)
    token = up_chain.advance(token)
    chains = [input_chain, gate_proj, out_chain, gate_chain, up_chain, down_chain]
    while any(chain.sums or chain.collects for chain in chains):
        for chain in chains:
            if chain.sums or chain.collects:
                token = chain.advance(token)
    param_sums = channel_sums(lane_sums, channels, decay_logits)
    param_sums = param_sums + links.swap("core", after(param_sums, up_sent))
    totals = gate_proj.rider
    gain_size = width // (lax.axis_size("seq") * lax.axis_size("fsdp"))
    gain_start = (place * lax.axis_size("fsdp") + core) * gain_size
    return (
        output,
        token_grad,
        gate_proj.total(),
        input_chain.total(),
        out_chain.total(),
        gate_chain.total(),
        up_chain.total(),
        down_chain.total(),
        lax.dynamic_slice_in_dim(totals, gain_start, gain_size, 0),
        lax.dynamic_slice_in_dim(totals, width + gain_start, gain_size, 0),
        param_sums[:TAPS],
        param_sums[TAPS],
        param_sums[TAPS + 1 : TAPS + 3],
        param_sums[TAPS + 3 : TAPS + 5],
        param_sums[TAPS + 5],
        jnp.sqrt(totals[2 * width :] / entry_total),
    )


def solution(mesh):
    in_specs = (
        P(("seq", "fsdp"), None),
        P(("seq", "fsdp"), None),
        P("fsdp", None),
        P("fsdp", None),
        P("fsdp", None),
        P("fsdp", None),
        P("fsdp", None),
        P("fsdp", None),
        P("fsdp"),
        P("fsdp"),
        P(None, "seq"),
        P("seq"),
        P(None, "seq"),
        P(None, "seq"),
        P("seq"),
        P("fsdp", None),
        P("fsdp", None),
    )
    out_specs = (
        P(("seq", "fsdp"), None),
        P(("seq", "fsdp"), None),
        P(("seq", "fsdp"), None),
        P(("seq", "fsdp"), None),
        P(("seq", "fsdp"), None),
        P(("seq", "fsdp"), None),
        P(("seq", "fsdp"), None),
        P(("seq", "fsdp"), None),
        P(("seq", "fsdp")),
        P(("seq", "fsdp")),
        P(None, "seq"),
        P("seq"),
        P(None, "seq"),
        P(None, "seq"),
        P("seq"),
        P(),
    )
    return jax.shard_map(
        per_device, mesh=mesh, in_specs=in_specs, out_specs=out_specs, check_vma=False
    )
```

```python
import math
from functools import partial

import jax
import jax.numpy as jnp
import numpy as np
from jax import lax
from jax.experimental import pallas as pl
from jax.experimental.pallas import tpu as pltpu
from jax.sharding import PartitionSpec as P

NORM_EPS = 1e-06
RATE_SCALE = 8.0
LANES = 640
SUB = 8
TAPS = 4
UNROLL = 4
VMEM_LIMIT = 60 << 20


def gelu_tanh(values):
    return jax.nn.gelu(values, approximate=True)


def rms_norm(values, norm_gain):
    return (
        values * lax.rsqrt(jnp.mean(values * values, axis=-1, keepdims=True) + NORM_EPS) * norm_gain
    )


def gated_state(state_in, gate_pre):
    return state_in * gelu_tanh(gate_pre)


def mixing(first_pre, second_pre):
    return gelu_tanh(first_pre) * second_pre


def one_minus_exp_neg(u):
    series = jnp.ones_like(u)
    for k in range(9, 1, -1):
        series = 1.0 - u * (1.0 / k) * series
    return jnp.where(u < 0.5, u * series, 1.0 - jnp.exp(-u))


def logistic(values):
    return 1.0 / (1.0 + jnp.exp(-values))


def earlier_chunk(values, channels):
    rolled = pltpu.roll(values, 1, 0)
    wrapped = pltpu.roll(rolled, channels, 1) if channels < LANES else rolled
    sub = lax.broadcasted_iota(jnp.int32, values.shape, 0)
    lane = lax.broadcasted_iota(jnp.int32, values.shape, 1)
    shifted = jnp.where(sub == 0, wrapped, rolled)
    return jnp.where((sub == 0) & (lane < channels), 0.0, shifted)


def later_chunk(values, channels):
    rolled = pltpu.roll(values, SUB - 1, 0)
    wrapped = pltpu.roll(rolled, LANES - channels, 1) if channels < LANES else rolled
    sub = lax.broadcasted_iota(jnp.int32, values.shape, 0)
    lane = lax.broadcasted_iota(jnp.int32, values.shape, 1)
    shifted = jnp.where(sub == SUB - 1, wrapped, rolled)
    return jnp.where((sub == SUB - 1) & (lane >= LANES - channels), 0.0, shifted)


def place_rows(slot_ref, source, group, rows):
    here = slot_ref[source] - group * rows
    row = lax.broadcasted_iota(jnp.int32, (rows, here.shape[-1]), 0)
    return jnp.where(row == here, 1.0, 0.0).astype(jnp.bfloat16)


def into_order(data_ref, column_ref, wide_ref, ordered_ref, first_row):
    blocks, per_block, tokens = column_ref.shape
    channels = data_ref.shape[1]
    rows = wide_ref.shape[1]
    for group in range(LANES // channels):

        def one_tile(tile, carry, group=group):
            start = group * rows + tile * tokens
            place = (lax.broadcasted_iota(jnp.int32, (tokens, tokens), 1) + start).astype(jnp.float32)

            def one_block(block, total):
                columns = column_ref[block].T
                for k in range(per_block):
                    here = jnp.where(columns[:, k : k + 1] == place, 1.0, 0.0).astype(jnp.bfloat16)
                    total = total + jnp.dot(
                        data_ref[block * per_block + k], here, preferred_element_type=jnp.float32
                    )
                return total

            total = jnp.zeros((channels, tokens), jnp.float32)
            total = lax.fori_loop(0, blocks, one_block, total)
            at = pl.ds(pl.multiple_of(tile * tokens, tokens), tokens)
            wide_ref[group * channels : (group + 1) * channels, at] = total
            return carry

        lax.fori_loop(0, rows // tokens, one_tile, 0)
    for start in range(0, rows, 128):
        ordered_ref[first_row + start : first_row + start + 128, :] = wide_ref[
            :, start : start + 128
        ].T


def out_of_order(ordered_ref, slot_ref, narrow_ref, data_ref):
    sources, channels, tokens = data_ref.shape
    groups, _, rows = narrow_ref.shape
    for start in range(0, rows, 128):
        wide = ordered_ref[start : start + 128, :].T
        for group in range(groups):
            narrow_ref[group, :, start : start + 128] = wide[
                group * channels : (group + 1) * channels, :
            ].astype(jnp.bfloat16)

    def one_source(source, carry):
        total = jnp.zeros((channels, tokens), jnp.float32)
        for group in range(groups):
            total = total + jnp.dot(
                narrow_ref[group],
                place_rows(slot_ref, source, group, rows),
                preferred_element_type=jnp.float32,
            )
        data_ref[source] = total.astype(jnp.bfloat16)
        return carry

    lax.fori_loop(0, sources, one_source, 0)


def forward_kernel(
    data_ref, slot_ref, column_ref, offset_ref, params_ref,
    states_ref, inputs_ref, filtered_ref, decay_ref, hidden_ref,
    wide_ref, reach_ref, narrow_ref,
):
    channels = data_ref.shape[1]
    rows = hidden_ref.shape[0]
    pad = (TAPS - 1) * SUB
    into_order(data_ref, column_ref, wide_ref, inputs_ref, pad)
    for tap in range(TAPS - 1):
        inputs_ref[tap * SUB : (tap + 1) * SUB, :] = earlier_chunk(
            inputs_ref[rows + tap * SUB : rows + (tap + 1) * SUB, :], channels
        )
    param = [params_ref[k : k + 1, :] for k in range(TAPS + 6)]
    block = UNROLL * SUB

    def local_steps(step, carry):
        state, reach = carry
        start = pl.multiple_of(step * block, block)
        offset = offset_ref[pl.ds(start, block), :]
        filtered = param[TAPS] + param[0] * inputs_ref[pl.ds(start + pad, block), :]
        for tap in range(1, TAPS):
            delayed = inputs_ref[pl.ds(start + pad - tap * SUB, block), :]
            filtered = filtered + param[tap] * jnp.where(offset >= tap, delayed, 0.0)
        recur_gate = logistic(param[TAPS + 1] * filtered + param[TAPS + 3])
        input_gate = logistic(param[TAPS + 2] * filtered + param[TAPS + 4])
        rate = param[TAPS + 5] * recur_gate
        decay = jnp.where(offset > 0, jnp.exp(-rate), 0.0)
        drive = jnp.sqrt(one_minus_exp_neg(2.0 * rate)) * input_gate * filtered
        filtered_ref[pl.ds(start, block), :] = filtered
        decay_ref[pl.ds(start, block), :] = decay
        for k in range(UNROLL):
            now = decay[k * SUB : (k + 1) * SUB, :]
            state = now * state + drive[k * SUB : (k + 1) * SUB, :]
            reach = now * reach
            hidden_ref[pl.ds(start + k * SUB, SUB), :] = state
            reach_ref[pl.ds(start + k * SUB, SUB), :] = reach
        return state, reach

    zeros = jnp.zeros((SUB, LANES), jnp.float32)
    last, reach = lax.fori_loop(0, rows // block, local_steps, (zeros, zeros + 1.0))
    chunks = SUB * (LANES // channels)
    entry = lax.fori_loop(
        0, chunks - 1, lambda _, entry: earlier_chunk(last + reach * entry, channels), zeros
    )
    entries = jnp.concatenate([entry] * UNROLL, axis=0)

    def carry_over(step, carry):
        start = pl.multiple_of(step * block, block)
        hidden_ref[pl.ds(start, block), :] += reach_ref[pl.ds(start, block), :] * entries
        return carry

    lax.fori_loop(0, rows // block, carry_over, 0)
    out_of_order(hidden_ref, slot_ref, narrow_ref, states_ref)


def backward_kernel(
    data_ref, slot_ref, column_ref, offset_ref, params_ref, inputs_ref, filtered_ref, decay_ref, hidden_ref,
    grads_ref, sums_ref,
    wide_ref, back_ref, reach_ref, narrow_ref, filtered_grad_ref, later_offset_ref,
):
    channels = data_ref.shape[1]
    rows = hidden_ref.shape[0]
    pad = (TAPS - 1) * SUB
    into_order(data_ref, column_ref, wide_ref, back_ref, 0)
    param = [params_ref[k : k + 1, :] for k in range(TAPS + 6)]
    block = UNROLL * SUB
    count = rows // block

    def local_steps(step, carry):
        passed, reach = carry
        start = pl.multiple_of((count - 1 - step) * block, block)
        decay = decay_ref[pl.ds(start, block), :]
        given = back_ref[pl.ds(start, block), :]
        for k in range(UNROLL - 1, -1, -1):
            back = given[k * SUB : (k + 1) * SUB, :] + passed
            back_ref[pl.ds(start + k * SUB, SUB), :] = back
            reach_ref[pl.ds(start + k * SUB, SUB), :] = reach
            now = decay[k * SUB : (k + 1) * SUB, :]
            passed = now * back
            reach = now * reach
        return passed, reach

    zeros = jnp.zeros((SUB, LANES), jnp.float32)
    first, reach = lax.fori_loop(0, count, local_steps, (zeros, zeros + 1.0))
    chunks = SUB * (LANES // channels)
    entry = lax.fori_loop(
        0, chunks - 1, lambda _, entry: later_chunk(first + reach * entry, channels), zeros
    )
    entries = jnp.concatenate([entry] * UNROLL, axis=0)
    sums_ref[...] = jnp.zeros_like(sums_ref)
    before_first = earlier_chunk(hidden_ref[rows - SUB : rows, :], channels)

    def add_up(index, values):
        total = values[:SUB, :]
        for k in range(1, UNROLL):
            total = total + values[k * SUB : (k + 1) * SUB, :]
        sums_ref[index] += total

    def through_gates(step, before):
        start = pl.multiple_of(step * block, block)
        offset = offset_ref[pl.ds(start, block), :]
        filtered = filtered_ref[pl.ds(start, block), :]
        hidden = hidden_ref[pl.ds(start, block), :]
        earlier = jnp.concatenate([before, hidden[: block - SUB, :]], axis=0)
        back = back_ref[pl.ds(start, block), :] + reach_ref[pl.ds(start, block), :] * entries
        recur_gate = logistic(param[TAPS + 1] * filtered + param[TAPS + 3])
        input_gate = logistic(param[TAPS + 2] * filtered + param[TAPS + 4])
        rate = param[TAPS + 5] * recur_gate
        decay = decay_ref[pl.ds(start, block), :]
        squared = one_minus_exp_neg(2.0 * rate)
        scale_inv = lax.rsqrt(jnp.maximum(squared, 1e-37))
        scale = squared * scale_inv
        scale_grad = back * input_gate * filtered
        input_gate_grad = back * scale * filtered
        rate_grad = scale_grad * (1.0 - squared) * scale_inv - decay * back * earlier
        recur_pre_grad = rate_grad * param[TAPS + 5] * recur_gate * (1.0 - recur_gate)
        input_pre_grad = input_gate_grad * input_gate * (1.0 - input_gate)
        filtered_grad = (
            back * scale * input_gate
            + recur_pre_grad * param[TAPS + 1]
            + input_pre_grad * param[TAPS + 2]
        )
        filtered_grad_ref[pl.ds(start, block), :] = filtered_grad
        add_up(0, filtered_grad * inputs_ref[pl.ds(start + pad, block), :])
        for tap in range(1, TAPS):
            delayed = inputs_ref[pl.ds(start + pad - tap * SUB, block), :]
            add_up(tap, filtered_grad * jnp.where(offset >= tap, delayed, 0.0))
        add_up(TAPS, filtered_grad)
        add_up(TAPS + 1, recur_pre_grad * filtered)
        add_up(TAPS + 2, input_pre_grad * filtered)
        add_up(TAPS + 3, recur_pre_grad)
        add_up(TAPS + 4, input_pre_grad)
        add_up(TAPS + 5, rate_grad * recur_gate)
        return hidden[block - SUB :, :]

    lax.fori_loop(0, count, through_gates, before_first)
    for tap in range(TAPS - 1):
        rows_here = slice(tap * SUB, (tap + 1) * SUB)
        filtered_grad_ref[rows + tap * SUB : rows + (tap + 1) * SUB, :] = later_chunk(
            filtered_grad_ref[rows_here, :], channels
        )
        later_offset_ref[block + tap * SUB : block + (tap + 1) * SUB, :] = later_chunk(
            offset_ref[rows_here, :], channels
        )
    later_offset_ref[:block, :] = offset_ref[rows - block :, :]

    def through_taps(start, offsets_ref, offset_start):
        total = param[0] * filtered_grad_ref[pl.ds(start, block), :]
        for tap in range(1, TAPS):
            later = filtered_grad_ref[pl.ds(start + tap * SUB, block), :]
            offset = offsets_ref[pl.ds(offset_start + tap * SUB, block), :]
            total = total + param[tap] * jnp.where(offset >= tap, later, 0.0)
        back_ref[pl.ds(start, block), :] = total

    def inner_taps(step, carry):
        start = pl.multiple_of(step * block, block)
        through_taps(start, offset_ref, start)
        return carry

    lax.fori_loop(0, count - 1, inner_taps, 0)
    through_taps(rows - block, later_offset_ref, 0)
    out_of_order(back_ref, slot_ref, narrow_ref, grads_ref)


def shapes_of(data):
    sources, channels, tokens = data.shape
    rows = sources * tokens * channels // LANES
    return sources, channels, tokens, rows


def slot_columns(slot):
    sources, _, tokens = slot.shape
    per_block = math.gcd(sources, 16)
    return slot.reshape(sources // per_block, per_block, tokens).astype(jnp.float32)


def recurrence_forward(data, slot, offset, params):
    sources, channels, tokens, rows = shapes_of(data)
    whole = jax.ShapeDtypeStruct((rows, LANES), jnp.float32)
    padded = jax.ShapeDtypeStruct((rows + (TAPS - 1) * SUB, LANES), jnp.float32)
    count = sources * tokens
    return pl.pallas_call(
        forward_kernel,
        out_shape=(jax.ShapeDtypeStruct(data.shape, jnp.bfloat16), padded, whole, whole, whole),
        scratch_shapes=[
            pltpu.VMEM((LANES, rows), jnp.float32),
            pltpu.VMEM((rows, LANES), jnp.float32),
            pltpu.VMEM((LANES // channels, channels, rows), jnp.bfloat16),
        ],
        compiler_params=pltpu.CompilerParams(vmem_limit_bytes=VMEM_LIMIT),
        cost_estimate=pl.CostEstimate(
            flops=0, bytes_accessed=0, transcendentals=0
        ),
        name="recurrence_forward",
    )(data, slot, slot_columns(slot), offset, params)


def recurrence_backward(data, slot, offset, params, inputs, filtered, decay, hidden):
    sources, channels, tokens, rows = shapes_of(data)
    count = sources * tokens
    return pl.pallas_call(
        backward_kernel,
        out_shape=(
            jax.ShapeDtypeStruct(data.shape, jnp.bfloat16),
            jax.ShapeDtypeStruct((TAPS + 6, SUB, LANES), jnp.float32),
        ),
        scratch_shapes=[
            pltpu.VMEM((LANES, rows), jnp.float32),
            pltpu.VMEM((rows, LANES), jnp.float32),
            pltpu.VMEM((rows, LANES), jnp.float32),
            pltpu.VMEM((LANES // channels, channels, rows), jnp.bfloat16),
            pltpu.VMEM((rows + (TAPS - 1) * SUB, LANES), jnp.float32),
            pltpu.VMEM((UNROLL * SUB + (TAPS - 1) * SUB, LANES), jnp.float32),
        ],
        compiler_params=pltpu.CompilerParams(vmem_limit_bytes=VMEM_LIMIT),
        cost_estimate=pl.CostEstimate(
            flops=0, bytes_accessed=0, transcendentals=0
        ),
        name="recurrence_backward",
    )(data, slot, slot_columns(slot), offset, params, inputs, filtered, decay, hidden)


def arrangement(lengths, permutation, sources, channels):
    total = permutation.shape[0]
    groups = LANES // channels
    rows = total // groups
    steps = rows // SUB
    chunk = permutation // steps
    slot = (chunk // SUB) * rows + (permutation % steps) * SUB + chunk % SUB
    seq_ends = jnp.cumsum(lengths)
    seq_starts = seq_ends - lengths
    row, lane = np.arange(rows), np.arange(LANES)
    of_row = jnp.asarray((row % SUB) * steps + row // SUB, jnp.int32)
    of_lane = jnp.asarray((lane // channels) * (SUB * steps), jnp.int32)
    position = of_row[:, None] + of_lane[None, :]
    seg_first = jnp.zeros_like(position)
    for k in range(lengths.shape[0]):
        start = seq_starts[k]
        seg_first = jnp.where(position >= start, start, seg_first)
    offset = jnp.minimum(position - seg_first, TAPS - 1).astype(jnp.float32)
    return slot.reshape(sources, 1, total // sources), offset


def lane_params(conv_weight, conv_bias, gate_weight, gate_bias, decay_logits):
    stacked = jnp.concatenate(
        [
            conv_weight,
            conv_bias[None],
            gate_weight,
            gate_bias,
            RATE_SCALE * jax.nn.softplus(-decay_logits)[None],
        ]
    )
    return jnp.tile(stacked, (1, LANES // stacked.shape[1]))


def channel_sums(sums, channels, decay_logits):
    sums = jnp.sum(sums, axis=1).reshape(TAPS + 6, LANES // channels, channels).sum(axis=1)
    logit = -RATE_SCALE * jax.nn.sigmoid(-decay_logits)[None] * sums[TAPS + 5 :]
    return jnp.concatenate([sums[: TAPS + 5], logit])


def swap_core(values):
    return lax.ppermute(values, "fsdp", [(0, 1), (1, 0)])


def swap_bit(values, bit):
    count = lax.axis_size("seq")
    return lax.ppermute(values, "seq", [(i, i ^ (1 << bit)) for i in range(count)])


def half(values, index, axis):
    size = values.shape[axis] // 2
    return lax.dynamic_slice_in_dim(values, index * size, size, axis)


def reorder_blocks(values, low_bit, high_bit, axis):
    width = high_bit - low_bit
    size = values.shape[axis] >> width
    pieces = []
    for place in range(1 << width):
        natural = sum(((place >> (width - 1 - k)) & 1) << k for k in range(width))
        pieces.append(lax.slice_in_dim(values, natural * size, (natural + 1) * size, axis=axis))
    return jnp.concatenate(pieces, axis=axis)


def trade_channels(values):
    return lax.all_to_all(values, "seq", split_axis=0, concat_axis=0, tiled=True)


def after(values, *earlier):
    return lax.optimization_barrier((values,) + earlier)[0]


def product(subscripts, left, right):
    return jnp.einsum(subscripts, left, right, preferred_element_type=jnp.float32)


class Links:
    def __init__(self, place, core):
        count = lax.axis_size("seq").bit_length() - 1
        self.core = core
        self.bits = [(place >> bit) & 1 for bit in range(count)]

    def own(self, link):
        return self.core if link == "core" else self.bits[link]

    def swap(self, link, values, *earlier):
        if earlier:
            values = after(values, *earlier)
        return swap_core(values) if link == "core" else swap_bit(values, link)


class Chain:
    def __init__(self, links, terms, sums, collects=(), turn=False, rider=None):
        self.links, self.terms, self.rider = links, list(terms), rider
        self.sums, self.collects, self.turn = list(sums), list(collects), turn
        self.send()

    def total(self):
        return sum(term.astype(jnp.float32) for term in self.terms)

    def send(self):
        if self.sums:
            self.link, self.axis = self.sums[0]
        elif self.collects:
            total = self.total()
            self.terms = [total.T if self.turn else total]
            self.turn = False
            self.link, self.axis = self.collects[0], 0
        else:
            return
        own_bit = self.links.own(self.link)
        sent = sum(half(term, 1 - own_bit, self.axis).astype(jnp.float32) for term in self.terms)
        self.sent = sent.astype(jnp.bfloat16)
        self.other = self.links.swap(self.link, self.sent)
        self.terms = [half(term, own_bit, self.axis) for term in self.terms]
        if self.rider is not None:
            self.rider_other = self.links.swap(self.link, self.rider)

    def advance(self, token):
        other = after(self.other, token)
        if self.rider is not None:
            self.rider = self.rider + after(self.rider_other, token)
        if self.sums:
            self.terms.append(other)
            self.sums.pop(0)
        else:
            own, other = self.terms[0], other.astype(jnp.float32)
            first = self.links.own(self.link) == 0
            low, high = jnp.where(first, own, other), jnp.where(first, other, own)
            self.terms = [jnp.concatenate([low, high], axis=1)]
            self.collects.pop(0)
        if not self.sums and not self.collects:
            return token
        self.send()
        return self.sent


def both_cores(values, *earlier):
    return lax.all_gather(after(values, *earlier) if earlier else values, "fsdp")


def pick(values, *index):
    for place in index:
        values = lax.dynamic_index_in_dim(values, place, 0, keepdims=False)
    return values


def largest_tile(size, most, step):
    return max(tile for tile in range(step, most + 1, step) if size % tile == 0)


def grad_kernel(count, turned, select_ref, *refs):
    per_piece = turned or 1
    lefts = [ref[...] for ref in refs[: count * per_piece]]
    rights = [ref[...] for ref in refs[count * per_piece : count * (per_piece + 1)]]
    rights = jnp.concatenate(rights, axis=0)
    if turned:
        if per_piece > 1:
            lefts = [
                jnp.concatenate(lefts[k * per_piece : (k + 1) * per_piece], axis=1)
                for k in range(count)
            ]
        total = lax.dot_general(
            jnp.concatenate(lefts, axis=0),
            rights,
            (((0,), (0,)), ((), ())),
            preferred_element_type=jnp.float32,
        )
    else:
        total = jnp.dot(
            jnp.concatenate(lefts, axis=1), rights, preferred_element_type=jnp.float32
        )
    for ref in refs[count * (per_piece + 1) : -1]:
        total = total + ref[...].astype(jnp.float32)
    refs[-1][...] = total.astype(jnp.bfloat16)


(CORE, OTHER_CORE), (X, OTHER_X), (Y, OTHER_Y), (LOW, OTHER_LOW), (TOP, OTHER_TOP) = (
    (("scalar", 2 * k), ("scalar", 2 * k + 1)) for k in range(5)
)


def grad_product(select, pieces, rows, row_half=None, added=None, columns=None, counted=False):
    cols = pieces[0][2].shape[-1]
    tile_rows = largest_tile(rows, 512, 16) if columns is None else rows // columns[0]
    tile_cols = largest_tile(cols, 1024 if columns is None else 1536, 256)

    def entry(index, select_ref):
        return select_ref[index[1]] if isinstance(index, tuple) else index

    def left_spec(left, lead):
        def place(m, n, select_ref):
            start = 0 if row_half is None else entry(row_half, select_ref) * (rows // tile_rows)
            return tuple(entry(i, select_ref) for i in lead) + (start + m, 0)

        return pl.BlockSpec((None,) * len(lead) + (tile_rows, left.shape[-1]), place)

    def column_spec(left, lead, which):
        def place(m, n, select_ref):
            block = columns[2](m, partial(entry, select_ref=select_ref))[which]
            return tuple(entry(i, select_ref) for i in lead) + (0, block)

        return pl.BlockSpec((None,) * len(lead) + (left.shape[-2], columns[1]), place)

    def right_spec(right, lead):
        def place(m, n, select_ref):
            return tuple(entry(i, select_ref) for i in lead) + (0, n)

        return pl.BlockSpec((None,) * len(lead) + (right.shape[-2], tile_cols), place)

    out_spec = pl.BlockSpec((tile_rows, tile_cols), lambda m, n, select_ref: (m, n))
    turned = 0 if columns is None else tile_rows // columns[1]
    if turned:
        in_specs = [column_spec(p[0], p[1], which) for p in pieces for which in range(turned)]
        operands = [p[0] for p in pieces for _ in range(turned)]
    else:
        in_specs = [left_spec(left, lead) for left, lead, _, _ in pieces]
        operands = [left for left, _, _, _ in pieces]
    in_specs += [right_spec(right, lead) for _, _, right, lead in pieces]
    operands += [right for _, _, right, _ in pieces]
    if added is not None:
        in_specs.append(out_spec)
        operands.append(added)
    return pl.pallas_call(
        partial(grad_kernel, len(pieces), turned),
        out_shape=jax.ShapeDtypeStruct((rows, cols), jnp.bfloat16),
        grid_spec=pltpu.PrefetchScalarGridSpec(
            num_scalar_prefetch=1,
            grid=(rows // tile_rows, cols // tile_cols),
            in_specs=in_specs,
            out_specs=out_spec,
        ),
        compiler_params=pltpu.CompilerParams(vmem_limit_bytes=VMEM_LIMIT),
        cost_estimate=pl.CostEstimate(
            flops=counted * 2 * rows * cols * sum(p[2].shape[-2] for p in pieces),
            bytes_accessed=counted * 2 * rows * cols,
            transcendentals=0,
        ),
        name="weight_grad",
    )(select, *operands)


GELU_SCALE = 0.7978845608028654
GELU_CUBE = 0.044715
HIDDEN_TILE = 512


def mlp_kernel(
    bits_ref, normed_ref, down_grad_ref, gate_ref, up_ref, down_ref,
    branch_ref, normed_grad_ref, mixed_ref, sent_gate_ref, sent_up_ref, kept_gate_ref, kept_up_ref,
):
    step = pl.program_id(0)
    by_columns = (((1,), (1,)), ((), ()))
    normed = normed_ref[...]
    first = jnp.dot(normed, gate_ref[...], preferred_element_type=jnp.float32)
    second = jnp.dot(normed, up_ref[...], preferred_element_type=jnp.float32)
    mixed_grad = lax.dot_general(
        down_grad_ref[...], down_ref[...], by_columns, preferred_element_type=jnp.float32
    )
    square = first * first
    bend = jnp.tanh(GELU_SCALE * first * (1.0 + GELU_CUBE * square))
    rise = 0.5 + 0.5 * bend
    gelu = first * rise
    slope = rise + 0.5 * GELU_SCALE * first * (1.0 - bend * bend) * (
        1.0 + 3.0 * GELU_CUBE * square
    )
    mixed = gelu * second
    first_low = (mixed_grad * slope * second).astype(jnp.bfloat16)
    second_low = (mixed_grad * gelu).astype(jnp.bfloat16)
    mixed_ref[...] = mixed.T.astype(jnp.bfloat16)

    side = (step // (pl.num_programs(0) // 4)) % 2
    for which, low, sent_ref, kept_ref in (
        (0, first_low, sent_gate_ref, kept_gate_ref),
        (1, second_low, sent_up_ref, kept_up_ref),
    ):

        @pl.when(side != bits_ref[which])
        def _(low=low, sent_ref=sent_ref):
            sent_ref[...] = low

        @pl.when(side == bits_ref[which])
        def _(low=low, kept_ref=kept_ref):
            kept_ref[...] = low

    @pl.when(step == 0)
    def _():
        branch_ref[...] = jnp.zeros_like(branch_ref)
        normed_grad_ref[...] = jnp.zeros_like(normed_grad_ref)

    branch_ref[...] += jnp.dot(
        mixed.astype(jnp.bfloat16), down_ref[...], preferred_element_type=jnp.float32
    )
    normed_grad_ref[...] += lax.dot_general(
        first_low, gate_ref[...], by_columns, preferred_element_type=jnp.float32
    ) + lax.dot_general(second_low, up_ref[...], by_columns, preferred_element_type=jnp.float32)


def mlp_both_ways(bits, normed, down_grad, w_gate, w_up, w_down):
    count, width = normed.shape
    hidden = w_gate.shape[1]
    steps = hidden // HIDDEN_TILE
    tiles = steps // 4

    whole = pl.BlockSpec((count, width), lambda t, bits_ref: (0, 0))
    column = pl.BlockSpec((width, HIDDEN_TILE), lambda t, bits_ref: (0, t))
    row = pl.BlockSpec((HIDDEN_TILE, width), lambda t, bits_ref: (t, 0))
    turned = pl.BlockSpec((HIDDEN_TILE, count), lambda t, bits_ref: (t, 0))

    def traded(which, kept):
        def place(t, bits_ref):
            wanted = bits_ref[which] if kept else 1 - bits_ref[which]
            side = (t // tiles) % 2
            resting = jnp.where(wanted == 0, tiles - 1, 0)
            return (t // (2 * tiles), 0, jnp.where(side == wanted, t % tiles, resting))

        return pl.BlockSpec((None, count, HIDDEN_TILE), place)

    summed = jax.ShapeDtypeStruct((count, width), jnp.float32)
    return pl.pallas_call(
        mlp_kernel,
        out_shape=(summed, summed, jax.ShapeDtypeStruct((hidden, count), jnp.bfloat16))
        + (jax.ShapeDtypeStruct((2, count, hidden // 4), jnp.bfloat16),) * 4,
        grid_spec=pltpu.PrefetchScalarGridSpec(
            num_scalar_prefetch=1,
            grid=(steps,),
            in_specs=[whole, whole, column, column, row],
            out_specs=[whole, whole, turned]
            + [traded(which, kept) for kept in (False, True) for which in (0, 1)],
        ),
        compiler_params=pltpu.CompilerParams(vmem_limit_bytes=VMEM_LIMIT),
        cost_estimate=pl.CostEstimate(flops=0, bytes_accessed=0, transcendentals=0),
        name="mlp_both_ways",
    )(jnp.stack(bits).astype(jnp.int32), normed, down_grad, w_gate, w_up, w_down)


MIDDLE_TILE = 512


def middle_kernel(
    core_ref, normed_grad_ref, middle_ref, cotangent_ref, gain_ref, output_ref, own_ref, other_ref,
    state_ref, pre_ref,
    middle_grad_ref, out_grad_ref, gain_grad_ref, state_grad_ref, gate_grad_ref, back_ref,
):
    by_columns = (((1,), (1,)), ((), ()))

    @pl.when(pl.program_id(0) == 0)
    def _():
        middle = middle_ref[...]
        normed_grad = normed_grad_ref[...]
        inverse = lax.rsqrt(jnp.mean(middle * middle, axis=1, keepdims=True) + NORM_EPS)
        scaled = normed_grad * gain_ref[...]
        lean = jnp.mean(scaled * middle, axis=1, keepdims=True)
        total = cotangent_ref[...] + inverse * scaled - middle * (inverse * inverse * inverse * lean)
        middle_grad_ref[...] = total
        out_grad_ref[...] = total.astype(jnp.bfloat16)
        gain_grad_ref[...] = jnp.sum(normed_grad * middle * inverse, axis=0, keepdims=True)
        back_ref[...] = jnp.zeros_like(back_ref)

    grad = lax.dot_general(
        output_ref[...], out_grad_ref[...], by_columns, preferred_element_type=jnp.float32
    )
    pre = pre_ref[...]
    square = pre * pre
    bend = jnp.tanh(GELU_SCALE * pre * (1.0 + GELU_CUBE * square))
    rise = 0.5 + 0.5 * bend
    slope = rise + 0.5 * GELU_SCALE * pre * (1.0 - bend * bend) * (1.0 + 3.0 * GELU_CUBE * square)
    state_grad_ref[...] = (grad * pre * rise).astype(jnp.bfloat16)
    gate_grad = (grad * state_ref[...].astype(jnp.float32) * slope).astype(jnp.bfloat16)
    gate_grad_ref[...] = gate_grad
    width = own_ref.shape[0]
    for ref, place in ((own_ref, core_ref[0]), (other_ref, 1 - core_ref[0])):
        columns = pl.ds(pl.multiple_of(place * width, width), width)
        back_ref[:, columns] += lax.dot_general(
            gate_grad, ref[...], (((0,), (1,)), ((), ())), preferred_element_type=jnp.float32
        )


def middle_backward(core, normed_grad, middle, cotangent, gain, w_output, own, other, states, pre):
    count, width = middle.shape
    channels = w_output.shape[0]
    whole = pl.BlockSpec((count, width), lambda t, core_ref: (0, 0))
    line = pl.BlockSpec((1, width), lambda t, core_ref: (0, 0))
    row = pl.BlockSpec((MIDDLE_TILE, width), lambda t, core_ref: (t, 0))
    column = pl.BlockSpec((width // 2, MIDDLE_TILE), lambda t, core_ref: (0, t))
    turned = pl.BlockSpec((MIDDLE_TILE, count), lambda t, core_ref: (t, 0))
    wide = jax.ShapeDtypeStruct((count, width), jnp.float32)
    low = jax.ShapeDtypeStruct((channels, count), jnp.bfloat16)
    return pl.pallas_call(
        middle_kernel,
        out_shape=(
            wide,
            jax.ShapeDtypeStruct((count, width), jnp.bfloat16),
            jax.ShapeDtypeStruct((1, width), jnp.float32),
            low,
            low,
            wide,
        ),
        grid_spec=pltpu.PrefetchScalarGridSpec(
            num_scalar_prefetch=1,
            grid=(channels // MIDDLE_TILE,),
            in_specs=[whole, whole, whole, line, row, column, column, turned, turned],
            out_specs=[whole, whole, line, turned, turned, whole],
        ),
        compiler_params=pltpu.CompilerParams(vmem_limit_bytes=VMEM_LIMIT),
        cost_estimate=pl.CostEstimate(flops=0, bytes_accessed=0, transcendentals=0),
        name="middle_backward",
    )(core.astype(jnp.int32).reshape(1), normed_grad, middle, cotangent, gain, w_output, own, other, states, pre)


class Traded:
    def __init__(self, links, channel_grad):
        channels, count = channel_grad.shape
        self.links = links
        self.mine = channel_grad.reshape(2, 2, channels // 4, count)
        self.by_core = links.swap("core", pick(self.mine, 1 - links.core))

    def trade_x(self, token):
        core, other = self.links.core, 1 - self.links.bits[0]
        self.by_core = after(self.by_core, token)
        sent = jnp.stack([pick(self.mine, core, other), pick(self.by_core, other)])
        self.by_x = self.links.swap(0, sent)
        return sent

    def grad(self, select, normed_pieces):
        lefts = [(self.mine, (CORE, X)), (self.by_core, (X,)), (self.by_x, (0,)), (self.by_x, (1,))]
        pieces = [left + right for left, right in zip(lefts, normed_pieces)]
        return grad_product(select, pieces, self.mine.shape[2])


def per_device(
    tokens,
    cotangent,
    gate_proj,
    input_proj,
    output_proj,
    mlp_gate,
    mlp_up,
    mlp_down,
    gain_a,
    gain_b,
    conv_weight,
    conv_bias,
    gate_weight,
    gate_bias,
    decay_logits,
    lengths,
    permutation,
):
    w_input, w_output, w_mlpgate, w_mlpup, w_down = (
        lax.all_gather(input_proj, "fsdp", axis=0, tiled=True),
        lax.all_gather(output_proj, "fsdp", axis=0, tiled=True),
        lax.all_gather(mlp_gate, "fsdp", axis=0, tiled=True),
        lax.all_gather(mlp_up, "fsdp", axis=0, tiled=True),
        lax.all_gather(mlp_down, "fsdp", axis=0, tiled=True),
    )
    core = lax.axis_index("fsdp")
    place = lax.axis_index("seq")
    links = Links(place, core)
    x, y = links.bits[0], links.bits[1]
    bit_count = len(links.bits)
    top = bit_count - 1
    low = links.bits[2]
    own_bits = (core, x, y, low, links.bits[top])
    select = jnp.stack([value for bit in own_bits for value in (bit, 1 - bit)]).astype(jnp.int32)
    channels = decay_logits.shape[0]
    count, width = tokens.shape
    block_shape = (lax.axis_size("seq"), channels, count)
    gains = jnp.stack([gain_a, gain_b])
    other_gains = links.swap("core", gains)
    full_gain_a, full_gain_b = jnp.where(
        core == 0,
        jnp.concatenate([gains, other_gains], axis=1),
        jnp.concatenate([other_gains, gains], axis=1),
    )
    other_input = links.swap("core", input_proj)
    other_gate = links.swap("core", gate_proj)
    normed_a, norm_back_a = jax.vjp(rms_norm, tokens, full_gain_a.astype(jnp.float32))
    normed_a_low = normed_a.astype(jnp.bfloat16)
    down_grad = cotangent.astype(jnp.bfloat16)
    input_pre = product("td,dr->rt", half(normed_a_low, core, 1), input_proj)
    input_pre = input_pre + product("td,dr->rt", half(normed_a_low, 1 - core, 1), other_input)
    input_low = input_pre.astype(jnp.bfloat16)
    channel_in = trade_channels(input_low)
    late_lengths, late_permutation = after((lengths, permutation), input_low)
    slot, offset = arrangement(late_lengths[0], late_permutation[0], block_shape[0], channels)
    params = lane_params(conv_weight, conv_bias, gate_weight, gate_bias, decay_logits)
    normed_late = after(normed_a_low, offset, slot, params)
    gate_pre = product("td,dr->rt", half(normed_late, core, 1), gate_proj)
    gate_pre = gate_pre + product("td,dr->rt", half(normed_late, 1 - core, 1), other_gate)
    normed_order = reorder_blocks(normed_a_low, 1, bit_count, 1)
    normed_core = both_cores(normed_order, channel_in)
    channel_in, gate_pre = lax.optimization_barrier((channel_in, gate_pre))
    down_y = links.swap(1, down_grad, channel_in)
    down_top = links.swap(top, down_grad, channel_in)
    normed_x = links.swap(0, normed_order, channel_in)
    states, *kept = recurrence_forward(channel_in.reshape(block_shape), slot, offset, params)
    states = after(states, normed_x, down_y, down_top)
    state_tokens = trade_channels(states.reshape(input_pre.shape))
    normed_both = both_cores(normed_x, states)
    normed_pieces = [(normed_order, ()), (normed_core, (OTHER_CORE,))]
    normed_pieces += [(normed_x, ()), (normed_both, (OTHER_CORE,))]
    gated_low = gated_state(state_tokens.astype(jnp.float32), gate_pre).astype(jnp.bfloat16)
    branch_a = product("rt,rd->td", gated_low, w_output)
    middle = tokens + branch_a
    gain_b_wide = full_gain_b.astype(jnp.float32)
    normed_b_low = rms_norm(middle, gain_b_wide).astype(jnp.bfloat16)
    rows_total = gated_low.shape[0]
    shape = (2,) * bit_count + (2, rows_total // (2 << bit_count), count)
    rest = tuple(range(bit_count - 3, -1, -1))
    out_order = (2, 0, 1, *range(3, bit_count))
    dims = (bit_count, *(top - bit for bit in out_order), bit_count + 1, bit_count + 2)
    shape_out, dims_out = shape, dims
    fars = [links.swap(bit, normed_b_low) for bit in (0, 2)]
    down_both = links.swap(top, after(down_y, normed_b_low))
    down_pieces = [(piece, ()) for piece in (down_grad, down_y, down_top, down_both)]
    mlp_parts = mlp_both_ways((x, low), normed_b_low, down_grad, w_mlpgate, w_mlpup, w_down)
    arrived = lax.optimization_barrier((*mlp_parts, down_both, *fars))
    branch_b, normed_b_grad, mixed, sent_gate, sent_up, kept_gate, kept_up = arrived[:7]
    fars = arrived[8:]
    hidden_far = [links.swap(0, sent_gate), links.swap(2, sent_up)]
    shape = (2,) * bit_count + (2, mixed.shape[0] // (2 << bit_count), count)
    axes = [top - bit for bit in (1, top)] + [bit_count] + [top - bit for bit in (0, *range(2, top))]
    mixed_mine = mixed.reshape(shape).transpose(axes + [bit_count + 1, bit_count + 2])
    mixed_mine = mixed_mine.reshape(2, 2, 2, mixed.shape[0] // 8, count)
    mixed_y = links.swap(1, pick(mixed_mine, 1 - y))
    output = middle + branch_b
    sums = jnp.stack(
        (
            jnp.sum(tokens * tokens),
            jnp.sum(branch_a * branch_a),
            jnp.sum(middle * middle),
            jnp.sum(branch_b * branch_b),
        )
    )
    entry_total = tokens.shape[0] * tokens.shape[1] * lax.axis_size("seq") * lax.axis_size("fsdp")
    middle_grad, out_grad_low, gain_b_grad, state_low, gate_low, gate_part = middle_backward(
        core,
        normed_b_grad,
        middle,
        cotangent,
        gain_b_wide[None],
        w_output,
        gate_proj,
        other_gate,
        state_tokens,
        gate_pre,
    )
    arrived = lax.optimization_barrier((state_low, gate_low, out_grad_low, *hidden_far, mixed_y))
    state_low, gate_low, out_grad_low, *hidden_far, mixed_y = arrived
    gain_b_grad = gain_b_grad[0]
    channel_grad = trade_channels(state_low)

    normed_b_core = both_cores(normed_b_low)
    hidden_pieces = []
    for index in (0, 1):
        mine, far = (kept_gate, kept_up)[index], hidden_far[index]
        far_core = both_cores(fars[index])
        both = jnp.stack([pick(mine, 1 - core), pick(after(far, state_low), 1 - core)])
        by_core = links.swap("core", both)
        hidden_pieces.append(
            [
                (normed_b_low, (), mine, (CORE,)),
                (fars[index], (), far, (CORE,)),
                (normed_b_core, (OTHER_CORE,), by_core, (0,)),
                (far_core, (OTHER_CORE,), by_core, (1,)),
            ]
        )
    aligned = (width >> bit_count) % 128 == 0
    hidden_orders = ((1, (*range(2, bit_count),), 0), (0, (1, *range(3, bit_count)), 2))
    if not aligned:
        for pieces, (summed, between, traded_bit) in zip(hidden_pieces, hidden_orders):
            for k, (left, lead, right, right_lead) in enumerate(pieces):
                split = left.reshape(left.shape[:-1] + (2,) * bit_count + (width >> bit_count,))
                first = left.ndim - 1
                axes = [first + top - bit for bit in (summed, *between, traded_bit)]
                axes = tuple(range(first)) + tuple(axes) + (first + bit_count,)
                split = split.transpose(axes).reshape(left.shape)
                pieces[k] = (jnp.swapaxes(split, -1, -2), lead, right, right_lead)

    def hidden_product(index, half_rows, token, added=None, counted=False):
        chosen = after(select, token)
        if not aligned:
            return grad_product(chosen, hidden_pieces[index], width // 2, half_rows, added)
        summed, between, traded_bit = hidden_orders[index]

        def blocks(m, entry):
            place = entry(half_rows) << summed
            for k, bit in enumerate(reversed(between)):
                place = place + (((m >> k) & 1) << bit)
            return [place >> 1] if traded_bit == 0 else [place, place + (1 << traded_bit)]

        columns = (1 << len(between), width >> (bit_count - (traded_bit == 0)), blocks)
        return grad_product(chosen, hidden_pieces[index], width // 2, None, added, columns, counted)

    rest_bits = range(2, bit_count)
    mixed_two = jnp.stack(
        [pick(mixed_mine, y, 1 - own_bits[4]), pick(mixed_y, 1 - own_bits[4])]
    )
    gate_traded = Traded(links, gate_low)
    gated_mine = after(gated_low, state_low).reshape(shape_out).transpose(dims_out)
    gated_mine = gated_mine.reshape(2, 2, rows_total // 4, count)
    gated_core = links.swap("core", pick(gated_mine, 1 - core))
    gated_two = jnp.stack([pick(gated_mine, core, 1 - low), pick(gated_core, 1 - low)])
    gate_sent = hidden_product(0, OTHER_Y, gated_two, None, True)
    up_sent = hidden_product(1, OTHER_X, gate_sent, None, True)
    channel_grad = after(channel_grad, mixed_two, up_sent, gate_traded.by_core)
    gate_received = links.swap(1, gate_sent, channel_grad)
    up_received = links.swap(0, up_sent, channel_grad)
    mixed_far = links.swap(top, mixed_two, channel_grad)
    out_far = links.swap(2, out_grad_low, channel_grad)
    channel_grad = after(channel_grad, up_sent)

    dealt_grad, lane_sums = recurrence_backward(
        channel_grad.reshape(block_shape), slot, offset, params, *kept
    )
    dealt_grad = after(dealt_grad, out_far)
    input_grad = trade_channels(dealt_grad.reshape(state_low.shape))
    def down_product(chosen, token, added=None):
        lefts = [(mixed_mine, (Y, TOP, chosen)), (mixed_y, (TOP, chosen))]
        lefts += [(mixed_far, (k, chosen)) for k in range(2)]
        pieces = [left + right for left, right in zip(lefts, down_pieces)]
        return grad_product(after(select, token), pieces, mixed.shape[0] // 8, None, added)

    hidden_sums = [(bit, 0) for bit in rest_bits]
    projection_sums = [(bit, 1) for bit in range(1, bit_count)]
    token = after(dealt_grad, gate_received, up_received, mixed_far)
    gate_total = hidden_product(0, Y, token, gate_received)
    gated_far = links.swap(2, gated_two, gate_total)
    token = gate_traded.trade_x(gate_total)
    gate_chain = Chain(links, [gate_total], hidden_sums, (0, "core"))
    up_total = hidden_product(1, X, token, up_received)
    up_sums = [(bit, 0) for bit in (1, *range(3, bit_count))]
    up_chain = Chain(links, [up_total], up_sums, (2, "core"))
    down_sent = down_product(OTHER_CORE, up_total)
    down_received = links.swap("core", down_sent)
    input_grad = after(input_grad, down_sent)
    input_traded = Traded(links, input_grad)
    token = input_traded.trade_x(input_grad)
    out_core = both_cores(out_grad_low, dealt_grad)
    out_both = both_cores(out_far, dealt_grad)
    out_pieces = [
        (gated_mine, (CORE, LOW), out_grad_low, ()),
        (gated_core, (LOW,), out_core, (OTHER_CORE,)),
        (gated_far, (0,), out_far, ()),
        (gated_far, (1,), out_both, (OTHER_CORE,)),
    ]
    down_total = down_product(CORE, token, down_received)
    input_total = input_traded.grad(after(select, down_total), normed_pieces)
    input_chain = Chain(links, [input_total], projection_sums, (0, "core"), True)
    down_total = after(down_total, input_chain.sent)
    down_chain = Chain(links, [down_total], [(bit, 0) for bit in (0, *range(2, top))])
    token = gate_chain.advance(down_chain.sent)
    token = up_chain.advance(token)
    input_grad = after(input_grad, token)
    normed_a_grad = gate_part + product("rt,dr->td", input_grad, w_input)
    token_norm_grad, gain_a_grad = norm_back_a(normed_a_grad)
    token_grad = middle_grad + token_norm_grad
    small = jnp.concatenate([gain_a_grad, gain_b_grad, sums])
    gate_proj_total = gate_traded.grad(after(select, token_grad), normed_pieces)
    token = input_chain.advance(gate_proj_total)
    gate_proj_total = after(gate_proj_total, token)
    gate_proj = Chain(links, [gate_proj_total], projection_sums, (0, "core"), True, small)
    out_sent = grad_product(after(select, gate_proj.sent), out_pieces, rows_total // 8, OTHER_X)
    token = down_chain.advance(out_sent)
    out_received = links.swap(0, out_sent, token)
    token = input_chain.advance(token)
    token = gate_chain.advance(token)
    token = gate_proj.advance(token)
    token = up_chain.advance(token)
    token = input_chain.advance(token)
    out_total = grad_product(after(select, token), out_pieces, rows_total // 8, X, out_received)
    out_chain = Chain(links, [out_total], up_sums)
    token = gate_proj.advance(out_total)
    chains = [gate_chain, down_chain, input_chain, out_chain, gate_proj, up_chain]
    while any(chain.sums or chain.collects for chain in chains):
        for chain in chains:
            if chain.sums or chain.collects:
                token = chain.advance(token)
    param_sums = channel_sums(lane_sums, channels, decay_logits)
    param_sums = param_sums + links.swap("core", after(param_sums, up_sent))
    totals = gate_proj.rider
    gain_size = width // (lax.axis_size("seq") * lax.axis_size("fsdp"))
    gain_start = (place * lax.axis_size("fsdp") + core) * gain_size
    return (
        output,
        token_grad,
        gate_proj.total(),
        input_chain.total(),
        out_chain.total(),
        gate_chain.total(),
        up_chain.total(),
        down_chain.total(),
        lax.dynamic_slice_in_dim(totals, gain_start, gain_size, 0),
        lax.dynamic_slice_in_dim(totals, width + gain_start, gain_size, 0),
        param_sums[:TAPS],
        param_sums[TAPS],
        param_sums[TAPS + 1 : TAPS + 3],
        param_sums[TAPS + 3 : TAPS + 5],
        param_sums[TAPS + 5],
        jnp.sqrt(totals[2 * width :] / entry_total),
    )


def solution(mesh):
    in_specs = (
        P(("seq", "fsdp"), None),
        P(("seq", "fsdp"), None),
        P("fsdp", None),
        P("fsdp", None),
        P("fsdp", None),
        P("fsdp", None),
        P("fsdp", None),
        P("fsdp", None),
        P("fsdp"),
        P("fsdp"),
        P(None, "seq"),
        P("seq"),
        P(None, "seq"),
        P(None, "seq"),
        P("seq"),
        P("fsdp", None),
        P("fsdp", None),
    )
    out_specs = (
        P(("seq", "fsdp"), None),
        P(("seq", "fsdp"), None),
        P(("seq", "fsdp"), None),
        P(("seq", "fsdp"), None),
        P(("seq", "fsdp"), None),
        P(("seq", "fsdp"), None),
        P(("seq", "fsdp"), None),
        P(("seq", "fsdp"), None),
        P(("seq", "fsdp")),
        P(("seq", "fsdp")),
        P(None, "seq"),
        P("seq"),
        P(None, "seq"),
        P(None, "seq"),
        P("seq"),
        P(),
    )
    return jax.shard_map(
        per_device, mesh=mesh, in_specs=in_specs, out_specs=out_specs, check_vma=False
    )
```

```python
import math
from functools import partial

import jax
import jax.numpy as jnp
import numpy as np
from jax import lax
from jax.experimental import pallas as pl
from jax.experimental.pallas import tpu as pltpu
from jax.sharding import PartitionSpec as P

NORM_EPS = 1e-06
RATE_SCALE = 8.0
LANES = 640
SUB = 8
TAPS = 4
UNROLL = 4
VMEM_LIMIT = 60 << 20


def gelu_tanh(values):
    return jax.nn.gelu(values, approximate=True)


def rms_norm(values, norm_gain):
    return (
        values * lax.rsqrt(jnp.mean(values * values, axis=-1, keepdims=True) + NORM_EPS) * norm_gain
    )


def gated_state(state_in, gate_pre):
    return state_in * gelu_tanh(gate_pre)


def mixing(first_pre, second_pre):
    return gelu_tanh(first_pre) * second_pre


def one_minus_exp_neg(u):
    series = jnp.ones_like(u)
    for k in range(9, 1, -1):
        series = 1.0 - u * (1.0 / k) * series
    return jnp.where(u < 0.5, u * series, 1.0 - jnp.exp(-u))


def logistic(values):
    return 1.0 / (1.0 + jnp.exp(-values))


def earlier_chunk(values, channels):
    rolled = pltpu.roll(values, 1, 0)
    wrapped = pltpu.roll(rolled, channels, 1) if channels < LANES else rolled
    sub = lax.broadcasted_iota(jnp.int32, values.shape, 0)
    lane = lax.broadcasted_iota(jnp.int32, values.shape, 1)
    shifted = jnp.where(sub == 0, wrapped, rolled)
    return jnp.where((sub == 0) & (lane < channels), 0.0, shifted)


def later_chunk(values, channels):
    rolled = pltpu.roll(values, SUB - 1, 0)
    wrapped = pltpu.roll(rolled, LANES - channels, 1) if channels < LANES else rolled
    sub = lax.broadcasted_iota(jnp.int32, values.shape, 0)
    lane = lax.broadcasted_iota(jnp.int32, values.shape, 1)
    shifted = jnp.where(sub == SUB - 1, wrapped, rolled)
    return jnp.where((sub == SUB - 1) & (lane >= LANES - channels), 0.0, shifted)


def place_rows(slot_ref, source, group, rows):
    here = slot_ref[source] - group * rows
    row = lax.broadcasted_iota(jnp.int32, (rows, here.shape[-1]), 0)
    return jnp.where(row == here, 1.0, 0.0).astype(jnp.bfloat16)


def into_order(data_ref, column_ref, spread_ref, wide_ref, ordered_ref, first_row):
    blocks, per_block, tokens = column_ref.shape
    channels = data_ref.shape[1]
    rows = wide_ref.shape[1]

    def spread(block, carry):
        columns = column_ref[block].T
        for k in range(per_block):
            spread_ref[block * per_block + k] = jnp.broadcast_to(columns[:, k : k + 1], (tokens, 128))
        return carry

    lax.fori_loop(0, blocks, spread, 0)
    for group in range(LANES // channels):

        def one_tile(tile, carry, group=group):
            start = group * rows + tile * tokens
            place = (lax.broadcasted_iota(jnp.int32, (tokens, tokens), 1) + start).astype(jnp.float32)

            def one_block(block, total):
                for k in range(per_block):
                    source = block * per_block + k
                    column = jnp.concatenate([spread_ref[source]] * (tokens // 128), axis=1)
                    here = jnp.where(column == place, 1.0, 0.0).astype(jnp.bfloat16)
                    total = total + jnp.dot(
                        data_ref[source], here, preferred_element_type=jnp.float32
                    )
                return total

            total = jnp.zeros((channels, tokens), jnp.float32)
            total = lax.fori_loop(0, blocks, one_block, total)
            at = pl.ds(pl.multiple_of(tile * tokens, tokens), tokens)
            wide_ref[group * channels : (group + 1) * channels, at] = total
            return carry

        lax.fori_loop(0, rows // tokens, one_tile, 0)
    for start in range(0, rows, 128):
        ordered_ref[first_row + start : first_row + start + 128, :] = wide_ref[
            :, start : start + 128
        ].T


def out_of_order(ordered_ref, slot_ref, narrow_ref, data_ref):
    sources, channels, tokens = data_ref.shape
    groups, _, rows = narrow_ref.shape
    for start in range(0, rows, 128):
        wide = ordered_ref[start : start + 128, :].T
        for group in range(groups):
            narrow_ref[group, :, start : start + 128] = wide[
                group * channels : (group + 1) * channels, :
            ].astype(jnp.bfloat16)

    def one_source(source, carry):
        total = jnp.zeros((channels, tokens), jnp.float32)
        for group in range(groups):
            total = total + jnp.dot(
                narrow_ref[group],
                place_rows(slot_ref, source, group, rows),
                preferred_element_type=jnp.float32,
            )
        data_ref[source] = total.astype(jnp.bfloat16)
        return carry

    lax.fori_loop(0, sources, one_source, 0)


def forward_kernel(
    data_ref, slot_ref, column_ref, offset_ref, params_ref,
    states_ref, inputs_out, filtered_out, decay_out, hidden_out,
    wide_ref, reach_ref, narrow_ref, spread_ref, inputs_ref, filtered_ref, decay_ref, hidden_ref, sems,
):
    channels = data_ref.shape[1]
    rows = hidden_ref.shape[0]
    pad = (TAPS - 1) * SUB
    into_order(data_ref, column_ref, spread_ref, wide_ref, inputs_ref, pad)
    for tap in range(TAPS - 1):
        inputs_ref[tap * SUB : (tap + 1) * SUB, :] = earlier_chunk(
            inputs_ref[rows + tap * SUB : rows + (tap + 1) * SUB, :], channels
        )
    param = [params_ref[k : k + 1, :] for k in range(TAPS + 6)]
    block = UNROLL * SUB

    def local_steps(step, carry):
        state, reach = carry
        start = pl.multiple_of(step * block, block)
        offset = offset_ref[pl.ds(start, block), :]
        filtered = param[TAPS] + param[0] * inputs_ref[pl.ds(start + pad, block), :]
        for tap in range(1, TAPS):
            delayed = inputs_ref[pl.ds(start + pad - tap * SUB, block), :]
            filtered = filtered + param[tap] * jnp.where(offset >= tap, delayed, 0.0)
        recur_gate = logistic(param[TAPS + 1] * filtered + param[TAPS + 3])
        input_gate = logistic(param[TAPS + 2] * filtered + param[TAPS + 4])
        rate = param[TAPS + 5] * recur_gate
        decay = jnp.where(offset > 0, jnp.exp(-rate), 0.0)
        drive = jnp.sqrt(one_minus_exp_neg(2.0 * rate)) * input_gate * filtered
        filtered_ref[pl.ds(start, block), :] = filtered
        decay_ref[pl.ds(start, block), :] = decay
        for k in range(UNROLL):
            now = decay[k * SUB : (k + 1) * SUB, :]
            state = now * state + drive[k * SUB : (k + 1) * SUB, :]
            reach = now * reach
            hidden_ref[pl.ds(start + k * SUB, SUB), :] = state
            reach_ref[pl.ds(start + k * SUB, SUB), :] = reach
        return state, reach

    zeros = jnp.zeros((SUB, LANES), jnp.float32)
    last, reach = lax.fori_loop(0, rows // block, local_steps, (zeros, zeros + 1.0))
    chunks = SUB * (LANES // channels)
    entry = lax.fori_loop(
        0, chunks - 1, lambda _, entry: earlier_chunk(last + reach * entry, channels), zeros
    )
    entries = jnp.concatenate([entry] * UNROLL, axis=0)

    def carry_over(step, carry):
        start = pl.multiple_of(step * block, block)
        hidden_ref[pl.ds(start, block), :] += reach_ref[pl.ds(start, block), :] * entries
        return carry

    pairs = ((inputs_ref, inputs_out), (filtered_ref, filtered_out), (decay_ref, decay_out))
    copies = [pltpu.make_async_copy(a, b, sems.at[k]) for k, (a, b) in enumerate(pairs)]
    for copy in copies:
        copy.start()
    lax.fori_loop(0, rows // block, carry_over, 0)
    copies.append(pltpu.make_async_copy(hidden_ref, hidden_out, sems.at[3]))
    copies[3].start()
    out_of_order(hidden_ref, slot_ref, narrow_ref, states_ref)
    for copy in copies:
        copy.wait()


def backward_kernel(
    data_ref, slot_ref, column_ref, offset_ref, params_ref, inputs_in, filtered_in, decay_in, hidden_in,
    grads_ref, sums_ref,
    wide_ref, back_ref, reach_ref, narrow_ref, filtered_grad_ref, later_offset_ref, spread_ref,
    inputs_ref, filtered_ref, decay_ref, hidden_ref, sems,
):
    channels = data_ref.shape[1]
    rows = hidden_ref.shape[0]
    pad = (TAPS - 1) * SUB
    pairs = (
        (inputs_in, inputs_ref),
        (filtered_in, filtered_ref),
        (decay_in, decay_ref),
        (hidden_in, hidden_ref),
    )
    copies = [pltpu.make_async_copy(a, b, sems.at[k]) for k, (a, b) in enumerate(pairs)]
    for copy in copies:
        copy.start()
    into_order(data_ref, column_ref, spread_ref, wide_ref, back_ref, 0)
    for copy in copies:
        copy.wait()
    param = [params_ref[k : k + 1, :] for k in range(TAPS + 6)]
    block = UNROLL * SUB
    count = rows // block

    def local_steps(step, carry):
        passed, reach = carry
        start = pl.multiple_of((count - 1 - step) * block, block)
        decay = decay_ref[pl.ds(start, block), :]
        given = back_ref[pl.ds(start, block), :]
        for k in range(UNROLL - 1, -1, -1):
            back = given[k * SUB : (k + 1) * SUB, :] + passed
            back_ref[pl.ds(start + k * SUB, SUB), :] = back
            reach_ref[pl.ds(start + k * SUB, SUB), :] = reach
            now = decay[k * SUB : (k + 1) * SUB, :]
            passed = now * back
            reach = now * reach
        return passed, reach

    zeros = jnp.zeros((SUB, LANES), jnp.float32)
    first, reach = lax.fori_loop(0, count, local_steps, (zeros, zeros + 1.0))
    chunks = SUB * (LANES // channels)
    entry = lax.fori_loop(
        0, chunks - 1, lambda _, entry: later_chunk(first + reach * entry, channels), zeros
    )
    entries = jnp.concatenate([entry] * UNROLL, axis=0)
    sums_ref[...] = jnp.zeros_like(sums_ref)
    before_first = earlier_chunk(hidden_ref[rows - SUB : rows, :], channels)

    def add_up(index, values):
        total = values[:SUB, :]
        for k in range(1, UNROLL):
            total = total + values[k * SUB : (k + 1) * SUB, :]
        sums_ref[index] += total

    def through_gates(step, before):
        start = pl.multiple_of(step * block, block)
        offset = offset_ref[pl.ds(start, block), :]
        filtered = filtered_ref[pl.ds(start, block), :]
        hidden = hidden_ref[pl.ds(start, block), :]
        earlier = jnp.concatenate([before, hidden[: block - SUB, :]], axis=0)
        back = back_ref[pl.ds(start, block), :] + reach_ref[pl.ds(start, block), :] * entries
        recur_gate = logistic(param[TAPS + 1] * filtered + param[TAPS + 3])
        input_gate = logistic(param[TAPS + 2] * filtered + param[TAPS + 4])
        rate = param[TAPS + 5] * recur_gate
        decay = decay_ref[pl.ds(start, block), :]
        squared = one_minus_exp_neg(2.0 * rate)
        scale_inv = lax.rsqrt(jnp.maximum(squared, 1e-37))
        scale = squared * scale_inv
        scale_grad = back * input_gate * filtered
        input_gate_grad = back * scale * filtered
        rate_grad = scale_grad * (1.0 - squared) * scale_inv - decay * back * earlier
        recur_pre_grad = rate_grad * param[TAPS + 5] * recur_gate * (1.0 - recur_gate)
        input_pre_grad = input_gate_grad * input_gate * (1.0 - input_gate)
        filtered_grad = (
            back * scale * input_gate
            + recur_pre_grad * param[TAPS + 1]
            + input_pre_grad * param[TAPS + 2]
        )
        filtered_grad_ref[pl.ds(start, block), :] = filtered_grad
        add_up(0, filtered_grad * inputs_ref[pl.ds(start + pad, block), :])
        for tap in range(1, TAPS):
            delayed = inputs_ref[pl.ds(start + pad - tap * SUB, block), :]
            add_up(tap, filtered_grad * jnp.where(offset >= tap, delayed, 0.0))
        add_up(TAPS, filtered_grad)
        add_up(TAPS + 1, recur_pre_grad * filtered)
        add_up(TAPS + 2, input_pre_grad * filtered)
        add_up(TAPS + 3, recur_pre_grad)
        add_up(TAPS + 4, input_pre_grad)
        add_up(TAPS + 5, rate_grad * recur_gate)
        return hidden[block - SUB :, :]

    lax.fori_loop(0, count, through_gates, before_first)
    for tap in range(TAPS - 1):
        rows_here = slice(tap * SUB, (tap + 1) * SUB)
        filtered_grad_ref[rows + tap * SUB : rows + (tap + 1) * SUB, :] = later_chunk(
            filtered_grad_ref[rows_here, :], channels
        )
        later_offset_ref[block + tap * SUB : block + (tap + 1) * SUB, :] = later_chunk(
            offset_ref[rows_here, :], channels
        )
    later_offset_ref[:block, :] = offset_ref[rows - block :, :]

    def through_taps(start, offsets_ref, offset_start):
        total = param[0] * filtered_grad_ref[pl.ds(start, block), :]
        for tap in range(1, TAPS):
            later = filtered_grad_ref[pl.ds(start + tap * SUB, block), :]
            offset = offsets_ref[pl.ds(offset_start + tap * SUB, block), :]
            total = total + param[tap] * jnp.where(offset >= tap, later, 0.0)
        back_ref[pl.ds(start, block), :] = total

    def inner_taps(step, carry):
        start = pl.multiple_of(step * block, block)
        through_taps(start, offset_ref, start)
        return carry

    lax.fori_loop(0, count - 1, inner_taps, 0)
    through_taps(rows - block, later_offset_ref, 0)
    out_of_order(back_ref, slot_ref, narrow_ref, grads_ref)


def shapes_of(data):
    sources, channels, tokens = data.shape
    rows = sources * tokens * channels // LANES
    return sources, channels, tokens, rows


def slot_columns(slot):
    sources, _, tokens = slot.shape
    per_block = math.gcd(sources, 16)
    return slot.reshape(sources // per_block, per_block, tokens).astype(jnp.float32)


def recurrence_forward(data, slot, offset, params):
    sources, channels, tokens, rows = shapes_of(data)
    whole = jax.ShapeDtypeStruct((rows, LANES), jnp.float32)
    padded = jax.ShapeDtypeStruct((rows + (TAPS - 1) * SUB, LANES), jnp.float32)
    count = sources * tokens
    return pl.pallas_call(
        forward_kernel,
        out_shape=(jax.ShapeDtypeStruct(data.shape, jnp.bfloat16), padded, whole, whole, whole),
        scratch_shapes=[
            pltpu.VMEM((LANES, rows), jnp.float32),
            pltpu.VMEM((rows, LANES), jnp.float32),
            pltpu.VMEM((LANES // channels, channels, rows), jnp.bfloat16),
            pltpu.VMEM((sources, tokens, 128), jnp.float32),
            pltpu.VMEM((rows + (TAPS - 1) * SUB, LANES), jnp.float32),
            pltpu.VMEM((rows, LANES), jnp.float32),
            pltpu.VMEM((rows, LANES), jnp.float32),
            pltpu.VMEM((rows, LANES), jnp.float32),
            pltpu.SemaphoreType.DMA((4,)),
        ],
        in_specs=[pl.BlockSpec(memory_space=pltpu.VMEM)] * 5,
        out_specs=(pl.BlockSpec(memory_space=pltpu.VMEM),)
        + (pl.BlockSpec(memory_space=pl.ANY),) * 4,
        compiler_params=pltpu.CompilerParams(vmem_limit_bytes=VMEM_LIMIT),
        cost_estimate=pl.CostEstimate(
            flops=0, bytes_accessed=0, transcendentals=0
        ),
        name="recurrence_forward",
    )(data, slot, slot_columns(slot), offset, params)


def recurrence_backward(data, slot, offset, params, inputs, filtered, decay, hidden):
    sources, channels, tokens, rows = shapes_of(data)
    count = sources * tokens
    return pl.pallas_call(
        backward_kernel,
        out_shape=(
            jax.ShapeDtypeStruct(data.shape, jnp.bfloat16),
            jax.ShapeDtypeStruct((TAPS + 6, SUB, LANES), jnp.float32),
        ),
        scratch_shapes=[
            pltpu.VMEM((LANES, rows), jnp.float32),
            pltpu.VMEM((rows, LANES), jnp.float32),
            pltpu.VMEM((rows, LANES), jnp.float32),
            pltpu.VMEM((LANES // channels, channels, rows), jnp.bfloat16),
            pltpu.VMEM((rows + (TAPS - 1) * SUB, LANES), jnp.float32),
            pltpu.VMEM((UNROLL * SUB + (TAPS - 1) * SUB, LANES), jnp.float32),
            pltpu.VMEM((sources, tokens, 128), jnp.float32),
            pltpu.VMEM((rows + (TAPS - 1) * SUB, LANES), jnp.float32),
            pltpu.VMEM((rows, LANES), jnp.float32),
            pltpu.VMEM((rows, LANES), jnp.float32),
            pltpu.VMEM((rows, LANES), jnp.float32),
            pltpu.SemaphoreType.DMA((4,)),
        ],
        in_specs=[pl.BlockSpec(memory_space=pltpu.VMEM)] * 5
        + [pl.BlockSpec(memory_space=pl.ANY)] * 4,
        compiler_params=pltpu.CompilerParams(vmem_limit_bytes=VMEM_LIMIT),
        cost_estimate=pl.CostEstimate(
            flops=0, bytes_accessed=0, transcendentals=0
        ),
        name="recurrence_backward",
    )(data, slot, slot_columns(slot), offset, params, inputs, filtered, decay, hidden)


def arrangement(lengths, permutation, sources, channels):
    total = permutation.shape[0]
    groups = LANES // channels
    rows = total // groups
    steps = rows // SUB
    chunk = permutation // steps
    slot = (chunk // SUB) * rows + (permutation % steps) * SUB + chunk % SUB
    seq_ends = jnp.cumsum(lengths)
    seq_starts = seq_ends - lengths
    row, lane = np.arange(rows), np.arange(LANES)
    of_row = jnp.asarray((row % SUB) * steps + row // SUB, jnp.int32)
    of_lane = jnp.asarray((lane // channels) * (SUB * steps), jnp.int32)
    position = of_row[:, None] + of_lane[None, :]
    seg_first = jnp.zeros_like(position)
    for k in range(lengths.shape[0]):
        start = seq_starts[k]
        seg_first = jnp.where(position >= start, start, seg_first)
    offset = jnp.minimum(position - seg_first, TAPS - 1).astype(jnp.float32)
    return slot.reshape(sources, 1, total // sources), offset


def lane_params(conv_weight, conv_bias, gate_weight, gate_bias, decay_logits):
    stacked = jnp.concatenate(
        [
            conv_weight,
            conv_bias[None],
            gate_weight,
            gate_bias,
            RATE_SCALE * jax.nn.softplus(-decay_logits)[None],
        ]
    )
    return jnp.tile(stacked, (1, LANES // stacked.shape[1]))


def channel_sums(sums, channels, decay_logits):
    sums = jnp.sum(sums, axis=1).reshape(TAPS + 6, LANES // channels, channels).sum(axis=1)
    logit = -RATE_SCALE * jax.nn.sigmoid(-decay_logits)[None] * sums[TAPS + 5 :]
    return jnp.concatenate([sums[: TAPS + 5], logit])


def swap_core(values):
    return lax.ppermute(values, "fsdp", [(0, 1), (1, 0)])


def swap_bit(values, bit):
    count = lax.axis_size("seq")
    return lax.ppermute(values, "seq", [(i, i ^ (1 << bit)) for i in range(count)])


def half(values, index, axis):
    size = values.shape[axis] // 2
    return lax.dynamic_slice_in_dim(values, index * size, size, axis)


def reorder_blocks(values, low_bit, high_bit, axis):
    width = high_bit - low_bit
    size = values.shape[axis] >> width
    pieces = []
    for place in range(1 << width):
        natural = sum(((place >> (width - 1 - k)) & 1) << k for k in range(width))
        pieces.append(lax.slice_in_dim(values, natural * size, (natural + 1) * size, axis=axis))
    return jnp.concatenate(pieces, axis=axis)


def trade_channels(values):
    return lax.all_to_all(values, "seq", split_axis=0, concat_axis=0, tiled=True)


def after(values, *earlier):
    return lax.optimization_barrier((values,) + earlier)[0]


def product(subscripts, left, right):
    return jnp.einsum(subscripts, left, right, preferred_element_type=jnp.float32)


class Links:
    def __init__(self, place, core):
        count = lax.axis_size("seq").bit_length() - 1
        self.core = core
        self.bits = [(place >> bit) & 1 for bit in range(count)]

    def own(self, link):
        return self.core if link == "core" else self.bits[link]

    def swap(self, link, values, *earlier):
        if earlier:
            values = after(values, *earlier)
        return swap_core(values) if link == "core" else swap_bit(values, link)


class Chain:
    def __init__(self, links, terms, sums, collects=(), turn=False, rider=None):
        self.links, self.terms, self.rider = links, list(terms), rider
        self.sums, self.collects, self.turn = list(sums), list(collects), turn
        self.send()

    def total(self):
        return sum(term.astype(jnp.float32) for term in self.terms)

    def send(self):
        if self.sums:
            self.link, self.axis = self.sums[0]
        elif self.collects:
            total = self.total()
            self.terms = [total.T if self.turn else total]
            self.turn = False
            self.link, self.axis = self.collects[0], 0
        else:
            return
        own_bit = self.links.own(self.link)
        sent = sum(half(term, 1 - own_bit, self.axis).astype(jnp.float32) for term in self.terms)
        self.sent = sent.astype(jnp.bfloat16)
        self.other = self.links.swap(self.link, self.sent)
        self.terms = [half(term, own_bit, self.axis) for term in self.terms]
        if self.rider is not None:
            self.rider_other = self.links.swap(self.link, self.rider)

    def advance(self, token):
        other = after(self.other, token)
        if self.rider is not None:
            self.rider = self.rider + after(self.rider_other, token)
        if self.sums:
            self.terms.append(other)
            self.sums.pop(0)
        else:
            own, other = self.terms[0], other.astype(jnp.float32)
            first = self.links.own(self.link) == 0
            low, high = jnp.where(first, own, other), jnp.where(first, other, own)
            self.terms = [jnp.concatenate([low, high], axis=1)]
            self.collects.pop(0)
        if not self.sums and not self.collects:
            return token
        self.send()
        return self.sent


def both_cores(values, *earlier):
    return lax.all_gather(after(values, *earlier) if earlier else values, "fsdp")


def pick(values, *index):
    for place in index:
        values = lax.dynamic_index_in_dim(values, place, 0, keepdims=False)
    return values


def largest_tile(size, most, step):
    return max(tile for tile in range(step, most + 1, step) if size % tile == 0)


def grad_kernel(count, turned, select_ref, *refs):
    per_piece = turned or 1
    lefts = [ref[...] for ref in refs[: count * per_piece]]
    rights = [ref[...] for ref in refs[count * per_piece : count * (per_piece + 1)]]
    rights = jnp.concatenate(rights, axis=0)
    if turned:
        if per_piece > 1:
            lefts = [
                jnp.concatenate(lefts[k * per_piece : (k + 1) * per_piece], axis=1)
                for k in range(count)
            ]
        total = lax.dot_general(
            jnp.concatenate(lefts, axis=0),
            rights,
            (((0,), (0,)), ((), ())),
            preferred_element_type=jnp.float32,
        )
    else:
        total = jnp.dot(
            jnp.concatenate(lefts, axis=1), rights, preferred_element_type=jnp.float32
        )
    for ref in refs[count * (per_piece + 1) : -1]:
        total = total + ref[...].astype(jnp.float32)
    refs[-1][...] = total.astype(jnp.bfloat16)


(CORE, OTHER_CORE), (X, OTHER_X), (Y, OTHER_Y), (LOW, OTHER_LOW), (TOP, OTHER_TOP) = (
    (("scalar", 2 * k), ("scalar", 2 * k + 1)) for k in range(5)
)


def grad_product(select, pieces, rows, row_half=None, added=None, columns=None, counted=False):
    cols = pieces[0][2].shape[-1]
    tile_rows = largest_tile(rows, 512, 16) if columns is None else rows // columns[0]
    tile_cols = largest_tile(cols, 1024 if columns is None else 1536, 256)

    def entry(index, select_ref):
        return select_ref[index[1]] if isinstance(index, tuple) else index

    def left_spec(left, lead):
        def place(m, n, select_ref):
            start = 0 if row_half is None else entry(row_half, select_ref) * (rows // tile_rows)
            return tuple(entry(i, select_ref) for i in lead) + (start + m, 0)

        return pl.BlockSpec((None,) * len(lead) + (tile_rows, left.shape[-1]), place)

    def column_spec(left, lead, which):
        def place(m, n, select_ref):
            block = columns[2](m, partial(entry, select_ref=select_ref))[which]
            return tuple(entry(i, select_ref) for i in lead) + (0, block)

        return pl.BlockSpec((None,) * len(lead) + (left.shape[-2], columns[1]), place)

    def right_spec(right, lead):
        def place(m, n, select_ref):
            return tuple(entry(i, select_ref) for i in lead) + (0, n)

        return pl.BlockSpec((None,) * len(lead) + (right.shape[-2], tile_cols), place)

    out_spec = pl.BlockSpec((tile_rows, tile_cols), lambda m, n, select_ref: (m, n))
    turned = 0 if columns is None else tile_rows // columns[1]
    if turned:
        in_specs = [column_spec(p[0], p[1], which) for p in pieces for which in range(turned)]
        operands = [p[0] for p in pieces for _ in range(turned)]
    else:
        in_specs = [left_spec(left, lead) for left, lead, _, _ in pieces]
        operands = [left for left, _, _, _ in pieces]
    in_specs += [right_spec(right, lead) for _, _, right, lead in pieces]
    operands += [right for _, _, right, _ in pieces]
    if added is not None:
        in_specs.append(out_spec)
        operands.append(added)
    return pl.pallas_call(
        partial(grad_kernel, len(pieces), turned),
        out_shape=jax.ShapeDtypeStruct((rows, cols), jnp.bfloat16),
        grid_spec=pltpu.PrefetchScalarGridSpec(
            num_scalar_prefetch=1,
            grid=(rows // tile_rows, cols // tile_cols),
            in_specs=in_specs,
            out_specs=out_spec,
        ),
        compiler_params=pltpu.CompilerParams(vmem_limit_bytes=VMEM_LIMIT),
        cost_estimate=pl.CostEstimate(
            flops=counted * 2 * rows * cols * sum(p[2].shape[-2] for p in pieces),
            bytes_accessed=counted * 2 * rows * cols,
            transcendentals=0,
        ),
        name="weight_grad",
    )(select, *operands)


GELU_SCALE = 0.7978845608028654
GELU_CUBE = 0.044715
HIDDEN_TILE = 512


def mlp_kernel(
    bits_ref, normed_ref, down_grad_ref, gate_ref, up_ref, down_ref,
    branch_ref, normed_grad_ref, mixed_ref, sent_gate_ref, sent_up_ref, kept_gate_ref, kept_up_ref,
):
    step = pl.program_id(0)
    by_columns = (((1,), (1,)), ((), ()))
    normed = normed_ref[...]
    first = jnp.dot(normed, gate_ref[...], preferred_element_type=jnp.float32)
    second = jnp.dot(normed, up_ref[...], preferred_element_type=jnp.float32)
    mixed_grad = lax.dot_general(
        down_grad_ref[...], down_ref[...], by_columns, preferred_element_type=jnp.float32
    )
    square = first * first
    bend = jnp.tanh(GELU_SCALE * first * (1.0 + GELU_CUBE * square))
    rise = 0.5 + 0.5 * bend
    gelu = first * rise
    slope = rise + 0.5 * GELU_SCALE * first * (1.0 - bend * bend) * (
        1.0 + 3.0 * GELU_CUBE * square
    )
    mixed = gelu * second
    first_low = (mixed_grad * slope * second).astype(jnp.bfloat16)
    second_low = (mixed_grad * gelu).astype(jnp.bfloat16)
    mixed_ref[...] = mixed.T.astype(jnp.bfloat16)

    side = (step // (pl.num_programs(0) // 4)) % 2
    for which, low, sent_ref, kept_ref in (
        (0, first_low, sent_gate_ref, kept_gate_ref),
        (1, second_low, sent_up_ref, kept_up_ref),
    ):

        @pl.when(side != bits_ref[which])
        def _(low=low, sent_ref=sent_ref):
            sent_ref[...] = low

        @pl.when(side == bits_ref[which])
        def _(low=low, kept_ref=kept_ref):
            kept_ref[...] = low

    @pl.when(step == 0)
    def _():
        branch_ref[...] = jnp.zeros_like(branch_ref)
        normed_grad_ref[...] = jnp.zeros_like(normed_grad_ref)

    branch_ref[...] += jnp.dot(
        mixed.astype(jnp.bfloat16), down_ref[...], preferred_element_type=jnp.float32
    )
    normed_grad_ref[...] += lax.dot_general(
        first_low, gate_ref[...], by_columns, preferred_element_type=jnp.float32
    ) + lax.dot_general(second_low, up_ref[...], by_columns, preferred_element_type=jnp.float32)


def mlp_both_ways(bits, normed, down_grad, w_gate, w_up, w_down):
    count, width = normed.shape
    hidden = w_gate.shape[1]
    steps = hidden // HIDDEN_TILE
    tiles = steps // 4

    whole = pl.BlockSpec((count, width), lambda t, bits_ref: (0, 0))
    column = pl.BlockSpec((width, HIDDEN_TILE), lambda t, bits_ref: (0, t))
    row = pl.BlockSpec((HIDDEN_TILE, width), lambda t, bits_ref: (t, 0))
    turned = pl.BlockSpec((HIDDEN_TILE, count), lambda t, bits_ref: (t, 0))

    def traded(which, kept):
        def place(t, bits_ref):
            wanted = bits_ref[which] if kept else 1 - bits_ref[which]
            side = (t // tiles) % 2
            resting = jnp.where(wanted == 0, tiles - 1, 0)
            return (t // (2 * tiles), 0, jnp.where(side == wanted, t % tiles, resting))

        return pl.BlockSpec((None, count, HIDDEN_TILE), place)

    summed = jax.ShapeDtypeStruct((count, width), jnp.float32)
    return pl.pallas_call(
        mlp_kernel,
        out_shape=(summed, summed, jax.ShapeDtypeStruct((hidden, count), jnp.bfloat16))
        + (jax.ShapeDtypeStruct((2, count, hidden // 4), jnp.bfloat16),) * 4,
        grid_spec=pltpu.PrefetchScalarGridSpec(
            num_scalar_prefetch=1,
            grid=(steps,),
            in_specs=[whole, whole, column, column, row],
            out_specs=[whole, whole, turned]
            + [traded(which, kept) for kept in (False, True) for which in (0, 1)],
        ),
        compiler_params=pltpu.CompilerParams(vmem_limit_bytes=VMEM_LIMIT),
        cost_estimate=pl.CostEstimate(flops=0, bytes_accessed=0, transcendentals=0),
        name="mlp_both_ways",
    )(jnp.stack(bits).astype(jnp.int32), normed, down_grad, w_gate, w_up, w_down)


MIDDLE_TILE = 512


def middle_kernel(
    core_ref, normed_grad_ref, middle_ref, cotangent_ref, gain_ref, output_ref, own_ref, other_ref,
    state_ref, pre_ref,
    middle_grad_ref, out_grad_ref, gain_grad_ref, state_grad_ref, gate_grad_ref, back_ref,
):
    by_columns = (((1,), (1,)), ((), ()))

    @pl.when(pl.program_id(0) == 0)
    def _():
        middle = middle_ref[...]
        normed_grad = normed_grad_ref[...]
        inverse = lax.rsqrt(jnp.mean(middle * middle, axis=1, keepdims=True) + NORM_EPS)
        scaled = normed_grad * gain_ref[...]
        lean = jnp.mean(scaled * middle, axis=1, keepdims=True)
        total = cotangent_ref[...] + inverse * scaled - middle * (inverse * inverse * inverse * lean)
        middle_grad_ref[...] = total
        out_grad_ref[...] = total.astype(jnp.bfloat16)
        gain_grad_ref[...] = jnp.sum(normed_grad * middle * inverse, axis=0, keepdims=True)
        back_ref[...] = jnp.zeros_like(back_ref)

    grad = lax.dot_general(
        output_ref[...], out_grad_ref[...], by_columns, preferred_element_type=jnp.float32
    )
    pre = pre_ref[...]
    square = pre * pre
    bend = jnp.tanh(GELU_SCALE * pre * (1.0 + GELU_CUBE * square))
    rise = 0.5 + 0.5 * bend
    slope = rise + 0.5 * GELU_SCALE * pre * (1.0 - bend * bend) * (1.0 + 3.0 * GELU_CUBE * square)
    state_grad_ref[...] = (grad * pre * rise).astype(jnp.bfloat16)
    gate_grad = (grad * state_ref[...].astype(jnp.float32) * slope).astype(jnp.bfloat16)
    gate_grad_ref[...] = gate_grad
    width = own_ref.shape[0]
    for ref, place in ((own_ref, core_ref[0]), (other_ref, 1 - core_ref[0])):
        columns = pl.ds(pl.multiple_of(place * width, width), width)
        back_ref[:, columns] += lax.dot_general(
            gate_grad, ref[...], (((0,), (1,)), ((), ())), preferred_element_type=jnp.float32
        )


def middle_backward(core, normed_grad, middle, cotangent, gain, w_output, own, other, states, pre):
    count, width = middle.shape
    channels = w_output.shape[0]
    whole = pl.BlockSpec((count, width), lambda t, core_ref: (0, 0))
    line = pl.BlockSpec((1, width), lambda t, core_ref: (0, 0))
    row = pl.BlockSpec((MIDDLE_TILE, width), lambda t, core_ref: (t, 0))
    column = pl.BlockSpec((width // 2, MIDDLE_TILE), lambda t, core_ref: (0, t))
    turned = pl.BlockSpec((MIDDLE_TILE, count), lambda t, core_ref: (t, 0))
    wide = jax.ShapeDtypeStruct((count, width), jnp.float32)
    low = jax.ShapeDtypeStruct((channels, count), jnp.bfloat16)
    return pl.pallas_call(
        middle_kernel,
        out_shape=(
            wide,
            jax.ShapeDtypeStruct((count, width), jnp.bfloat16),
            jax.ShapeDtypeStruct((1, width), jnp.float32),
            low,
            low,
            wide,
        ),
        grid_spec=pltpu.PrefetchScalarGridSpec(
            num_scalar_prefetch=1,
            grid=(channels // MIDDLE_TILE,),
            in_specs=[whole, whole, whole, line, row, column, column, turned, turned],
            out_specs=[whole, whole, line, turned, turned, whole],
        ),
        compiler_params=pltpu.CompilerParams(vmem_limit_bytes=VMEM_LIMIT),
        cost_estimate=pl.CostEstimate(flops=0, bytes_accessed=0, transcendentals=0),
        name="middle_backward",
    )(core.astype(jnp.int32).reshape(1), normed_grad, middle, cotangent, gain, w_output, own, other, states, pre)


class Traded:
    def __init__(self, links, channel_grad):
        channels, count = channel_grad.shape
        self.links = links
        self.mine = channel_grad.reshape(2, 2, channels // 4, count)
        self.by_core = links.swap("core", pick(self.mine, 1 - links.core))

    def trade_x(self, token):
        core, other = self.links.core, 1 - self.links.bits[0]
        self.by_core = after(self.by_core, token)
        sent = jnp.stack([pick(self.mine, core, other), pick(self.by_core, other)])
        self.by_x = self.links.swap(0, sent)
        return sent

    def grad(self, select, normed_pieces):
        lefts = [(self.mine, (CORE, X)), (self.by_core, (X,)), (self.by_x, (0,)), (self.by_x, (1,))]
        pieces = [left + right for left, right in zip(lefts, normed_pieces)]
        return grad_product(select, pieces, self.mine.shape[2])


def per_device(
    tokens,
    cotangent,
    gate_proj,
    input_proj,
    output_proj,
    mlp_gate,
    mlp_up,
    mlp_down,
    gain_a,
    gain_b,
    conv_weight,
    conv_bias,
    gate_weight,
    gate_bias,
    decay_logits,
    lengths,
    permutation,
):
    w_input, w_output, w_mlpgate, w_mlpup, w_down = (
        lax.all_gather(input_proj, "fsdp", axis=0, tiled=True),
        lax.all_gather(output_proj, "fsdp", axis=0, tiled=True),
        lax.all_gather(mlp_gate, "fsdp", axis=0, tiled=True),
        lax.all_gather(mlp_up, "fsdp", axis=0, tiled=True),
        lax.all_gather(mlp_down, "fsdp", axis=0, tiled=True),
    )
    core = lax.axis_index("fsdp")
    place = lax.axis_index("seq")
    links = Links(place, core)
    x, y = links.bits[0], links.bits[1]
    bit_count = len(links.bits)
    top = bit_count - 1
    low = links.bits[2]
    own_bits = (core, x, y, low, links.bits[top])
    select = jnp.stack([value for bit in own_bits for value in (bit, 1 - bit)]).astype(jnp.int32)
    channels = decay_logits.shape[0]
    count, width = tokens.shape
    block_shape = (lax.axis_size("seq"), channels, count)
    gains = jnp.stack([gain_a, gain_b])
    other_gains = links.swap("core", gains)
    full_gain_a, full_gain_b = jnp.where(
        core == 0,
        jnp.concatenate([gains, other_gains], axis=1),
        jnp.concatenate([other_gains, gains], axis=1),
    )
    other_input = links.swap("core", input_proj)
    other_gate = links.swap("core", gate_proj)
    normed_a, norm_back_a = jax.vjp(rms_norm, tokens, full_gain_a.astype(jnp.float32))
    normed_a_low = normed_a.astype(jnp.bfloat16)
    down_grad = cotangent.astype(jnp.bfloat16)
    input_pre = product("td,dr->rt", half(normed_a_low, core, 1), input_proj)
    input_pre = input_pre + product("td,dr->rt", half(normed_a_low, 1 - core, 1), other_input)
    input_low = input_pre.astype(jnp.bfloat16)
    channel_in = trade_channels(input_low)
    late_lengths, late_permutation = after((lengths, permutation), input_low)
    slot, offset = arrangement(late_lengths[0], late_permutation[0], block_shape[0], channels)
    params = lane_params(conv_weight, conv_bias, gate_weight, gate_bias, decay_logits)
    normed_late = after(normed_a_low, offset, slot, params)
    gate_pre = product("td,dr->rt", half(normed_late, core, 1), gate_proj)
    gate_pre = gate_pre + product("td,dr->rt", half(normed_late, 1 - core, 1), other_gate)
    normed_order = reorder_blocks(normed_a_low, 1, bit_count, 1)
    normed_core = both_cores(normed_order, channel_in)
    channel_in, gate_pre = lax.optimization_barrier((channel_in, gate_pre))
    down_y = links.swap(1, down_grad, channel_in)
    normed_x = links.swap(0, normed_order, channel_in)
    states, *kept = recurrence_forward(channel_in.reshape(block_shape), slot, offset, params)
    states = after(states, normed_x, down_y)
    state_tokens = trade_channels(states.reshape(input_pre.shape))
    normed_both = both_cores(normed_x, states)
    normed_pieces = [(normed_order, ()), (normed_core, (OTHER_CORE,))]
    normed_pieces += [(normed_x, ()), (normed_both, (OTHER_CORE,))]
    gated_low = gated_state(state_tokens.astype(jnp.float32), gate_pre).astype(jnp.bfloat16)
    branch_a = product("rt,rd->td", gated_low, w_output)
    middle = tokens + branch_a
    gain_b_wide = full_gain_b.astype(jnp.float32)
    normed_b_low = rms_norm(middle, gain_b_wide).astype(jnp.bfloat16)
    rows_total = gated_low.shape[0]
    shape = (2,) * bit_count + (2, rows_total // (2 << bit_count), count)
    rest = tuple(range(bit_count - 3, -1, -1))
    out_order = (2, 0, 1, *range(3, bit_count))
    dims = (bit_count, *(top - bit for bit in out_order), bit_count + 1, bit_count + 2)
    shape_out, dims_out = shape, dims
    fars = [links.swap(bit, normed_b_low) for bit in (0, 2)]
    down_top = links.swap(top, after(down_grad, normed_b_low))
    mlp_parts = mlp_both_ways((x, low), normed_b_low, down_grad, w_mlpgate, w_mlpup, w_down)
    arrived = lax.optimization_barrier((*mlp_parts, down_top, *fars))
    branch_b, normed_b_grad, mixed, sent_gate, sent_up, kept_gate, kept_up = arrived[:7]
    down_top, *fars = arrived[7:]
    hidden_far = [links.swap(0, sent_gate), links.swap(2, sent_up)]
    high = mixed.reshape((1 << (bit_count - 2), 2, mixed.shape[0] >> (bit_count - 1), count))
    mixed_send = lax.dynamic_index_in_dim(high, 1 - y, 1, keepdims=False)
    mixed_y = links.swap(1, mixed_send)
    output = middle + branch_b
    sums = jnp.stack(
        (
            jnp.sum(tokens * tokens),
            jnp.sum(branch_a * branch_a),
            jnp.sum(middle * middle),
            jnp.sum(branch_b * branch_b),
        )
    )
    entry_total = tokens.shape[0] * tokens.shape[1] * lax.axis_size("seq") * lax.axis_size("fsdp")
    middle_grad, out_grad_low, gain_b_grad, state_low, gate_low, gate_part = middle_backward(
        core,
        normed_b_grad,
        middle,
        cotangent,
        gain_b_wide[None],
        w_output,
        gate_proj,
        other_gate,
        state_tokens,
        gate_pre,
    )
    arrived = lax.optimization_barrier((state_low, gate_low, out_grad_low, *hidden_far, mixed_y))
    state_low, gate_low, out_grad_low, *hidden_far, mixed_y = arrived
    block = mixed.shape[0] // (2 << bit_count)
    axes = [top - bit for bit in (1, top)] + [bit_count] + [top - bit for bit in (0, *range(2, top))]
    mixed_mine = after(mixed, state_low).reshape((2,) * bit_count + (2, block, count))
    mixed_mine = mixed_mine.transpose(axes + [bit_count + 1, bit_count + 2])
    mixed_mine = mixed_mine.reshape(2, 2, 2, mixed.shape[0] // 8, count)
    axes = [0, bit_count - 1, bit_count - 2] + [top - bit for bit in range(2, top)]
    mixed_y = mixed_y.reshape((2,) * bit_count + (block, count))
    mixed_y = mixed_y.transpose(axes + [bit_count, bit_count + 1])
    mixed_y = mixed_y.reshape(2, 2, mixed.shape[0] // 8, count)
    gain_b_grad = gain_b_grad[0]
    channel_grad = trade_channels(state_low)

    normed_b_core = both_cores(normed_b_low)
    hidden_pieces = []
    for index in (0, 1):
        mine, far = (kept_gate, kept_up)[index], hidden_far[index]
        far_core = both_cores(fars[index], mixed_send)
        both = jnp.stack([pick(mine, 1 - core), pick(after(far, state_low), 1 - core)])
        by_core = links.swap("core", both)
        hidden_pieces.append(
            [
                (normed_b_low, (), mine, (CORE,)),
                (fars[index], (), far, (CORE,)),
                (normed_b_core, (OTHER_CORE,), by_core, (0,)),
                (far_core, (OTHER_CORE,), by_core, (1,)),
            ]
        )
    aligned = (width >> bit_count) % 128 == 0
    hidden_orders = ((1, (*range(2, bit_count),), 0), (0, (1, *range(3, bit_count)), 2))
    if not aligned:
        for pieces, (summed, between, traded_bit) in zip(hidden_pieces, hidden_orders):
            for k, (left, lead, right, right_lead) in enumerate(pieces):
                split = left.reshape(left.shape[:-1] + (2,) * bit_count + (width >> bit_count,))
                first = left.ndim - 1
                axes = [first + top - bit for bit in (summed, *between, traded_bit)]
                axes = tuple(range(first)) + tuple(axes) + (first + bit_count,)
                split = split.transpose(axes).reshape(left.shape)
                pieces[k] = (jnp.swapaxes(split, -1, -2), lead, right, right_lead)

    def hidden_product(index, half_rows, token, added=None, counted=False):
        chosen = after(select, token)
        if not aligned:
            return grad_product(chosen, hidden_pieces[index], width // 2, half_rows, added)
        summed, between, traded_bit = hidden_orders[index]

        def blocks(m, entry):
            place = entry(half_rows) << summed
            for k, bit in enumerate(reversed(between)):
                place = place + (((m >> k) & 1) << bit)
            return [place >> 1] if traded_bit == 0 else [place, place + (1 << traded_bit)]

        columns = (1 << len(between), width >> (bit_count - (traded_bit == 0)), blocks)
        return grad_product(chosen, hidden_pieces[index], width // 2, None, added, columns, counted)

    rest_bits = range(2, bit_count)
    mixed_two = jnp.stack(
        [pick(mixed_mine, y, 1 - own_bits[4]), pick(mixed_y, 1 - own_bits[4])]
    )
    down_both = links.swap(1, down_top, state_low)
    down_pieces = [(piece, ()) for piece in (down_grad, down_y, down_top, down_both)]
    gate_traded = Traded(links, gate_low)
    gated_mine = after(gated_low, state_low).reshape(shape_out).transpose(dims_out)
    gated_mine = gated_mine.reshape(2, 2, rows_total // 4, count)
    gated_core = links.swap("core", pick(gated_mine, 1 - core))
    gated_two = jnp.stack([pick(gated_mine, core, 1 - low), pick(gated_core, 1 - low)])
    gate_sent = hidden_product(0, OTHER_Y, gated_two, None, True)
    up_sent = hidden_product(1, OTHER_X, gate_sent, None, True)
    channel_grad = after(channel_grad, mixed_two, up_sent, gate_traded.by_core, down_both)
    gate_received = links.swap(1, gate_sent, channel_grad)
    up_received = links.swap(0, up_sent, channel_grad)
    mixed_far = links.swap(top, mixed_two, channel_grad)
    out_far = links.swap(2, out_grad_low, channel_grad)
    channel_grad = after(channel_grad, up_sent)

    dealt_grad, lane_sums = recurrence_backward(
        channel_grad.reshape(block_shape), slot, offset, params, *kept
    )
    dealt_grad = after(dealt_grad, out_far)
    input_grad = trade_channels(dealt_grad.reshape(state_low.shape))
    def down_product(chosen, token, added=None):
        lefts = [(mixed_mine, (Y, TOP, chosen)), (mixed_y, (TOP, chosen))]
        lefts += [(mixed_far, (k, chosen)) for k in range(2)]
        pieces = [left + right for left, right in zip(lefts, down_pieces)]
        return grad_product(after(select, token), pieces, mixed.shape[0] // 8, None, added)

    hidden_sums = [(bit, 0) for bit in rest_bits]
    projection_sums = [(bit, 1) for bit in range(1, bit_count)]
    token = after(dealt_grad, gate_received, up_received, mixed_far)
    gate_total = hidden_product(0, Y, token, gate_received)
    gated_far = links.swap(2, gated_two, gate_total)
    token = gate_traded.trade_x(gate_total)
    gate_chain = Chain(links, [gate_total], hidden_sums, (0, "core"))
    up_total = hidden_product(1, X, token, up_received)
    up_sums = [(bit, 0) for bit in (1, *range(3, bit_count))]
    up_chain = Chain(links, [up_total], up_sums, (2, "core"))
    down_sent = down_product(OTHER_CORE, up_total)
    down_received = links.swap("core", down_sent)
    input_grad = after(input_grad, down_sent)
    input_traded = Traded(links, input_grad)
    token = input_traded.trade_x(input_grad)
    out_core = both_cores(out_grad_low, dealt_grad)
    out_both = both_cores(out_far, dealt_grad)
    out_pieces = [
        (gated_mine, (CORE, LOW), out_grad_low, ()),
        (gated_core, (LOW,), out_core, (OTHER_CORE,)),
        (gated_far, (0,), out_far, ()),
        (gated_far, (1,), out_both, (OTHER_CORE,)),
    ]
    down_total = down_product(CORE, token, down_received)
    input_total = input_traded.grad(after(select, down_total), normed_pieces)
    input_chain = Chain(links, [input_total], projection_sums, (0, "core"), True)
    down_total = after(down_total, input_chain.sent)
    down_chain = Chain(links, [down_total], [(bit, 0) for bit in (0, *range(2, top))])
    token = gate_chain.advance(down_chain.sent)
    token = up_chain.advance(token)
    input_grad = after(input_grad, token)
    normed_a_grad = gate_part + product("rt,dr->td", input_grad, w_input)
    token_norm_grad, gain_a_grad = norm_back_a(normed_a_grad)
    token_grad = middle_grad + token_norm_grad
    small = jnp.concatenate([gain_a_grad, gain_b_grad, sums])
    gate_proj_total = gate_traded.grad(after(select, token_grad), normed_pieces)
    token = input_chain.advance(gate_proj_total)
    gate_proj_total = after(gate_proj_total, token)
    gate_proj = Chain(links, [gate_proj_total], projection_sums, (0, "core"), True, small)
    out_sent = grad_product(after(select, gate_proj.sent), out_pieces, rows_total // 8, OTHER_X)
    token = down_chain.advance(out_sent)
    out_received = links.swap(0, out_sent, token)
    token = input_chain.advance(token)
    token = gate_chain.advance(token)
    token = gate_proj.advance(token)
    token = up_chain.advance(token)
    token = input_chain.advance(token)
    out_total = grad_product(after(select, token), out_pieces, rows_total // 8, X, out_received)
    out_chain = Chain(links, [out_total], up_sums)
    token = gate_proj.advance(out_total)
    chains = [gate_chain, down_chain, input_chain, out_chain, gate_proj, up_chain]
    while any(chain.sums or chain.collects for chain in chains):
        for chain in chains:
            if chain.sums or chain.collects:
                token = chain.advance(token)
    param_sums = channel_sums(lane_sums, channels, decay_logits)
    param_sums = param_sums + links.swap("core", after(param_sums, up_sent))
    totals = gate_proj.rider
    gain_size = width // (lax.axis_size("seq") * lax.axis_size("fsdp"))
    gain_start = (place * lax.axis_size("fsdp") + core) * gain_size
    return (
        output,
        token_grad,
        gate_proj.total(),
        input_chain.total(),
        out_chain.total(),
        gate_chain.total(),
        up_chain.total(),
        down_chain.total(),
        lax.dynamic_slice_in_dim(totals, gain_start, gain_size, 0),
        lax.dynamic_slice_in_dim(totals, width + gain_start, gain_size, 0),
        param_sums[:TAPS],
        param_sums[TAPS],
        param_sums[TAPS + 1 : TAPS + 3],
        param_sums[TAPS + 3 : TAPS + 5],
        param_sums[TAPS + 5],
        jnp.sqrt(totals[2 * width :] / entry_total),
    )


def solution(mesh):
    in_specs = (
        P(("seq", "fsdp"), None),
        P(("seq", "fsdp"), None),
        P("fsdp", None),
        P("fsdp", None),
        P("fsdp", None),
        P("fsdp", None),
        P("fsdp", None),
        P("fsdp", None),
        P("fsdp"),
        P("fsdp"),
        P(None, "seq"),
        P("seq"),
        P(None, "seq"),
        P(None, "seq"),
        P("seq"),
        P("fsdp", None),
        P("fsdp", None),
    )
    out_specs = (
        P(("seq", "fsdp"), None),
        P(("seq", "fsdp"), None),
        P(("seq", "fsdp"), None),
        P(("seq", "fsdp"), None),
        P(("seq", "fsdp"), None),
        P(("seq", "fsdp"), None),
        P(("seq", "fsdp"), None),
        P(("seq", "fsdp"), None),
        P(("seq", "fsdp")),
        P(("seq", "fsdp")),
        P(None, "seq"),
        P("seq"),
        P(None, "seq"),
        P(None, "seq"),
        P("seq"),
        P(),
    )
    return jax.shard_map(
        per_device, mesh=mesh, in_specs=in_specs, out_specs=out_specs, check_vma=False
    )
```

```python
import math
from functools import partial

import jax
import jax.numpy as jnp
import numpy as np
from jax import lax
from jax.experimental import pallas as pl
from jax.experimental.pallas import tpu as pltpu
from jax.sharding import PartitionSpec as P

NORM_EPS = 1e-06
RATE_SCALE = 8.0
LANES = 640
SUB = 8
TAPS = 4
UNROLL = 4
VMEM_LIMIT = 60 << 20


def gelu_tanh(values):
    return jax.nn.gelu(values, approximate=True)


def rms_norm(values, norm_gain):
    return (
        values * lax.rsqrt(jnp.mean(values * values, axis=-1, keepdims=True) + NORM_EPS) * norm_gain
    )


def gated_state(state_in, gate_pre):
    return state_in * gelu_tanh(gate_pre)


def mixing(first_pre, second_pre):
    return gelu_tanh(first_pre) * second_pre


def one_minus_exp_neg(u):
    series = jnp.ones_like(u)
    for k in range(9, 1, -1):
        series = 1.0 - u * (1.0 / k) * series
    return jnp.where(u < 0.5, u * series, 1.0 - jnp.exp(-u))


def logistic(values):
    return 1.0 / (1.0 + jnp.exp(-values))


def earlier_chunk(values, channels):
    rolled = pltpu.roll(values, 1, 0)
    wrapped = pltpu.roll(rolled, channels, 1) if channels < LANES else rolled
    sub = lax.broadcasted_iota(jnp.int32, values.shape, 0)
    lane = lax.broadcasted_iota(jnp.int32, values.shape, 1)
    shifted = jnp.where(sub == 0, wrapped, rolled)
    return jnp.where((sub == 0) & (lane < channels), 0.0, shifted)


def later_chunk(values, channels):
    rolled = pltpu.roll(values, SUB - 1, 0)
    wrapped = pltpu.roll(rolled, LANES - channels, 1) if channels < LANES else rolled
    sub = lax.broadcasted_iota(jnp.int32, values.shape, 0)
    lane = lax.broadcasted_iota(jnp.int32, values.shape, 1)
    shifted = jnp.where(sub == SUB - 1, wrapped, rolled)
    return jnp.where((sub == SUB - 1) & (lane >= LANES - channels), 0.0, shifted)


def place_rows(slot_ref, source, group, rows):
    here = slot_ref[source] - group * rows
    row = lax.broadcasted_iota(jnp.int32, (rows, here.shape[-1]), 0)
    return jnp.where(row == here, 1.0, 0.0).astype(jnp.bfloat16)


def into_order(data_ref, column_ref, spread_ref, wide_ref, ordered_ref, first_row):
    blocks, per_block, tokens = column_ref.shape
    channels = data_ref.shape[1]
    rows = wide_ref.shape[1]

    def spread(block, carry):
        columns = column_ref[block].T
        for k in range(per_block):
            spread_ref[block * per_block + k] = jnp.broadcast_to(columns[:, k : k + 1], (tokens, 128))
        return carry

    lax.fori_loop(0, blocks, spread, 0)
    for group in range(LANES // channels):

        def one_tile(tile, carry, group=group):
            start = group * rows + tile * tokens
            place = (lax.broadcasted_iota(jnp.int32, (tokens, tokens), 1) + start).astype(jnp.float32)

            def one_block(block, total):
                for k in range(per_block):
                    source = block * per_block + k
                    column = jnp.concatenate([spread_ref[source]] * (tokens // 128), axis=1)
                    here = jnp.where(column == place, 1.0, 0.0).astype(jnp.bfloat16)
                    total = total + jnp.dot(
                        data_ref[source], here, preferred_element_type=jnp.float32
                    )
                return total

            total = jnp.zeros((channels, tokens), jnp.float32)
            total = lax.fori_loop(0, blocks, one_block, total)
            at = pl.ds(pl.multiple_of(tile * tokens, tokens), tokens)
            wide_ref[group * channels : (group + 1) * channels, at] = total
            return carry

        lax.fori_loop(0, rows // tokens, one_tile, 0)
    for start in range(0, rows, 128):
        ordered_ref[first_row + start : first_row + start + 128, :] = wide_ref[
            :, start : start + 128
        ].T


def out_of_order(ordered_ref, slot_ref, narrow_ref, data_ref):
    sources, channels, tokens = data_ref.shape
    groups, _, rows = narrow_ref.shape
    for start in range(0, rows, 128):
        wide = ordered_ref[start : start + 128, :].T
        for group in range(groups):
            narrow_ref[group, :, start : start + 128] = wide[
                group * channels : (group + 1) * channels, :
            ].astype(jnp.bfloat16)

    def one_source(source, carry):
        total = jnp.zeros((channels, tokens), jnp.float32)
        for group in range(groups):
            total = total + jnp.dot(
                narrow_ref[group],
                place_rows(slot_ref, source, group, rows),
                preferred_element_type=jnp.float32,
            )
        data_ref[source] = total.astype(jnp.bfloat16)
        return carry

    lax.fori_loop(0, sources, one_source, 0)


def forward_kernel(
    data_ref, slot_ref, column_ref, offset_ref, params_ref,
    states_ref, inputs_out, filtered_out, decay_out, hidden_out,
    wide_ref, reach_ref, narrow_ref, spread_ref, inputs_ref, filtered_ref, decay_ref, hidden_ref, sems,
):
    channels = data_ref.shape[1]
    rows = hidden_ref.shape[0]
    pad = (TAPS - 1) * SUB
    into_order(data_ref, column_ref, spread_ref, wide_ref, inputs_ref, pad)
    for tap in range(TAPS - 1):
        inputs_ref[tap * SUB : (tap + 1) * SUB, :] = earlier_chunk(
            inputs_ref[rows + tap * SUB : rows + (tap + 1) * SUB, :], channels
        )
    param = [params_ref[k : k + 1, :] for k in range(TAPS + 6)]
    block = UNROLL * SUB

    def local_steps(step, carry):
        state, reach = carry
        start = pl.multiple_of(step * block, block)
        offset = offset_ref[pl.ds(start, block), :]
        filtered = param[TAPS] + param[0] * inputs_ref[pl.ds(start + pad, block), :]
        for tap in range(1, TAPS):
            delayed = inputs_ref[pl.ds(start + pad - tap * SUB, block), :]
            filtered = filtered + param[tap] * jnp.where(offset >= tap, delayed, 0.0)
        recur_gate = logistic(param[TAPS + 1] * filtered + param[TAPS + 3])
        input_gate = logistic(param[TAPS + 2] * filtered + param[TAPS + 4])
        rate = param[TAPS + 5] * recur_gate
        decay = jnp.where(offset > 0, jnp.exp(-rate), 0.0)
        drive = jnp.sqrt(one_minus_exp_neg(2.0 * rate)) * input_gate * filtered
        filtered_ref[pl.ds(start, block), :] = filtered
        decay_ref[pl.ds(start, block), :] = decay
        for k in range(UNROLL):
            now = decay[k * SUB : (k + 1) * SUB, :]
            state = now * state + drive[k * SUB : (k + 1) * SUB, :]
            reach = now * reach
            hidden_ref[pl.ds(start + k * SUB, SUB), :] = state
            reach_ref[pl.ds(start + k * SUB, SUB), :] = reach
        return state, reach

    zeros = jnp.zeros((SUB, LANES), jnp.float32)
    last, reach = lax.fori_loop(0, rows // block, local_steps, (zeros, zeros + 1.0))
    chunks = SUB * (LANES // channels)
    entry = lax.fori_loop(
        0, chunks - 1, lambda _, entry: earlier_chunk(last + reach * entry, channels), zeros
    )
    entries = jnp.concatenate([entry] * UNROLL, axis=0)

    def carry_over(step, carry):
        start = pl.multiple_of(step * block, block)
        hidden_ref[pl.ds(start, block), :] += reach_ref[pl.ds(start, block), :] * entries
        return carry

    pairs = ((inputs_ref, inputs_out), (filtered_ref, filtered_out), (decay_ref, decay_out))
    copies = [pltpu.make_async_copy(a, b, sems.at[k]) for k, (a, b) in enumerate(pairs)]
    for copy in copies:
        copy.start()
    lax.fori_loop(0, rows // block, carry_over, 0)
    copies.append(pltpu.make_async_copy(hidden_ref, hidden_out, sems.at[3]))
    copies[3].start()
    out_of_order(hidden_ref, slot_ref, narrow_ref, states_ref)
    for copy in copies:
        copy.wait()


def backward_kernel(
    data_ref, slot_ref, column_ref, offset_ref, params_ref, inputs_in, filtered_in, decay_in, hidden_in,
    grads_ref, sums_ref,
    wide_ref, back_ref, reach_ref, narrow_ref, filtered_grad_ref, later_offset_ref, spread_ref,
    inputs_ref, filtered_ref, decay_ref, hidden_ref, sems,
):
    channels = data_ref.shape[1]
    rows = hidden_ref.shape[0]
    pad = (TAPS - 1) * SUB
    pairs = (
        (inputs_in, inputs_ref),
        (filtered_in, filtered_ref),
        (decay_in, decay_ref),
        (hidden_in, hidden_ref),
    )
    copies = [pltpu.make_async_copy(a, b, sems.at[k]) for k, (a, b) in enumerate(pairs)]
    for copy in copies:
        copy.start()
    into_order(data_ref, column_ref, spread_ref, wide_ref, back_ref, 0)
    for copy in copies:
        copy.wait()
    param = [params_ref[k : k + 1, :] for k in range(TAPS + 6)]
    block = UNROLL * SUB
    count = rows // block

    def local_steps(step, carry):
        passed, reach = carry
        start = pl.multiple_of((count - 1 - step) * block, block)
        decay = decay_ref[pl.ds(start, block), :]
        given = back_ref[pl.ds(start, block), :]
        for k in range(UNROLL - 1, -1, -1):
            back = given[k * SUB : (k + 1) * SUB, :] + passed
            back_ref[pl.ds(start + k * SUB, SUB), :] = back
            reach_ref[pl.ds(start + k * SUB, SUB), :] = reach
            now = decay[k * SUB : (k + 1) * SUB, :]
            passed = now * back
            reach = now * reach
        return passed, reach

    zeros = jnp.zeros((SUB, LANES), jnp.float32)
    first, reach = lax.fori_loop(0, count, local_steps, (zeros, zeros + 1.0))
    chunks = SUB * (LANES // channels)
    entry = lax.fori_loop(
        0, chunks - 1, lambda _, entry: later_chunk(first + reach * entry, channels), zeros
    )
    entries = jnp.concatenate([entry] * UNROLL, axis=0)
    sums_ref[...] = jnp.zeros_like(sums_ref)
    before_first = earlier_chunk(hidden_ref[rows - SUB : rows, :], channels)

    def add_up(index, values):
        total = values[:SUB, :]
        for k in range(1, UNROLL):
            total = total + values[k * SUB : (k + 1) * SUB, :]
        sums_ref[index] += total

    def through_gates(step, before):
        start = pl.multiple_of(step * block, block)
        offset = offset_ref[pl.ds(start, block), :]
        filtered = filtered_ref[pl.ds(start, block), :]
        hidden = hidden_ref[pl.ds(start, block), :]
        earlier = jnp.concatenate([before, hidden[: block - SUB, :]], axis=0)
        back = back_ref[pl.ds(start, block), :] + reach_ref[pl.ds(start, block), :] * entries
        recur_gate = logistic(param[TAPS + 1] * filtered + param[TAPS + 3])
        input_gate = logistic(param[TAPS + 2] * filtered + param[TAPS + 4])
        rate = param[TAPS + 5] * recur_gate
        decay = decay_ref[pl.ds(start, block), :]
        squared = one_minus_exp_neg(2.0 * rate)
        scale_inv = lax.rsqrt(jnp.maximum(squared, 1e-37))
        scale = squared * scale_inv
        scale_grad = back * input_gate * filtered
        input_gate_grad = back * scale * filtered
        rate_grad = scale_grad * (1.0 - squared) * scale_inv - decay * back * earlier
        recur_pre_grad = rate_grad * param[TAPS + 5] * recur_gate * (1.0 - recur_gate)
        input_pre_grad = input_gate_grad * input_gate * (1.0 - input_gate)
        filtered_grad = (
            back * scale * input_gate
            + recur_pre_grad * param[TAPS + 1]
            + input_pre_grad * param[TAPS + 2]
        )
        filtered_grad_ref[pl.ds(start, block), :] = filtered_grad
        add_up(0, filtered_grad * inputs_ref[pl.ds(start + pad, block), :])
        for tap in range(1, TAPS):
            delayed = inputs_ref[pl.ds(start + pad - tap * SUB, block), :]
            add_up(tap, filtered_grad * jnp.where(offset >= tap, delayed, 0.0))
        add_up(TAPS, filtered_grad)
        add_up(TAPS + 1, recur_pre_grad * filtered)
        add_up(TAPS + 2, input_pre_grad * filtered)
        add_up(TAPS + 3, recur_pre_grad)
        add_up(TAPS + 4, input_pre_grad)
        add_up(TAPS + 5, rate_grad * recur_gate)
        return hidden[block - SUB :, :]

    lax.fori_loop(0, count, through_gates, before_first)
    for tap in range(TAPS - 1):
        rows_here = slice(tap * SUB, (tap + 1) * SUB)
        filtered_grad_ref[rows + tap * SUB : rows + (tap + 1) * SUB, :] = later_chunk(
            filtered_grad_ref[rows_here, :], channels
        )
        later_offset_ref[block + tap * SUB : block + (tap + 1) * SUB, :] = later_chunk(
            offset_ref[rows_here, :], channels
        )
    later_offset_ref[:block, :] = offset_ref[rows - block :, :]

    def through_taps(start, offsets_ref, offset_start):
        total = param[0] * filtered_grad_ref[pl.ds(start, block), :]
        for tap in range(1, TAPS):
            later = filtered_grad_ref[pl.ds(start + tap * SUB, block), :]
            offset = offsets_ref[pl.ds(offset_start + tap * SUB, block), :]
            total = total + param[tap] * jnp.where(offset >= tap, later, 0.0)
        back_ref[pl.ds(start, block), :] = total

    def inner_taps(step, carry):
        start = pl.multiple_of(step * block, block)
        through_taps(start, offset_ref, start)
        return carry

    lax.fori_loop(0, count - 1, inner_taps, 0)
    through_taps(rows - block, later_offset_ref, 0)
    out_of_order(back_ref, slot_ref, narrow_ref, grads_ref)


def shapes_of(data):
    sources, channels, tokens = data.shape
    rows = sources * tokens * channels // LANES
    return sources, channels, tokens, rows


def slot_columns(slot):
    sources, _, tokens = slot.shape
    per_block = math.gcd(sources, 16)
    return slot.reshape(sources // per_block, per_block, tokens).astype(jnp.float32)


def recurrence_forward(data, slot, offset, params):
    sources, channels, tokens, rows = shapes_of(data)
    whole = jax.ShapeDtypeStruct((rows, LANES), jnp.float32)
    padded = jax.ShapeDtypeStruct((rows + (TAPS - 1) * SUB, LANES), jnp.float32)
    count = sources * tokens
    return pl.pallas_call(
        forward_kernel,
        out_shape=(jax.ShapeDtypeStruct(data.shape, jnp.bfloat16), padded, whole, whole, whole),
        scratch_shapes=[
            pltpu.VMEM((LANES, rows), jnp.float32),
            pltpu.VMEM((rows, LANES), jnp.float32),
            pltpu.VMEM((LANES // channels, channels, rows), jnp.bfloat16),
            pltpu.VMEM((sources, tokens, 128), jnp.float32),
            pltpu.VMEM((rows + (TAPS - 1) * SUB, LANES), jnp.float32),
            pltpu.VMEM((rows, LANES), jnp.float32),
            pltpu.VMEM((rows, LANES), jnp.float32),
            pltpu.VMEM((rows, LANES), jnp.float32),
            pltpu.SemaphoreType.DMA((4,)),
        ],
        in_specs=[pl.BlockSpec(memory_space=pltpu.VMEM)] * 5,
        out_specs=(pl.BlockSpec(memory_space=pltpu.VMEM),)
        + (pl.BlockSpec(memory_space=pl.ANY),) * 4,
        compiler_params=pltpu.CompilerParams(vmem_limit_bytes=VMEM_LIMIT),
        cost_estimate=pl.CostEstimate(
            flops=0, bytes_accessed=0, transcendentals=0
        ),
        name="recurrence_forward",
    )(data, slot, slot_columns(slot), offset, params)


def recurrence_backward(data, slot, offset, params, inputs, filtered, decay, hidden):
    sources, channels, tokens, rows = shapes_of(data)
    count = sources * tokens
    return pl.pallas_call(
        backward_kernel,
        out_shape=(
            jax.ShapeDtypeStruct(data.shape, jnp.bfloat16),
            jax.ShapeDtypeStruct((TAPS + 6, SUB, LANES), jnp.float32),
        ),
        scratch_shapes=[
            pltpu.VMEM((LANES, rows), jnp.float32),
            pltpu.VMEM((rows, LANES), jnp.float32),
            pltpu.VMEM((rows, LANES), jnp.float32),
            pltpu.VMEM((LANES // channels, channels, rows), jnp.bfloat16),
            pltpu.VMEM((rows + (TAPS - 1) * SUB, LANES), jnp.float32),
            pltpu.VMEM((UNROLL * SUB + (TAPS - 1) * SUB, LANES), jnp.float32),
            pltpu.VMEM((sources, tokens, 128), jnp.float32),
            pltpu.VMEM((rows + (TAPS - 1) * SUB, LANES), jnp.float32),
            pltpu.VMEM((rows, LANES), jnp.float32),
            pltpu.VMEM((rows, LANES), jnp.float32),
            pltpu.VMEM((rows, LANES), jnp.float32),
            pltpu.SemaphoreType.DMA((4,)),
        ],
        in_specs=[pl.BlockSpec(memory_space=pltpu.VMEM)] * 5
        + [pl.BlockSpec(memory_space=pl.ANY)] * 4,
        compiler_params=pltpu.CompilerParams(vmem_limit_bytes=VMEM_LIMIT),
        cost_estimate=pl.CostEstimate(
            flops=0, bytes_accessed=0, transcendentals=0
        ),
        name="recurrence_backward",
    )(data, slot, slot_columns(slot), offset, params, inputs, filtered, decay, hidden)


def arrangement(lengths, permutation, sources, channels):
    total = permutation.shape[0]
    groups = LANES // channels
    rows = total // groups
    steps = rows // SUB
    chunk = permutation // steps
    slot = (chunk // SUB) * rows + (permutation % steps) * SUB + chunk % SUB
    seq_ends = jnp.cumsum(lengths)
    seq_starts = seq_ends - lengths
    row, lane = np.arange(rows), np.arange(LANES)
    of_row = jnp.asarray((row % SUB) * steps + row // SUB, jnp.int32)
    of_lane = jnp.asarray((lane // channels) * (SUB * steps), jnp.int32)
    position = of_row[:, None] + of_lane[None, :]
    seg_first = jnp.zeros_like(position)
    for k in range(lengths.shape[0]):
        start = seq_starts[k]
        seg_first = jnp.where(position >= start, start, seg_first)
    offset = jnp.minimum(position - seg_first, TAPS - 1).astype(jnp.float32)
    return slot.reshape(sources, 1, total // sources), offset


def lane_params(conv_weight, conv_bias, gate_weight, gate_bias, decay_logits):
    stacked = jnp.concatenate(
        [
            conv_weight,
            conv_bias[None],
            gate_weight,
            gate_bias,
            RATE_SCALE * jax.nn.softplus(-decay_logits)[None],
        ]
    )
    return jnp.tile(stacked, (1, LANES // stacked.shape[1]))


def channel_sums(sums, channels, decay_logits):
    sums = jnp.sum(sums, axis=1).reshape(TAPS + 6, LANES // channels, channels).sum(axis=1)
    logit = -RATE_SCALE * jax.nn.sigmoid(-decay_logits)[None] * sums[TAPS + 5 :]
    return jnp.concatenate([sums[: TAPS + 5], logit])


def swap_core(values):
    return lax.ppermute(values, "fsdp", [(0, 1), (1, 0)])


def swap_bit(values, bit):
    count = lax.axis_size("seq")
    return lax.ppermute(values, "seq", [(i, i ^ (1 << bit)) for i in range(count)])


def half(values, index, axis):
    size = values.shape[axis] // 2
    return lax.dynamic_slice_in_dim(values, index * size, size, axis)


def reorder_blocks(values, low_bit, high_bit, axis):
    width = high_bit - low_bit
    size = values.shape[axis] >> width
    pieces = []
    for place in range(1 << width):
        natural = sum(((place >> (width - 1 - k)) & 1) << k for k in range(width))
        pieces.append(lax.slice_in_dim(values, natural * size, (natural + 1) * size, axis=axis))
    return jnp.concatenate(pieces, axis=axis)


def trade_channels(values):
    return lax.all_to_all(values, "seq", split_axis=0, concat_axis=0, tiled=True)


def after(values, *earlier):
    return lax.optimization_barrier((values,) + earlier)[0]


def product(subscripts, left, right):
    return jnp.einsum(subscripts, left, right, preferred_element_type=jnp.float32)


class Links:
    def __init__(self, place, core):
        count = lax.axis_size("seq").bit_length() - 1
        self.core = core
        self.bits = [(place >> bit) & 1 for bit in range(count)]

    def own(self, link):
        return self.core if link == "core" else self.bits[link]

    def swap(self, link, values, *earlier):
        if earlier:
            values = after(values, *earlier)
        return swap_core(values) if link == "core" else swap_bit(values, link)


class Chain:
    def __init__(self, links, terms, sums, collects=(), turn=False, rider=None):
        self.links, self.terms, self.rider = links, list(terms), rider
        self.sums, self.collects, self.turn = list(sums), list(collects), turn
        self.send()

    def total(self):
        return sum(term.astype(jnp.float32) for term in self.terms)

    def send(self):
        if self.sums:
            self.link, self.axis = self.sums[0]
        elif self.collects:
            total = self.total()
            self.terms = [total.T if self.turn else total]
            self.turn = False
            self.link, self.axis = self.collects[0], 0
        else:
            return
        own_bit = self.links.own(self.link)
        sent = sum(half(term, 1 - own_bit, self.axis).astype(jnp.float32) for term in self.terms)
        self.sent = sent.astype(jnp.bfloat16)
        self.other = self.links.swap(self.link, self.sent)
        self.terms = [half(term, own_bit, self.axis) for term in self.terms]
        if self.rider is not None:
            self.rider_other = self.links.swap(self.link, self.rider)

    def advance(self, token):
        other = after(self.other, token)
        if self.rider is not None:
            self.rider = self.rider + after(self.rider_other, token)
        if self.sums:
            self.terms.append(other)
            self.sums.pop(0)
        else:
            own, other = self.terms[0], other.astype(jnp.float32)
            first = self.links.own(self.link) == 0
            low, high = jnp.where(first, own, other), jnp.where(first, other, own)
            self.terms = [jnp.concatenate([low, high], axis=1)]
            self.collects.pop(0)
        if not self.sums and not self.collects:
            return token
        self.send()
        return self.sent


def both_cores(values, *earlier):
    return lax.all_gather(after(values, *earlier) if earlier else values, "fsdp")


def pick(values, *index):
    for place in index:
        values = lax.dynamic_index_in_dim(values, place, 0, keepdims=False)
    return values


def largest_tile(size, most, step):
    return max(tile for tile in range(step, most + 1, step) if size % tile == 0)


def grad_kernel(count, turned, select_ref, *refs):
    per_piece = turned or 1
    lefts = [ref[...] for ref in refs[: count * per_piece]]
    rights = [ref[...] for ref in refs[count * per_piece : count * (per_piece + 1)]]
    rights = jnp.concatenate(rights, axis=0)
    if turned:
        if per_piece > 1:
            lefts = [
                jnp.concatenate(lefts[k * per_piece : (k + 1) * per_piece], axis=1)
                for k in range(count)
            ]
        total = lax.dot_general(
            jnp.concatenate(lefts, axis=0),
            rights,
            (((0,), (0,)), ((), ())),
            preferred_element_type=jnp.float32,
        )
    else:
        total = jnp.dot(
            jnp.concatenate(lefts, axis=1), rights, preferred_element_type=jnp.float32
        )
    for ref in refs[count * (per_piece + 1) : -1]:
        total = total + ref[...].astype(jnp.float32)
    refs[-1][...] = total.astype(jnp.bfloat16)


(CORE, OTHER_CORE), (X, OTHER_X), (Y, OTHER_Y), (LOW, OTHER_LOW), (TOP, OTHER_TOP) = (
    (("scalar", 2 * k), ("scalar", 2 * k + 1)) for k in range(5)
)


def grad_product(select, pieces, rows, row_half=None, added=None, columns=None, counted=False):
    cols = pieces[0][2].shape[-1]
    tile_rows = largest_tile(rows, 1024, 16) if columns is None else rows // columns[0]
    tile_cols = largest_tile(cols, 1024 if columns is None else 512, 256)

    def entry(index, select_ref):
        return select_ref[index[1]] if isinstance(index, tuple) else index

    def left_spec(left, lead):
        def place(m, n, select_ref):
            start = 0 if row_half is None else entry(row_half, select_ref) * (rows // tile_rows)
            return tuple(entry(i, select_ref) for i in lead) + (start + m, 0)

        return pl.BlockSpec((None,) * len(lead) + (tile_rows, left.shape[-1]), place)

    def column_spec(left, lead, which):
        def place(m, n, select_ref):
            block = columns[2](m, partial(entry, select_ref=select_ref))[which]
            return tuple(entry(i, select_ref) for i in lead) + (0, block)

        return pl.BlockSpec((None,) * len(lead) + (left.shape[-2], columns[1]), place)

    def right_spec(right, lead):
        def place(m, n, select_ref):
            return tuple(entry(i, select_ref) for i in lead) + (0, n)

        return pl.BlockSpec((None,) * len(lead) + (right.shape[-2], tile_cols), place)

    out_spec = pl.BlockSpec((tile_rows, tile_cols), lambda m, n, select_ref: (m, n))
    turned = 0 if columns is None else tile_rows // columns[1]
    if turned:
        in_specs = [column_spec(p[0], p[1], which) for p in pieces for which in range(turned)]
        operands = [p[0] for p in pieces for _ in range(turned)]
    else:
        in_specs = [left_spec(left, lead) for left, lead, _, _ in pieces]
        operands = [left for left, _, _, _ in pieces]
    in_specs += [right_spec(right, lead) for _, _, right, lead in pieces]
    operands += [right for _, _, right, _ in pieces]
    if added is not None:
        in_specs.append(out_spec)
        operands.append(added)
    return pl.pallas_call(
        partial(grad_kernel, len(pieces), turned),
        out_shape=jax.ShapeDtypeStruct((rows, cols), jnp.bfloat16),
        grid_spec=pltpu.PrefetchScalarGridSpec(
            num_scalar_prefetch=1,
            grid=(rows // tile_rows, cols // tile_cols),
            in_specs=in_specs,
            out_specs=out_spec,
        ),
        compiler_params=pltpu.CompilerParams(vmem_limit_bytes=VMEM_LIMIT),
        cost_estimate=pl.CostEstimate(
            flops=counted * 2 * rows * cols * sum(p[2].shape[-2] for p in pieces),
            bytes_accessed=counted * 2 * rows * cols,
            transcendentals=0,
        ),
        name="weight_grad",
    )(select, *operands)


GELU_SCALE = 0.7978845608028654
GELU_CUBE = 0.044715
HIDDEN_TILE = 512


def mlp_kernel(
    bits_ref, normed_ref, down_grad_ref, gate_ref, up_ref, down_ref,
    branch_ref, normed_grad_ref, mixed_ref, sent_gate_ref, sent_up_ref, kept_gate_ref, kept_up_ref,
):
    step = pl.program_id(0)
    by_columns = (((1,), (1,)), ((), ()))
    normed = normed_ref[...]
    first = jnp.dot(normed, gate_ref[...], preferred_element_type=jnp.float32)
    second = jnp.dot(normed, up_ref[...], preferred_element_type=jnp.float32)
    mixed_grad = lax.dot_general(
        down_grad_ref[...], down_ref[...], by_columns, preferred_element_type=jnp.float32
    )
    square = first * first
    bend = jnp.tanh(GELU_SCALE * first * (1.0 + GELU_CUBE * square))
    rise = 0.5 + 0.5 * bend
    gelu = first * rise
    slope = rise + 0.5 * GELU_SCALE * first * (1.0 - bend * bend) * (
        1.0 + 3.0 * GELU_CUBE * square
    )
    mixed = gelu * second
    first_low = (mixed_grad * slope * second).astype(jnp.bfloat16)
    second_low = (mixed_grad * gelu).astype(jnp.bfloat16)
    mixed_ref[...] = mixed.T.astype(jnp.bfloat16)

    side = (step // (pl.num_programs(0) // 4)) % 2
    for which, low, sent_ref, kept_ref in (
        (0, first_low, sent_gate_ref, kept_gate_ref),
        (1, second_low, sent_up_ref, kept_up_ref),
    ):

        @pl.when(side != bits_ref[which])
        def _(low=low, sent_ref=sent_ref):
            sent_ref[...] = low

        @pl.when(side == bits_ref[which])
        def _(low=low, kept_ref=kept_ref):
            kept_ref[...] = low

    @pl.when(step == 0)
    def _():
        branch_ref[...] = jnp.zeros_like(branch_ref)
        normed_grad_ref[...] = jnp.zeros_like(normed_grad_ref)

    branch_ref[...] += jnp.dot(
        mixed.astype(jnp.bfloat16), down_ref[...], preferred_element_type=jnp.float32
    )
    normed_grad_ref[...] += lax.dot_general(
        first_low, gate_ref[...], by_columns, preferred_element_type=jnp.float32
    ) + lax.dot_general(second_low, up_ref[...], by_columns, preferred_element_type=jnp.float32)


def mlp_both_ways(bits, normed, down_grad, w_gate, w_up, w_down):
    count, width = normed.shape
    hidden = w_gate.shape[1]
    steps = hidden // HIDDEN_TILE
    tiles = steps // 4

    whole = pl.BlockSpec((count, width), lambda t, bits_ref: (0, 0))
    column = pl.BlockSpec((width, HIDDEN_TILE), lambda t, bits_ref: (0, t))
    row = pl.BlockSpec((HIDDEN_TILE, width), lambda t, bits_ref: (t, 0))
    turned = pl.BlockSpec((HIDDEN_TILE, count), lambda t, bits_ref: (t, 0))

    def traded(which, kept):
        def place(t, bits_ref):
            wanted = bits_ref[which] if kept else 1 - bits_ref[which]
            side = (t // tiles) % 2
            resting = jnp.where(wanted == 0, tiles - 1, 0)
            return (t // (2 * tiles), 0, jnp.where(side == wanted, t % tiles, resting))

        return pl.BlockSpec((None, count, HIDDEN_TILE), place)

    summed = jax.ShapeDtypeStruct((count, width), jnp.float32)
    return pl.pallas_call(
        mlp_kernel,
        out_shape=(summed, summed, jax.ShapeDtypeStruct((hidden, count), jnp.bfloat16))
        + (jax.ShapeDtypeStruct((2, count, hidden // 4), jnp.bfloat16),) * 4,
        grid_spec=pltpu.PrefetchScalarGridSpec(
            num_scalar_prefetch=1,
            grid=(steps,),
            in_specs=[whole, whole, column, column, row],
            out_specs=[whole, whole, turned]
            + [traded(which, kept) for kept in (False, True) for which in (0, 1)],
        ),
        compiler_params=pltpu.CompilerParams(vmem_limit_bytes=VMEM_LIMIT),
        cost_estimate=pl.CostEstimate(flops=0, bytes_accessed=0, transcendentals=0),
        name="mlp_both_ways",
    )(jnp.stack(bits).astype(jnp.int32), normed, down_grad, w_gate, w_up, w_down)


MIDDLE_TILE = 512


def middle_kernel(
    core_ref, normed_grad_ref, middle_ref, cotangent_ref, gain_ref, output_ref, own_ref, other_ref,
    state_ref, pre_ref,
    middle_grad_ref, out_grad_ref, gain_grad_ref, state_grad_ref, gate_grad_ref, back_ref,
):
    by_columns = (((1,), (1,)), ((), ()))

    @pl.when(pl.program_id(0) == 0)
    def _():
        middle = middle_ref[...]
        normed_grad = normed_grad_ref[...]
        inverse = lax.rsqrt(jnp.mean(middle * middle, axis=1, keepdims=True) + NORM_EPS)
        scaled = normed_grad * gain_ref[...]
        lean = jnp.mean(scaled * middle, axis=1, keepdims=True)
        total = cotangent_ref[...] + inverse * scaled - middle * (inverse * inverse * inverse * lean)
        middle_grad_ref[...] = total
        out_grad_ref[...] = total.astype(jnp.bfloat16)
        gain_grad_ref[...] = jnp.sum(normed_grad * middle * inverse, axis=0, keepdims=True)
        back_ref[...] = jnp.zeros_like(back_ref)

    grad = lax.dot_general(
        output_ref[...], out_grad_ref[...], by_columns, preferred_element_type=jnp.float32
    )
    pre = pre_ref[...]
    square = pre * pre
    bend = jnp.tanh(GELU_SCALE * pre * (1.0 + GELU_CUBE * square))
    rise = 0.5 + 0.5 * bend
    slope = rise + 0.5 * GELU_SCALE * pre * (1.0 - bend * bend) * (1.0 + 3.0 * GELU_CUBE * square)
    state_grad_ref[...] = (grad * pre * rise).astype(jnp.bfloat16)
    gate_grad = (grad * state_ref[...].astype(jnp.float32) * slope).astype(jnp.bfloat16)
    gate_grad_ref[...] = gate_grad
    width = own_ref.shape[0]
    for ref, place in ((own_ref, core_ref[0]), (other_ref, 1 - core_ref[0])):
        columns = pl.ds(pl.multiple_of(place * width, width), width)
        back_ref[:, columns] += lax.dot_general(
            gate_grad, ref[...], (((0,), (1,)), ((), ())), preferred_element_type=jnp.float32
        )


def middle_backward(core, normed_grad, middle, cotangent, gain, w_output, own, other, states, pre):
    count, width = middle.shape
    channels = w_output.shape[0]
    whole = pl.BlockSpec((count, width), lambda t, core_ref: (0, 0))
    line = pl.BlockSpec((1, width), lambda t, core_ref: (0, 0))
    row = pl.BlockSpec((MIDDLE_TILE, width), lambda t, core_ref: (t, 0))
    column = pl.BlockSpec((width // 2, MIDDLE_TILE), lambda t, core_ref: (0, t))
    turned = pl.BlockSpec((MIDDLE_TILE, count), lambda t, core_ref: (t, 0))
    wide = jax.ShapeDtypeStruct((count, width), jnp.float32)
    low = jax.ShapeDtypeStruct((channels, count), jnp.bfloat16)
    return pl.pallas_call(
        middle_kernel,
        out_shape=(
            wide,
            jax.ShapeDtypeStruct((count, width), jnp.bfloat16),
            jax.ShapeDtypeStruct((1, width), jnp.float32),
            low,
            low,
            wide,
        ),
        grid_spec=pltpu.PrefetchScalarGridSpec(
            num_scalar_prefetch=1,
            grid=(channels // MIDDLE_TILE,),
            in_specs=[whole, whole, whole, line, row, column, column, turned, turned],
            out_specs=[whole, whole, line, turned, turned, whole],
        ),
        compiler_params=pltpu.CompilerParams(vmem_limit_bytes=VMEM_LIMIT),
        cost_estimate=pl.CostEstimate(flops=0, bytes_accessed=0, transcendentals=0),
        name="middle_backward",
    )(core.astype(jnp.int32).reshape(1), normed_grad, middle, cotangent, gain, w_output, own, other, states, pre)


class Traded:
    def __init__(self, links, channel_grad):
        channels, count = channel_grad.shape
        self.links = links
        self.mine = channel_grad.reshape(2, 2, channels // 4, count)
        self.by_core = links.swap("core", pick(self.mine, 1 - links.core))

    def trade_x(self, token):
        core, other = self.links.core, 1 - self.links.bits[0]
        self.by_core = after(self.by_core, token)
        sent = jnp.stack([pick(self.mine, core, other), pick(self.by_core, other)])
        self.by_x = self.links.swap(0, sent)
        return sent

    def grad(self, select, normed_pieces):
        lefts = [(self.mine, (CORE, X)), (self.by_core, (X,)), (self.by_x, (0,)), (self.by_x, (1,))]
        pieces = [left + right for left, right in zip(lefts, normed_pieces)]
        return grad_product(select, pieces, self.mine.shape[2])


def per_device(
    tokens,
    cotangent,
    gate_proj,
    input_proj,
    output_proj,
    mlp_gate,
    mlp_up,
    mlp_down,
    gain_a,
    gain_b,
    conv_weight,
    conv_bias,
    gate_weight,
    gate_bias,
    decay_logits,
    lengths,
    permutation,
):
    w_input, w_output, w_mlpgate, w_mlpup, w_down = (
        lax.all_gather(input_proj, "fsdp", axis=0, tiled=True),
        lax.all_gather(output_proj, "fsdp", axis=0, tiled=True),
        lax.all_gather(mlp_gate, "fsdp", axis=0, tiled=True),
        lax.all_gather(mlp_up, "fsdp", axis=0, tiled=True),
        lax.all_gather(mlp_down, "fsdp", axis=0, tiled=True),
    )
    core = lax.axis_index("fsdp")
    place = lax.axis_index("seq")
    links = Links(place, core)
    x, y = links.bits[0], links.bits[1]
    bit_count = len(links.bits)
    top = bit_count - 1
    low = links.bits[2]
    own_bits = (core, x, y, low, links.bits[top])
    select = jnp.stack([value for bit in own_bits for value in (bit, 1 - bit)]).astype(jnp.int32)
    channels = decay_logits.shape[0]
    count, width = tokens.shape
    block_shape = (lax.axis_size("seq"), channels, count)
    gains = jnp.stack([gain_a, gain_b])
    other_gains = links.swap("core", gains)
    full_gain_a, full_gain_b = jnp.where(
        core == 0,
        jnp.concatenate([gains, other_gains], axis=1),
        jnp.concatenate([other_gains, gains], axis=1),
    )
    other_input = links.swap("core", input_proj)
    other_gate = links.swap("core", gate_proj)
    normed_a, norm_back_a = jax.vjp(rms_norm, tokens, full_gain_a.astype(jnp.float32))
    normed_a_low = normed_a.astype(jnp.bfloat16)
    down_grad = cotangent.astype(jnp.bfloat16)
    input_pre = product("td,dr->rt", half(normed_a_low, core, 1), input_proj)
    input_pre = input_pre + product("td,dr->rt", half(normed_a_low, 1 - core, 1), other_input)
    input_low = input_pre.astype(jnp.bfloat16)
    channel_in = trade_channels(input_low)
    late_lengths, late_permutation = after((lengths, permutation), input_low)
    slot, offset = arrangement(late_lengths[0], late_permutation[0], block_shape[0], channels)
    params = lane_params(conv_weight, conv_bias, gate_weight, gate_bias, decay_logits)
    normed_late = after(normed_a_low, offset, slot, params)
    gate_pre = product("td,dr->rt", half(normed_late, core, 1), gate_proj)
    gate_pre = gate_pre + product("td,dr->rt", half(normed_late, 1 - core, 1), other_gate)
    normed_order = reorder_blocks(normed_a_low, 1, bit_count, 1)
    normed_core = both_cores(normed_order, channel_in)
    channel_in, gate_pre = lax.optimization_barrier((channel_in, gate_pre))
    down_y = links.swap(1, down_grad, channel_in)
    normed_x = links.swap(0, normed_order, channel_in)
    states, *kept = recurrence_forward(channel_in.reshape(block_shape), slot, offset, params)
    states = after(states, normed_x, down_y)
    state_tokens = trade_channels(states.reshape(input_pre.shape))
    normed_both = both_cores(normed_x, states)
    normed_pieces = [(normed_order, ()), (normed_core, (OTHER_CORE,))]
    normed_pieces += [(normed_x, ()), (normed_both, (OTHER_CORE,))]
    gated_low = gated_state(state_tokens.astype(jnp.float32), gate_pre).astype(jnp.bfloat16)
    branch_a = product("rt,rd->td", gated_low, w_output)
    middle = tokens + branch_a
    gain_b_wide = full_gain_b.astype(jnp.float32)
    normed_b_low = rms_norm(middle, gain_b_wide).astype(jnp.bfloat16)
    rows_total = gated_low.shape[0]
    shape = (2,) * bit_count + (2, rows_total // (2 << bit_count), count)
    rest = tuple(range(bit_count - 3, -1, -1))
    out_order = (2, 0, 1, *range(3, bit_count))
    dims = (bit_count, *(top - bit for bit in out_order), bit_count + 1, bit_count + 2)
    shape_out, dims_out = shape, dims
    fars = [links.swap(bit, normed_b_low) for bit in (0, 2)]
    down_top = links.swap(top, after(down_grad, normed_b_low))
    mlp_parts = mlp_both_ways((x, low), normed_b_low, down_grad, w_mlpgate, w_mlpup, w_down)
    arrived = lax.optimization_barrier((*mlp_parts, down_top, *fars))
    branch_b, normed_b_grad, mixed, sent_gate, sent_up, kept_gate, kept_up = arrived[:7]
    down_top, *fars = arrived[7:]
    hidden_far = [links.swap(0, sent_gate), links.swap(2, sent_up)]
    high = mixed.reshape((1 << (bit_count - 2), 2, mixed.shape[0] >> (bit_count - 1), count))
    mixed_send = lax.dynamic_index_in_dim(high, 1 - y, 1, keepdims=False)
    mixed_y = links.swap(1, mixed_send)
    output = middle + branch_b
    sums = jnp.stack(
        (
            jnp.sum(tokens * tokens),
            jnp.sum(branch_a * branch_a),
            jnp.sum(middle * middle),
            jnp.sum(branch_b * branch_b),
        )
    )
    entry_total = tokens.shape[0] * tokens.shape[1] * lax.axis_size("seq") * lax.axis_size("fsdp")
    middle_grad, out_grad_low, gain_b_grad, state_low, gate_low, gate_part = middle_backward(
        core,
        normed_b_grad,
        middle,
        cotangent,
        gain_b_wide[None],
        w_output,
        gate_proj,
        other_gate,
        state_tokens,
        gate_pre,
    )
    arrived = lax.optimization_barrier((state_low, gate_low, out_grad_low, *hidden_far, mixed_y))
    state_low, gate_low, out_grad_low, *hidden_far, mixed_y = arrived
    block = mixed.shape[0] // (2 << bit_count)
    axes = [top - bit for bit in (1, top)] + [bit_count] + [top - bit for bit in (0, *range(2, top))]
    mixed_mine = after(mixed, state_low).reshape((2,) * bit_count + (2, block, count))
    mixed_mine = mixed_mine.transpose(axes + [bit_count + 1, bit_count + 2])
    mixed_mine = mixed_mine.reshape(2, 2, 2, mixed.shape[0] // 8, count)
    axes = [0, bit_count - 1, bit_count - 2] + [top - bit for bit in range(2, top)]
    mixed_y = mixed_y.reshape((2,) * bit_count + (block, count))
    mixed_y = mixed_y.transpose(axes + [bit_count, bit_count + 1])
    mixed_y = mixed_y.reshape(2, 2, mixed.shape[0] // 8, count)
    gain_b_grad = gain_b_grad[0]
    channel_grad = trade_channels(state_low)

    normed_b_core = both_cores(normed_b_low)
    hidden_pieces = []
    for index in (0, 1):
        mine, far = (kept_gate, kept_up)[index], hidden_far[index]
        far_core = both_cores(fars[index], mixed_send)
        both = jnp.stack([pick(mine, 1 - core), pick(after(far, state_low), 1 - core)])
        by_core = links.swap("core", both)
        hidden_pieces.append(
            [
                (normed_b_low, (), mine, (CORE,)),
                (fars[index], (), far, (CORE,)),
                (normed_b_core, (OTHER_CORE,), by_core, (0,)),
                (far_core, (OTHER_CORE,), by_core, (1,)),
            ]
        )
    aligned = (width >> bit_count) % 128 == 0
    hidden_orders = ((1, (*range(2, bit_count),), 0), (0, (1, *range(3, bit_count)), 2))
    if not aligned:
        for pieces, (summed, between, traded_bit) in zip(hidden_pieces, hidden_orders):
            for k, (left, lead, right, right_lead) in enumerate(pieces):
                split = left.reshape(left.shape[:-1] + (2,) * bit_count + (width >> bit_count,))
                first = left.ndim - 1
                axes = [first + top - bit for bit in (summed, *between, traded_bit)]
                axes = tuple(range(first)) + tuple(axes) + (first + bit_count,)
                split = split.transpose(axes).reshape(left.shape)
                pieces[k] = (jnp.swapaxes(split, -1, -2), lead, right, right_lead)

    def hidden_product(index, half_rows, token, added=None, counted=False):
        chosen = after(select, token)
        if not aligned:
            return grad_product(chosen, hidden_pieces[index], width // 2, half_rows, added)
        summed, between, traded_bit = hidden_orders[index]

        def blocks(m, entry):
            found = []
            for tile in range(1 << len(between)):
                place = entry(half_rows) << summed
                for k, bit in enumerate(reversed(between)):
                    place = place + (((tile >> k) & 1) << bit)
                found += [place >> 1] if traded_bit == 0 else [place, place + (1 << traded_bit)]
            return found

        columns = (1, width >> (bit_count - (traded_bit == 0)), blocks)
        return grad_product(chosen, hidden_pieces[index], width // 2, None, added, columns, counted)

    rest_bits = range(2, bit_count)
    mixed_two = jnp.stack(
        [pick(mixed_mine, y, 1 - own_bits[4]), pick(mixed_y, 1 - own_bits[4])]
    )
    down_both = links.swap(1, down_top, state_low)
    down_pieces = [(piece, ()) for piece in (down_grad, down_y, down_top, down_both)]
    gate_traded = Traded(links, gate_low)
    gated_mine = after(gated_low, state_low).reshape(shape_out).transpose(dims_out)
    gated_mine = gated_mine.reshape(2, 2, rows_total // 4, count)
    gated_core = links.swap("core", pick(gated_mine, 1 - core))
    gated_two = jnp.stack([pick(gated_mine, core, 1 - low), pick(gated_core, 1 - low)])
    gate_sent = hidden_product(0, OTHER_Y, gated_two, None, True)
    up_sent = hidden_product(1, OTHER_X, gate_sent, None, True)
    channel_grad = after(channel_grad, mixed_two, up_sent, gate_traded.by_core, down_both)
    gate_received = links.swap(1, gate_sent, channel_grad)
    up_received = links.swap(0, up_sent, channel_grad)
    mixed_far = links.swap(top, mixed_two, channel_grad)
    out_far = links.swap(2, out_grad_low, channel_grad)
    channel_grad = after(channel_grad, up_sent)

    dealt_grad, lane_sums = recurrence_backward(
        channel_grad.reshape(block_shape), slot, offset, params, *kept
    )
    dealt_grad = after(dealt_grad, out_far)
    input_grad = trade_channels(dealt_grad.reshape(state_low.shape))
    def down_product(chosen, token, added=None):
        lefts = [(mixed_mine, (Y, TOP, chosen)), (mixed_y, (TOP, chosen))]
        lefts += [(mixed_far, (k, chosen)) for k in range(2)]
        pieces = [left + right for left, right in zip(lefts, down_pieces)]
        return grad_product(after(select, token), pieces, mixed.shape[0] // 8, None, added)

    hidden_sums = [(bit, 0) for bit in rest_bits]
    projection_sums = [(bit, 1) for bit in range(1, bit_count)]
    token = after(dealt_grad, gate_received, up_received, mixed_far)
    gate_total = hidden_product(0, Y, token, gate_received)
    gated_far = links.swap(2, gated_two, gate_total)
    token = gate_traded.trade_x(gate_total)
    gate_chain = Chain(links, [gate_total], hidden_sums, (0, "core"))
    up_total = hidden_product(1, X, token, up_received)
    up_sums = [(bit, 0) for bit in (1, *range(3, bit_count))]
    up_chain = Chain(links, [up_total], up_sums, (2, "core"))
    down_sent = down_product(OTHER_CORE, up_total)
    down_received = links.swap("core", down_sent)
    input_grad = after(input_grad, down_sent)
    input_traded = Traded(links, input_grad)
    token = input_traded.trade_x(input_grad)
    out_core = both_cores(out_grad_low, dealt_grad)
    out_both = both_cores(out_far, dealt_grad)
    out_pieces = [
        (gated_mine, (CORE, LOW), out_grad_low, ()),
        (gated_core, (LOW,), out_core, (OTHER_CORE,)),
        (gated_far, (0,), out_far, ()),
        (gated_far, (1,), out_both, (OTHER_CORE,)),
    ]
    down_total = down_product(CORE, token, down_received)
    input_total = input_traded.grad(after(select, down_total), normed_pieces)
    input_chain = Chain(links, [input_total], projection_sums, (0, "core"), True)
    down_total = after(down_total, input_chain.sent)
    down_chain = Chain(links, [down_total], [(bit, 0) for bit in (0, *range(2, top))])
    token = gate_chain.advance(down_chain.sent)
    token = up_chain.advance(token)
    input_grad = after(input_grad, token)
    normed_a_grad = gate_part + product("rt,dr->td", input_grad, w_input)
    token_norm_grad, gain_a_grad = norm_back_a(normed_a_grad)
    token_grad = middle_grad + token_norm_grad
    small = jnp.concatenate([gain_a_grad, gain_b_grad, sums])
    gate_proj_total = gate_traded.grad(after(select, token_grad), normed_pieces)
    token = input_chain.advance(gate_proj_total)
    gate_proj_total = after(gate_proj_total, token)
    gate_proj = Chain(links, [gate_proj_total], projection_sums, (0, "core"), True, small)
    out_sent = grad_product(after(select, gate_proj.sent), out_pieces, rows_total // 8, OTHER_X)
    token = down_chain.advance(out_sent)
    out_received = links.swap(0, out_sent, token)
    token = input_chain.advance(token)
    token = gate_chain.advance(token)
    token = gate_proj.advance(token)
    token = up_chain.advance(token)
    token = input_chain.advance(token)
    out_total = grad_product(after(select, token), out_pieces, rows_total // 8, X, out_received)
    out_chain = Chain(links, [out_total], up_sums)
    token = gate_proj.advance(out_total)
    chains = [gate_chain, down_chain, input_chain, out_chain, gate_proj, up_chain]
    while any(chain.sums or chain.collects for chain in chains):
        for chain in chains:
            if chain.sums or chain.collects:
                token = chain.advance(token)
    param_sums = channel_sums(lane_sums, channels, decay_logits)
    param_sums = param_sums + links.swap("core", after(param_sums, up_sent))
    totals = gate_proj.rider
    gain_size = width // (lax.axis_size("seq") * lax.axis_size("fsdp"))
    gain_start = (place * lax.axis_size("fsdp") + core) * gain_size
    return (
        output,
        token_grad,
        gate_proj.total(),
        input_chain.total(),
        out_chain.total(),
        gate_chain.total(),
        up_chain.total(),
        down_chain.total(),
        lax.dynamic_slice_in_dim(totals, gain_start, gain_size, 0),
        lax.dynamic_slice_in_dim(totals, width + gain_start, gain_size, 0),
        param_sums[:TAPS],
        param_sums[TAPS],
        param_sums[TAPS + 1 : TAPS + 3],
        param_sums[TAPS + 3 : TAPS + 5],
        param_sums[TAPS + 5],
        jnp.sqrt(totals[2 * width :] / entry_total),
    )


def solution(mesh):
    in_specs = (
        P(("seq", "fsdp"), None),
        P(("seq", "fsdp"), None),
        P("fsdp", None),
        P("fsdp", None),
        P("fsdp", None),
        P("fsdp", None),
        P("fsdp", None),
        P("fsdp", None),
        P("fsdp"),
        P("fsdp"),
        P(None, "seq"),
        P("seq"),
        P(None, "seq"),
        P(None, "seq"),
        P("seq"),
        P("fsdp", None),
        P("fsdp", None),
    )
    out_specs = (
        P(("seq", "fsdp"), None),
        P(("seq", "fsdp"), None),
        P(("seq", "fsdp"), None),
        P(("seq", "fsdp"), None),
        P(("seq", "fsdp"), None),
        P(("seq", "fsdp"), None),
        P(("seq", "fsdp"), None),
        P(("seq", "fsdp"), None),
        P(("seq", "fsdp")),
        P(("seq", "fsdp")),
        P(None, "seq"),
        P("seq"),
        P(None, "seq"),
        P(None, "seq"),
        P("seq"),
        P(),
    )
    return jax.shard_map(
        per_device, mesh=mesh, in_specs=in_specs, out_specs=out_specs, check_vma=False
    )
```

```python
import math
from functools import partial

import jax
import jax.numpy as jnp
import numpy as np
from jax import lax
from jax.experimental import pallas as pl
from jax.experimental.pallas import tpu as pltpu
from jax.sharding import PartitionSpec as P

NORM_EPS = 1e-06
RATE_SCALE = 8.0
LANES = 640
SUB = 8
TAPS = 4
UNROLL = 8
VMEM_LIMIT = 60 << 20


def gelu_tanh(values):
    return jax.nn.gelu(values, approximate=True)


def rms_norm(values, norm_gain):
    return (
        values * lax.rsqrt(jnp.mean(values * values, axis=-1, keepdims=True) + NORM_EPS) * norm_gain
    )


def gated_state(state_in, gate_pre):
    return state_in * gelu_tanh(gate_pre)


def mixing(first_pre, second_pre):
    return gelu_tanh(first_pre) * second_pre


def one_minus_exp_neg(u):
    series = jnp.ones_like(u)
    for k in range(9, 1, -1):
        series = 1.0 - u * (1.0 / k) * series
    return jnp.where(u < 0.5, u * series, 1.0 - jnp.exp(-u))


def logistic(values):
    return 1.0 / (1.0 + jnp.exp(-values))


def earlier_chunk(values, channels):
    rolled = pltpu.roll(values, 1, 0)
    wrapped = pltpu.roll(rolled, channels, 1) if channels < LANES else rolled
    sub = lax.broadcasted_iota(jnp.int32, values.shape, 0)
    lane = lax.broadcasted_iota(jnp.int32, values.shape, 1)
    shifted = jnp.where(sub == 0, wrapped, rolled)
    return jnp.where((sub == 0) & (lane < channels), 0.0, shifted)


def later_chunk(values, channels):
    rolled = pltpu.roll(values, SUB - 1, 0)
    wrapped = pltpu.roll(rolled, LANES - channels, 1) if channels < LANES else rolled
    sub = lax.broadcasted_iota(jnp.int32, values.shape, 0)
    lane = lax.broadcasted_iota(jnp.int32, values.shape, 1)
    shifted = jnp.where(sub == SUB - 1, wrapped, rolled)
    return jnp.where((sub == SUB - 1) & (lane >= LANES - channels), 0.0, shifted)


def place_rows(slot_ref, source, group, rows):
    here = slot_ref[source] - group * rows
    row = lax.broadcasted_iota(jnp.int32, (rows, here.shape[-1]), 0)
    return jnp.where(row == here, 1.0, 0.0).astype(jnp.bfloat16)


def into_order(data_ref, column_ref, spread_ref, wide_ref, ordered_ref, first_row):
    blocks, per_block, tokens = column_ref.shape
    channels = data_ref.shape[1]
    rows = wide_ref.shape[1]

    def spread(block, carry):
        columns = column_ref[block].T
        for k in range(per_block):
            spread_ref[block * per_block + k] = jnp.broadcast_to(columns[:, k : k + 1], (tokens, 128))
        return carry

    lax.fori_loop(0, blocks, spread, 0)
    for group in range(LANES // channels):

        def one_tile(tile, carry, group=group):
            start = group * rows + tile * tokens
            place = (lax.broadcasted_iota(jnp.int32, (tokens, tokens), 1) + start).astype(jnp.float32)

            def one_block(block, total):
                for k in range(per_block):
                    source = block * per_block + k
                    column = jnp.concatenate([spread_ref[source]] * (tokens // 128), axis=1)
                    here = jnp.where(column == place, 1.0, 0.0).astype(jnp.bfloat16)
                    total = total + jnp.dot(
                        data_ref[source], here, preferred_element_type=jnp.float32
                    )
                return total

            total = jnp.zeros((channels, tokens), jnp.float32)
            total = lax.fori_loop(0, blocks, one_block, total)
            at = pl.ds(pl.multiple_of(tile * tokens, tokens), tokens)
            wide_ref[group * channels : (group + 1) * channels, at] = total
            return carry

        lax.fori_loop(0, rows // tokens, one_tile, 0)
    for start in range(0, rows, 128):
        ordered_ref[first_row + start : first_row + start + 128, :] = wide_ref[
            :, start : start + 128
        ].T


def out_of_order(ordered_ref, slot_ref, narrow_ref, data_ref):
    sources, channels, tokens = data_ref.shape
    groups, _, rows = narrow_ref.shape
    for start in range(0, rows, 128):
        wide = ordered_ref[start : start + 128, :].T
        for group in range(groups):
            narrow_ref[group, :, start : start + 128] = wide[
                group * channels : (group + 1) * channels, :
            ].astype(jnp.bfloat16)

    def one_source(source, carry):
        total = jnp.zeros((channels, tokens), jnp.float32)
        for group in range(groups):
            total = total + jnp.dot(
                narrow_ref[group],
                place_rows(slot_ref, source, group, rows),
                preferred_element_type=jnp.float32,
            )
        data_ref[source] = total.astype(jnp.bfloat16)
        return carry

    lax.fori_loop(0, sources, one_source, 0)


def forward_kernel(
    data_ref, slot_ref, column_ref, offset_ref, params_ref,
    states_ref, inputs_out, filtered_out, decay_out, hidden_out,
    wide_ref, reach_ref, narrow_ref, spread_ref, inputs_ref, filtered_ref, decay_ref, hidden_ref, sems,
):
    channels = data_ref.shape[1]
    rows = hidden_ref.shape[0]
    pad = (TAPS - 1) * SUB
    into_order(data_ref, column_ref, spread_ref, wide_ref, inputs_ref, pad)
    for tap in range(TAPS - 1):
        inputs_ref[tap * SUB : (tap + 1) * SUB, :] = earlier_chunk(
            inputs_ref[rows + tap * SUB : rows + (tap + 1) * SUB, :], channels
        )
    param = [params_ref[k : k + 1, :] for k in range(TAPS + 6)]
    block = UNROLL * SUB

    def local_steps(step, carry):
        state, reach = carry
        start = pl.multiple_of(step * block, block)
        offset = offset_ref[pl.ds(start, block), :]
        filtered = param[TAPS] + param[0] * inputs_ref[pl.ds(start + pad, block), :]
        for tap in range(1, TAPS):
            delayed = inputs_ref[pl.ds(start + pad - tap * SUB, block), :]
            filtered = filtered + param[tap] * jnp.where(offset >= tap, delayed, 0.0)
        recur_gate = logistic(param[TAPS + 1] * filtered + param[TAPS + 3])
        input_gate = logistic(param[TAPS + 2] * filtered + param[TAPS + 4])
        rate = param[TAPS + 5] * recur_gate
        decay = jnp.where(offset > 0, jnp.exp(-rate), 0.0)
        drive = jnp.sqrt(one_minus_exp_neg(2.0 * rate)) * input_gate * filtered
        filtered_ref[pl.ds(start, block), :] = filtered
        decay_ref[pl.ds(start, block), :] = decay
        for k in range(UNROLL):
            now = decay[k * SUB : (k + 1) * SUB, :]
            state = now * state + drive[k * SUB : (k + 1) * SUB, :]
            reach = now * reach
            hidden_ref[pl.ds(start + k * SUB, SUB), :] = state
            reach_ref[pl.ds(start + k * SUB, SUB), :] = reach
        return state, reach

    zeros = jnp.zeros((SUB, LANES), jnp.float32)
    last, reach = lax.fori_loop(0, rows // block, local_steps, (zeros, zeros + 1.0))
    chunks = SUB * (LANES // channels)
    entry = lax.fori_loop(
        0, chunks - 1, lambda _, entry: earlier_chunk(last + reach * entry, channels), zeros
    )
    entries = jnp.concatenate([entry] * UNROLL, axis=0)

    def carry_over(step, carry):
        start = pl.multiple_of(step * block, block)
        hidden_ref[pl.ds(start, block), :] += reach_ref[pl.ds(start, block), :] * entries
        return carry

    pairs = ((inputs_ref, inputs_out), (filtered_ref, filtered_out), (decay_ref, decay_out))
    copies = [pltpu.make_async_copy(a, b, sems.at[k]) for k, (a, b) in enumerate(pairs)]
    for copy in copies:
        copy.start()
    lax.fori_loop(0, rows // block, carry_over, 0)
    copies.append(pltpu.make_async_copy(hidden_ref, hidden_out, sems.at[3]))
    copies[3].start()
    out_of_order(hidden_ref, slot_ref, narrow_ref, states_ref)
    for copy in copies:
        copy.wait()


def backward_kernel(
    data_ref, slot_ref, column_ref, offset_ref, params_ref, inputs_in, filtered_in, decay_in, hidden_in,
    grads_ref, sums_ref,
    wide_ref, back_ref, reach_ref, narrow_ref, filtered_grad_ref, later_offset_ref, spread_ref,
    inputs_ref, filtered_ref, decay_ref, hidden_ref, sems,
):
    channels = data_ref.shape[1]
    rows = hidden_ref.shape[0]
    pad = (TAPS - 1) * SUB
    pairs = (
        (inputs_in, inputs_ref),
        (filtered_in, filtered_ref),
        (decay_in, decay_ref),
        (hidden_in, hidden_ref),
    )
    copies = [pltpu.make_async_copy(a, b, sems.at[k]) for k, (a, b) in enumerate(pairs)]
    for copy in copies:
        copy.start()
    into_order(data_ref, column_ref, spread_ref, wide_ref, back_ref, 0)
    for copy in copies:
        copy.wait()
    param = [params_ref[k : k + 1, :] for k in range(TAPS + 6)]
    block = UNROLL * SUB
    count = rows // block

    def local_steps(step, carry):
        passed, reach = carry
        start = pl.multiple_of((count - 1 - step) * block, block)
        decay = decay_ref[pl.ds(start, block), :]
        given = back_ref[pl.ds(start, block), :]
        for k in range(UNROLL - 1, -1, -1):
            back = given[k * SUB : (k + 1) * SUB, :] + passed
            back_ref[pl.ds(start + k * SUB, SUB), :] = back
            reach_ref[pl.ds(start + k * SUB, SUB), :] = reach
            now = decay[k * SUB : (k + 1) * SUB, :]
            passed = now * back
            reach = now * reach
        return passed, reach

    zeros = jnp.zeros((SUB, LANES), jnp.float32)
    first, reach = lax.fori_loop(0, count, local_steps, (zeros, zeros + 1.0))
    chunks = SUB * (LANES // channels)
    entry = lax.fori_loop(
        0, chunks - 1, lambda _, entry: later_chunk(first + reach * entry, channels), zeros
    )
    entries = jnp.concatenate([entry] * UNROLL, axis=0)
    sums_ref[...] = jnp.zeros_like(sums_ref)
    before_first = earlier_chunk(hidden_ref[rows - SUB : rows, :], channels)

    def add_up(index, values):
        total = values[:SUB, :]
        for k in range(1, UNROLL):
            total = total + values[k * SUB : (k + 1) * SUB, :]
        sums_ref[index] += total

    def through_gates(step, before):
        start = pl.multiple_of(step * block, block)
        offset = offset_ref[pl.ds(start, block), :]
        filtered = filtered_ref[pl.ds(start, block), :]
        hidden = hidden_ref[pl.ds(start, block), :]
        earlier = jnp.concatenate([before, hidden[: block - SUB, :]], axis=0)
        back = back_ref[pl.ds(start, block), :] + reach_ref[pl.ds(start, block), :] * entries
        recur_gate = logistic(param[TAPS + 1] * filtered + param[TAPS + 3])
        input_gate = logistic(param[TAPS + 2] * filtered + param[TAPS + 4])
        rate = param[TAPS + 5] * recur_gate
        decay = decay_ref[pl.ds(start, block), :]
        squared = one_minus_exp_neg(2.0 * rate)
        scale_inv = lax.rsqrt(jnp.maximum(squared, 1e-37))
        scale = squared * scale_inv
        scale_grad = back * input_gate * filtered
        input_gate_grad = back * scale * filtered
        rate_grad = scale_grad * (1.0 - squared) * scale_inv - decay * back * earlier
        recur_pre_grad = rate_grad * param[TAPS + 5] * recur_gate * (1.0 - recur_gate)
        input_pre_grad = input_gate_grad * input_gate * (1.0 - input_gate)
        filtered_grad = (
            back * scale * input_gate
            + recur_pre_grad * param[TAPS + 1]
            + input_pre_grad * param[TAPS + 2]
        )
        filtered_grad_ref[pl.ds(start, block), :] = filtered_grad
        add_up(0, filtered_grad * inputs_ref[pl.ds(start + pad, block), :])
        for tap in range(1, TAPS):
            delayed = inputs_ref[pl.ds(start + pad - tap * SUB, block), :]
            add_up(tap, filtered_grad * jnp.where(offset >= tap, delayed, 0.0))
        add_up(TAPS, filtered_grad)
        add_up(TAPS + 1, recur_pre_grad * filtered)
        add_up(TAPS + 2, input_pre_grad * filtered)
        add_up(TAPS + 3, recur_pre_grad)
        add_up(TAPS + 4, input_pre_grad)
        add_up(TAPS + 5, rate_grad * recur_gate)
        return hidden[block - SUB :, :]

    lax.fori_loop(0, count, through_gates, before_first)
    for tap in range(TAPS - 1):
        rows_here = slice(tap * SUB, (tap + 1) * SUB)
        filtered_grad_ref[rows + tap * SUB : rows + (tap + 1) * SUB, :] = later_chunk(
            filtered_grad_ref[rows_here, :], channels
        )
        later_offset_ref[block + tap * SUB : block + (tap + 1) * SUB, :] = later_chunk(
            offset_ref[rows_here, :], channels
        )
    later_offset_ref[:block, :] = offset_ref[rows - block :, :]

    def through_taps(start, offsets_ref, offset_start):
        total = param[0] * filtered_grad_ref[pl.ds(start, block), :]
        for tap in range(1, TAPS):
            later = filtered_grad_ref[pl.ds(start + tap * SUB, block), :]
            offset = offsets_ref[pl.ds(offset_start + tap * SUB, block), :]
            total = total + param[tap] * jnp.where(offset >= tap, later, 0.0)
        back_ref[pl.ds(start, block), :] = total

    def inner_taps(step, carry):
        start = pl.multiple_of(step * block, block)
        through_taps(start, offset_ref, start)
        return carry

    lax.fori_loop(0, count - 1, inner_taps, 0)
    through_taps(rows - block, later_offset_ref, 0)
    out_of_order(back_ref, slot_ref, narrow_ref, grads_ref)


def shapes_of(data):
    sources, channels, tokens = data.shape
    rows = sources * tokens * channels // LANES
    return sources, channels, tokens, rows


def slot_columns(slot):
    sources, _, tokens = slot.shape
    per_block = math.gcd(sources, 16)
    return slot.reshape(sources // per_block, per_block, tokens).astype(jnp.float32)


def recurrence_forward(data, slot, offset, params):
    sources, channels, tokens, rows = shapes_of(data)
    whole = jax.ShapeDtypeStruct((rows, LANES), jnp.float32)
    padded = jax.ShapeDtypeStruct((rows + (TAPS - 1) * SUB, LANES), jnp.float32)
    count = sources * tokens
    return pl.pallas_call(
        forward_kernel,
        out_shape=(jax.ShapeDtypeStruct(data.shape, jnp.bfloat16), padded, whole, whole, whole),
        scratch_shapes=[
            pltpu.VMEM((LANES, rows), jnp.float32),
            pltpu.VMEM((rows, LANES), jnp.float32),
            pltpu.VMEM((LANES // channels, channels, rows), jnp.bfloat16),
            pltpu.VMEM((sources, tokens, 128), jnp.float32),
            pltpu.VMEM((rows + (TAPS - 1) * SUB, LANES), jnp.float32),
            pltpu.VMEM((rows, LANES), jnp.float32),
            pltpu.VMEM((rows, LANES), jnp.float32),
            pltpu.VMEM((rows, LANES), jnp.float32),
            pltpu.SemaphoreType.DMA((4,)),
        ],
        in_specs=[pl.BlockSpec(memory_space=pltpu.VMEM)] * 5,
        out_specs=(pl.BlockSpec(memory_space=pltpu.VMEM),)
        + (pl.BlockSpec(memory_space=pl.ANY),) * 4,
        compiler_params=pltpu.CompilerParams(vmem_limit_bytes=VMEM_LIMIT),
        cost_estimate=pl.CostEstimate(
            flops=0, bytes_accessed=0, transcendentals=0
        ),
        name="recurrence_forward",
    )(data, slot, slot_columns(slot), offset, params)


def recurrence_backward(data, slot, offset, params, inputs, filtered, decay, hidden):
    sources, channels, tokens, rows = shapes_of(data)
    count = sources * tokens
    return pl.pallas_call(
        backward_kernel,
        out_shape=(
            jax.ShapeDtypeStruct(data.shape, jnp.bfloat16),
            jax.ShapeDtypeStruct((TAPS + 6, SUB, LANES), jnp.float32),
        ),
        scratch_shapes=[
            pltpu.VMEM((LANES, rows), jnp.float32),
            pltpu.VMEM((rows, LANES), jnp.float32),
            pltpu.VMEM((rows, LANES), jnp.float32),
            pltpu.VMEM((LANES // channels, channels, rows), jnp.bfloat16),
            pltpu.VMEM((rows + (TAPS - 1) * SUB, LANES), jnp.float32),
            pltpu.VMEM((UNROLL * SUB + (TAPS - 1) * SUB, LANES), jnp.float32),
            pltpu.VMEM((sources, tokens, 128), jnp.float32),
            pltpu.VMEM((rows + (TAPS - 1) * SUB, LANES), jnp.float32),
            pltpu.VMEM((rows, LANES), jnp.float32),
            pltpu.VMEM((rows, LANES), jnp.float32),
            pltpu.VMEM((rows, LANES), jnp.float32),
            pltpu.SemaphoreType.DMA((4,)),
        ],
        in_specs=[pl.BlockSpec(memory_space=pltpu.VMEM)] * 5
        + [pl.BlockSpec(memory_space=pl.ANY)] * 4,
        compiler_params=pltpu.CompilerParams(vmem_limit_bytes=VMEM_LIMIT),
        cost_estimate=pl.CostEstimate(
            flops=0, bytes_accessed=0, transcendentals=0
        ),
        name="recurrence_backward",
    )(data, slot, slot_columns(slot), offset, params, inputs, filtered, decay, hidden)


def arrangement(lengths, permutation, sources, channels):
    total = permutation.shape[0]
    groups = LANES // channels
    rows = total // groups
    steps = rows // SUB
    chunk = permutation // steps
    slot = (chunk // SUB) * rows + (permutation % steps) * SUB + chunk % SUB
    seq_ends = jnp.cumsum(lengths)
    seq_starts = seq_ends - lengths
    row, lane = np.arange(rows), np.arange(LANES)
    of_row = jnp.asarray((row % SUB) * steps + row // SUB, jnp.int32)
    of_lane = jnp.asarray((lane // channels) * (SUB * steps), jnp.int32)
    position = of_row[:, None] + of_lane[None, :]
    seg_first = jnp.zeros_like(position)
    for k in range(lengths.shape[0]):
        start = seq_starts[k]
        seg_first = jnp.where(position >= start, start, seg_first)
    offset = jnp.minimum(position - seg_first, TAPS - 1).astype(jnp.float32)
    return slot.reshape(sources, 1, total // sources), offset


def lane_params(conv_weight, conv_bias, gate_weight, gate_bias, decay_logits):
    stacked = jnp.concatenate(
        [
            conv_weight,
            conv_bias[None],
            gate_weight,
            gate_bias,
            RATE_SCALE * jax.nn.softplus(-decay_logits)[None],
        ]
    )
    return jnp.tile(stacked, (1, LANES // stacked.shape[1]))


def channel_sums(sums, channels, decay_logits):
    sums = jnp.sum(sums, axis=1).reshape(TAPS + 6, LANES // channels, channels).sum(axis=1)
    logit = -RATE_SCALE * jax.nn.sigmoid(-decay_logits)[None] * sums[TAPS + 5 :]
    return jnp.concatenate([sums[: TAPS + 5], logit])


def swap_core(values):
    return lax.ppermute(values, "fsdp", [(0, 1), (1, 0)])


def swap_bit(values, bit):
    count = lax.axis_size("seq")
    return lax.ppermute(values, "seq", [(i, i ^ (1 << bit)) for i in range(count)])


def half(values, index, axis):
    size = values.shape[axis] // 2
    return lax.dynamic_slice_in_dim(values, index * size, size, axis)


def reorder_blocks(values, low_bit, high_bit, axis):
    width = high_bit - low_bit
    size = values.shape[axis] >> width
    pieces = []
    for place in range(1 << width):
        natural = sum(((place >> (width - 1 - k)) & 1) << k for k in range(width))
        pieces.append(lax.slice_in_dim(values, natural * size, (natural + 1) * size, axis=axis))
    return jnp.concatenate(pieces, axis=axis)


def trade_channels(values):
    return lax.all_to_all(values, "seq", split_axis=0, concat_axis=0, tiled=True)


def after(values, *earlier):
    return lax.optimization_barrier((values,) + earlier)[0]


def product(subscripts, left, right):
    return jnp.einsum(subscripts, left, right, preferred_element_type=jnp.float32)


class Links:
    def __init__(self, place, core):
        count = lax.axis_size("seq").bit_length() - 1
        self.core = core
        self.bits = [(place >> bit) & 1 for bit in range(count)]

    def own(self, link):
        return self.core if link == "core" else self.bits[link]

    def swap(self, link, values, *earlier):
        if earlier:
            values = after(values, *earlier)
        return swap_core(values) if link == "core" else swap_bit(values, link)


class Chain:
    def __init__(self, links, terms, sums, collects=(), turn=False, rider=None):
        self.links, self.terms, self.rider = links, list(terms), rider
        self.sums, self.collects, self.turn = list(sums), list(collects), turn
        self.send()

    def total(self):
        return sum(term.astype(jnp.float32) for term in self.terms)

    def send(self):
        if self.sums:
            self.link, self.axis = self.sums[0]
        elif self.collects:
            total = self.total()
            self.terms = [total.T if self.turn else total]
            self.turn = False
            self.link, self.axis = self.collects[0], 0
        else:
            return
        own_bit = self.links.own(self.link)
        sent = sum(half(term, 1 - own_bit, self.axis).astype(jnp.float32) for term in self.terms)
        self.sent = sent.astype(jnp.bfloat16)
        self.other = self.links.swap(self.link, self.sent)
        self.terms = [half(term, own_bit, self.axis) for term in self.terms]
        if self.rider is not None:
            self.rider_other = self.links.swap(self.link, self.rider)

    def advance(self, token):
        other = after(self.other, token)
        if self.rider is not None:
            self.rider = self.rider + after(self.rider_other, token)
        if self.sums:
            self.terms.append(other)
            self.sums.pop(0)
        else:
            own, other = self.terms[0], other.astype(jnp.float32)
            first = self.links.own(self.link) == 0
            low, high = jnp.where(first, own, other), jnp.where(first, other, own)
            self.terms = [jnp.concatenate([low, high], axis=1)]
            self.collects.pop(0)
        if not self.sums and not self.collects:
            return token
        self.send()
        return self.sent


def both_cores(values, *earlier):
    return lax.all_gather(after(values, *earlier) if earlier else values, "fsdp")


def pick(values, *index):
    for place in index:
        values = lax.dynamic_index_in_dim(values, place, 0, keepdims=False)
    return values


def largest_tile(size, most, step):
    return max(tile for tile in range(step, most + 1, step) if size % tile == 0)


def grad_kernel(count, turned, select_ref, *refs):
    per_piece = turned or 1
    lefts = [ref[...] for ref in refs[: count * per_piece]]
    rights = [ref[...] for ref in refs[count * per_piece : count * (per_piece + 1)]]
    rights = jnp.concatenate(rights, axis=0)
    if turned:
        if per_piece > 1:
            lefts = [
                jnp.concatenate(lefts[k * per_piece : (k + 1) * per_piece], axis=1)
                for k in range(count)
            ]
        total = lax.dot_general(
            jnp.concatenate(lefts, axis=0),
            rights,
            (((0,), (0,)), ((), ())),
            preferred_element_type=jnp.float32,
        )
    else:
        total = jnp.dot(
            jnp.concatenate(lefts, axis=1), rights, preferred_element_type=jnp.float32
        )
    for ref in refs[count * (per_piece + 1) : -1]:
        total = total + ref[...].astype(jnp.float32)
    refs[-1][...] = total.astype(jnp.bfloat16)


(CORE, OTHER_CORE), (X, OTHER_X), (Y, OTHER_Y), (LOW, OTHER_LOW), (TOP, OTHER_TOP) = (
    (("scalar", 2 * k), ("scalar", 2 * k + 1)) for k in range(5)
)


def grad_product(select, pieces, rows, row_half=None, added=None, columns=None, counted=False):
    cols = pieces[0][2].shape[-1]
    tile_rows = largest_tile(rows, 1024, 16) if columns is None else rows // columns[0]
    tile_cols = largest_tile(cols, 512 if columns is None else 768, 256)

    def entry(index, select_ref):
        return select_ref[index[1]] if isinstance(index, tuple) else index

    def left_spec(left, lead):
        def place(m, n, select_ref):
            start = 0 if row_half is None else entry(row_half, select_ref) * (rows // tile_rows)
            return tuple(entry(i, select_ref) for i in lead) + (start + m, 0)

        return pl.BlockSpec((None,) * len(lead) + (tile_rows, left.shape[-1]), place)

    def column_spec(left, lead, which):
        def place(m, n, select_ref):
            block = columns[2](m, partial(entry, select_ref=select_ref))[which]
            return tuple(entry(i, select_ref) for i in lead) + (0, block)

        return pl.BlockSpec((None,) * len(lead) + (left.shape[-2], columns[1]), place)

    def right_spec(right, lead):
        def place(m, n, select_ref):
            return tuple(entry(i, select_ref) for i in lead) + (0, n)

        return pl.BlockSpec((None,) * len(lead) + (right.shape[-2], tile_cols), place)

    out_spec = pl.BlockSpec((tile_rows, tile_cols), lambda m, n, select_ref: (m, n))
    turned = 0 if columns is None else tile_rows // columns[1]
    if turned:
        in_specs = [column_spec(p[0], p[1], which) for p in pieces for which in range(turned)]
        operands = [p[0] for p in pieces for _ in range(turned)]
    else:
        in_specs = [left_spec(left, lead) for left, lead, _, _ in pieces]
        operands = [left for left, _, _, _ in pieces]
    in_specs += [right_spec(right, lead) for _, _, right, lead in pieces]
    operands += [right for _, _, right, _ in pieces]
    if added is not None:
        in_specs.append(out_spec)
        operands.append(added)
    return pl.pallas_call(
        partial(grad_kernel, len(pieces), turned),
        out_shape=jax.ShapeDtypeStruct((rows, cols), jnp.bfloat16),
        grid_spec=pltpu.PrefetchScalarGridSpec(
            num_scalar_prefetch=1,
            grid=(rows // tile_rows, cols // tile_cols),
            in_specs=in_specs,
            out_specs=out_spec,
        ),
        compiler_params=pltpu.CompilerParams(vmem_limit_bytes=VMEM_LIMIT),
        cost_estimate=pl.CostEstimate(
            flops=counted * 2 * rows * cols * sum(p[2].shape[-2] for p in pieces),
            bytes_accessed=counted * 2 * rows * cols,
            transcendentals=0,
        ),
        name="weight_grad",
    )(select, *operands)


GELU_SCALE = 0.7978845608028654
GELU_CUBE = 0.044715
HIDDEN_TILE = 512


def mlp_kernel(
    bits_ref, normed_ref, down_grad_ref, gate_ref, up_ref, down_ref,
    branch_ref, normed_grad_ref, mixed_ref, sent_gate_ref, sent_up_ref, kept_gate_ref, kept_up_ref,
):
    step = pl.program_id(0)
    by_columns = (((1,), (1,)), ((), ()))
    normed = normed_ref[...]
    first = jnp.dot(normed, gate_ref[...], preferred_element_type=jnp.float32)
    second = jnp.dot(normed, up_ref[...], preferred_element_type=jnp.float32)
    mixed_grad = lax.dot_general(
        down_grad_ref[...], down_ref[...], by_columns, preferred_element_type=jnp.float32
    )
    square = first * first
    bend = jnp.tanh(GELU_SCALE * first * (1.0 + GELU_CUBE * square))
    rise = 0.5 + 0.5 * bend
    gelu = first * rise
    slope = rise + 0.5 * GELU_SCALE * first * (1.0 - bend * bend) * (
        1.0 + 3.0 * GELU_CUBE * square
    )
    mixed = gelu * second
    first_low = (mixed_grad * slope * second).astype(jnp.bfloat16)
    second_low = (mixed_grad * gelu).astype(jnp.bfloat16)
    mixed_ref[...] = mixed.T.astype(jnp.bfloat16)

    side = (step // (pl.num_programs(0) // 4)) % 2
    for which, low, sent_ref, kept_ref in (
        (0, first_low, sent_gate_ref, kept_gate_ref),
        (1, second_low, sent_up_ref, kept_up_ref),
    ):

        @pl.when(side != bits_ref[which])
        def _(low=low, sent_ref=sent_ref):
            sent_ref[...] = low

        @pl.when(side == bits_ref[which])
        def _(low=low, kept_ref=kept_ref):
            kept_ref[...] = low

    @pl.when(step == 0)
    def _():
        branch_ref[...] = jnp.zeros_like(branch_ref)
        normed_grad_ref[...] = jnp.zeros_like(normed_grad_ref)

    branch_ref[...] += jnp.dot(
        mixed.astype(jnp.bfloat16), down_ref[...], preferred_element_type=jnp.float32
    )
    normed_grad_ref[...] += lax.dot_general(
        first_low, gate_ref[...], by_columns, preferred_element_type=jnp.float32
    ) + lax.dot_general(second_low, up_ref[...], by_columns, preferred_element_type=jnp.float32)


def mlp_both_ways(bits, normed, down_grad, w_gate, w_up, w_down):
    count, width = normed.shape
    hidden = w_gate.shape[1]
    steps = hidden // HIDDEN_TILE
    tiles = steps // 4

    whole = pl.BlockSpec((count, width), lambda t, bits_ref: (0, 0))
    column = pl.BlockSpec((width, HIDDEN_TILE), lambda t, bits_ref: (0, t))
    row = pl.BlockSpec((HIDDEN_TILE, width), lambda t, bits_ref: (t, 0))
    turned = pl.BlockSpec((HIDDEN_TILE, count), lambda t, bits_ref: (t, 0))

    def traded(which, kept):
        def place(t, bits_ref):
            wanted = bits_ref[which] if kept else 1 - bits_ref[which]
            side = (t // tiles) % 2
            resting = jnp.where(wanted == 0, tiles - 1, 0)
            return (t // (2 * tiles), 0, jnp.where(side == wanted, t % tiles, resting))

        return pl.BlockSpec((None, count, HIDDEN_TILE), place)

    summed = jax.ShapeDtypeStruct((count, width), jnp.float32)
    return pl.pallas_call(
        mlp_kernel,
        out_shape=(summed, summed, jax.ShapeDtypeStruct((hidden, count), jnp.bfloat16))
        + (jax.ShapeDtypeStruct((2, count, hidden // 4), jnp.bfloat16),) * 4,
        grid_spec=pltpu.PrefetchScalarGridSpec(
            num_scalar_prefetch=1,
            grid=(steps,),
            in_specs=[whole, whole, column, column, row],
            out_specs=[whole, whole, turned]
            + [traded(which, kept) for kept in (False, True) for which in (0, 1)],
        ),
        compiler_params=pltpu.CompilerParams(vmem_limit_bytes=VMEM_LIMIT),
        cost_estimate=pl.CostEstimate(flops=0, bytes_accessed=0, transcendentals=0),
        name="mlp_both_ways",
    )(jnp.stack(bits).astype(jnp.int32), normed, down_grad, w_gate, w_up, w_down)


MIDDLE_TILE = 512


def middle_kernel(
    core_ref, normed_grad_ref, middle_ref, cotangent_ref, gain_ref, output_ref, own_ref, other_ref,
    state_ref, pre_ref,
    middle_grad_ref, out_grad_ref, gain_grad_ref, state_grad_ref, gate_grad_ref, back_ref,
):
    by_columns = (((1,), (1,)), ((), ()))

    @pl.when(pl.program_id(0) == 0)
    def _():
        middle = middle_ref[...]
        normed_grad = normed_grad_ref[...]
        inverse = lax.rsqrt(jnp.mean(middle * middle, axis=1, keepdims=True) + NORM_EPS)
        scaled = normed_grad * gain_ref[...]
        lean = jnp.mean(scaled * middle, axis=1, keepdims=True)
        total = cotangent_ref[...] + inverse * scaled - middle * (inverse * inverse * inverse * lean)
        middle_grad_ref[...] = total
        out_grad_ref[...] = total.astype(jnp.bfloat16)
        gain_grad_ref[...] = jnp.sum(normed_grad * middle * inverse, axis=0, keepdims=True)
        back_ref[...] = jnp.zeros_like(back_ref)

    grad = lax.dot_general(
        output_ref[...], out_grad_ref[...], by_columns, preferred_element_type=jnp.float32
    )
    pre = pre_ref[...]
    square = pre * pre
    bend = jnp.tanh(GELU_SCALE * pre * (1.0 + GELU_CUBE * square))
    rise = 0.5 + 0.5 * bend
    slope = rise + 0.5 * GELU_SCALE * pre * (1.0 - bend * bend) * (1.0 + 3.0 * GELU_CUBE * square)
    state_grad_ref[...] = (grad * pre * rise).astype(jnp.bfloat16)
    gate_grad = (grad * state_ref[...].astype(jnp.float32) * slope).astype(jnp.bfloat16)
    gate_grad_ref[...] = gate_grad
    width = own_ref.shape[0]
    for ref, place in ((own_ref, core_ref[0]), (other_ref, 1 - core_ref[0])):
        columns = pl.ds(pl.multiple_of(place * width, width), width)
        back_ref[:, columns] += lax.dot_general(
            gate_grad, ref[...], (((0,), (1,)), ((), ())), preferred_element_type=jnp.float32
        )


def middle_backward(core, normed_grad, middle, cotangent, gain, w_output, own, other, states, pre):
    count, width = middle.shape
    channels = w_output.shape[0]
    whole = pl.BlockSpec((count, width), lambda t, core_ref: (0, 0))
    line = pl.BlockSpec((1, width), lambda t, core_ref: (0, 0))
    row = pl.BlockSpec((MIDDLE_TILE, width), lambda t, core_ref: (t, 0))
    column = pl.BlockSpec((width // 2, MIDDLE_TILE), lambda t, core_ref: (0, t))
    turned = pl.BlockSpec((MIDDLE_TILE, count), lambda t, core_ref: (t, 0))
    wide = jax.ShapeDtypeStruct((count, width), jnp.float32)
    low = jax.ShapeDtypeStruct((channels, count), jnp.bfloat16)
    return pl.pallas_call(
        middle_kernel,
        out_shape=(
            wide,
            jax.ShapeDtypeStruct((count, width), jnp.bfloat16),
            jax.ShapeDtypeStruct((1, width), jnp.float32),
            low,
            low,
            wide,
        ),
        grid_spec=pltpu.PrefetchScalarGridSpec(
            num_scalar_prefetch=1,
            grid=(channels // MIDDLE_TILE,),
            in_specs=[whole, whole, whole, line, row, column, column, turned, turned],
            out_specs=[whole, whole, line, turned, turned, whole],
        ),
        compiler_params=pltpu.CompilerParams(vmem_limit_bytes=VMEM_LIMIT),
        cost_estimate=pl.CostEstimate(flops=0, bytes_accessed=0, transcendentals=0),
        name="middle_backward",
    )(core.astype(jnp.int32).reshape(1), normed_grad, middle, cotangent, gain, w_output, own, other, states, pre)


class Traded:
    def __init__(self, links, channel_grad):
        channels, count = channel_grad.shape
        self.links = links
        self.mine = channel_grad.reshape(2, 2, channels // 4, count)
        self.by_core = links.swap("core", pick(self.mine, 1 - links.core))

    def trade_x(self, token):
        core, other = self.links.core, 1 - self.links.bits[0]
        self.by_core = after(self.by_core, token)
        sent = jnp.stack([pick(self.mine, core, other), pick(self.by_core, other)])
        self.by_x = self.links.swap(0, sent)
        return sent

    def grad(self, select, normed_pieces):
        lefts = [(self.mine, (CORE, X)), (self.by_core, (X,)), (self.by_x, (0,)), (self.by_x, (1,))]
        pieces = [left + right for left, right in zip(lefts, normed_pieces)]
        return grad_product(select, pieces, self.mine.shape[2])


def per_device(
    tokens,
    cotangent,
    gate_proj,
    input_proj,
    output_proj,
    mlp_gate,
    mlp_up,
    mlp_down,
    gain_a,
    gain_b,
    conv_weight,
    conv_bias,
    gate_weight,
    gate_bias,
    decay_logits,
    lengths,
    permutation,
):
    w_input, w_output, w_mlpgate, w_mlpup, w_down = (
        lax.all_gather(input_proj, "fsdp", axis=0, tiled=True),
        lax.all_gather(output_proj, "fsdp", axis=0, tiled=True),
        lax.all_gather(mlp_gate, "fsdp", axis=0, tiled=True),
        lax.all_gather(mlp_up, "fsdp", axis=0, tiled=True),
        lax.all_gather(mlp_down, "fsdp", axis=0, tiled=True),
    )
    core = lax.axis_index("fsdp")
    place = lax.axis_index("seq")
    links = Links(place, core)
    x, y = links.bits[0], links.bits[1]
    bit_count = len(links.bits)
    top = bit_count - 1
    low = links.bits[2]
    own_bits = (core, x, y, low, links.bits[top])
    select = jnp.stack([value for bit in own_bits for value in (bit, 1 - bit)]).astype(jnp.int32)
    channels = decay_logits.shape[0]
    count, width = tokens.shape
    block_shape = (lax.axis_size("seq"), channels, count)
    gains = jnp.stack([gain_a, gain_b])
    other_gains = links.swap("core", gains)
    full_gain_a, full_gain_b = jnp.where(
        core == 0,
        jnp.concatenate([gains, other_gains], axis=1),
        jnp.concatenate([other_gains, gains], axis=1),
    )
    other_input = links.swap("core", input_proj)
    other_gate = links.swap("core", gate_proj)
    normed_a, norm_back_a = jax.vjp(rms_norm, tokens, full_gain_a.astype(jnp.float32))
    normed_a_low = normed_a.astype(jnp.bfloat16)
    down_grad = cotangent.astype(jnp.bfloat16)
    input_pre = product("td,dr->rt", half(normed_a_low, core, 1), input_proj)
    input_pre = input_pre + product("td,dr->rt", half(normed_a_low, 1 - core, 1), other_input)
    input_low = input_pre.astype(jnp.bfloat16)
    channel_in = trade_channels(input_low)
    late_lengths, late_permutation = after((lengths, permutation), input_low)
    slot, offset = arrangement(late_lengths[0], late_permutation[0], block_shape[0], channels)
    params = lane_params(conv_weight, conv_bias, gate_weight, gate_bias, decay_logits)
    normed_late = after(normed_a_low, offset, slot, params)
    gate_pre = product("td,dr->rt", half(normed_late, core, 1), gate_proj)
    gate_pre = gate_pre + product("td,dr->rt", half(normed_late, 1 - core, 1), other_gate)
    normed_order = reorder_blocks(normed_a_low, 1, bit_count, 1)
    normed_core = both_cores(normed_order, channel_in)
    channel_in, gate_pre = lax.optimization_barrier((channel_in, gate_pre))
    down_y = links.swap(1, down_grad, channel_in)
    normed_x = links.swap(0, normed_order, channel_in)
    states, *kept = recurrence_forward(channel_in.reshape(block_shape), slot, offset, params)
    states = after(states, normed_x, down_y)
    state_tokens = trade_channels(states.reshape(input_pre.shape))
    normed_both = both_cores(normed_x, states)
    normed_pieces = [(normed_order, ()), (normed_core, (OTHER_CORE,))]
    normed_pieces += [(normed_x, ()), (normed_both, (OTHER_CORE,))]
    gated_low = gated_state(state_tokens.astype(jnp.float32), gate_pre).astype(jnp.bfloat16)
    branch_a = product("rt,rd->td", gated_low, w_output)
    middle = tokens + branch_a
    gain_b_wide = full_gain_b.astype(jnp.float32)
    normed_b_low = rms_norm(middle, gain_b_wide).astype(jnp.bfloat16)
    rows_total = gated_low.shape[0]
    shape = (2,) * bit_count + (2, rows_total // (2 << bit_count), count)
    rest = tuple(range(bit_count - 3, -1, -1))
    out_order = (2, 0, 1, *range(3, bit_count))
    dims = (bit_count, *(top - bit for bit in out_order), bit_count + 1, bit_count + 2)
    shape_out, dims_out = shape, dims
    fars = [links.swap(bit, normed_b_low) for bit in (0, 2)]
    down_top = links.swap(top, after(down_grad, normed_b_low))
    mlp_parts = mlp_both_ways((x, low), normed_b_low, down_grad, w_mlpgate, w_mlpup, w_down)
    arrived = lax.optimization_barrier((*mlp_parts, down_top, *fars))
    branch_b, normed_b_grad, mixed, sent_gate, sent_up, kept_gate, kept_up = arrived[:7]
    down_top, *fars = arrived[7:]
    hidden_far = [links.swap(0, sent_gate), links.swap(2, sent_up)]
    high = mixed.reshape((1 << (bit_count - 2), 2, mixed.shape[0] >> (bit_count - 1), count))
    mixed_send = lax.dynamic_index_in_dim(high, 1 - y, 1, keepdims=False)
    mixed_y = links.swap(1, mixed_send)
    output = middle + branch_b
    sums = jnp.stack(
        (
            jnp.sum(tokens * tokens),
            jnp.sum(branch_a * branch_a),
            jnp.sum(middle * middle),
            jnp.sum(branch_b * branch_b),
        )
    )
    entry_total = tokens.shape[0] * tokens.shape[1] * lax.axis_size("seq") * lax.axis_size("fsdp")
    middle_grad, out_grad_low, gain_b_grad, state_low, gate_low, gate_part = middle_backward(
        core,
        normed_b_grad,
        middle,
        cotangent,
        gain_b_wide[None],
        w_output,
        gate_proj,
        other_gate,
        state_tokens,
        gate_pre,
    )
    arrived = lax.optimization_barrier((state_low, gate_low, out_grad_low, *hidden_far, mixed_y))
    state_low, gate_low, out_grad_low, *hidden_far, mixed_y = arrived
    block = mixed.shape[0] // (2 << bit_count)
    axes = [top - bit for bit in (1, top)] + [bit_count] + [top - bit for bit in (0, *range(2, top))]
    mixed_mine = after(mixed, state_low).reshape((2,) * bit_count + (2, block, count))
    mixed_mine = mixed_mine.transpose(axes + [bit_count + 1, bit_count + 2])
    mixed_mine = mixed_mine.reshape(2, 2, 2, mixed.shape[0] // 8, count)
    axes = [0, bit_count - 1, bit_count - 2] + [top - bit for bit in range(2, top)]
    mixed_y = mixed_y.reshape((2,) * bit_count + (block, count))
    mixed_y = mixed_y.transpose(axes + [bit_count, bit_count + 1])
    mixed_y = mixed_y.reshape(2, 2, mixed.shape[0] // 8, count)
    gain_b_grad = gain_b_grad[0]
    channel_grad = trade_channels(state_low)

    normed_b_core = both_cores(normed_b_low)
    hidden_pieces = []
    for index in (0, 1):
        mine, far = (kept_gate, kept_up)[index], hidden_far[index]
        far_core = both_cores(fars[index], mixed_send)
        both = jnp.stack([pick(mine, 1 - core), pick(after(far, state_low), 1 - core)])
        by_core = links.swap("core", both)
        hidden_pieces.append(
            [
                (normed_b_low, (), mine, (CORE,)),
                (fars[index], (), far, (CORE,)),
                (normed_b_core, (OTHER_CORE,), by_core, (0,)),
                (far_core, (OTHER_CORE,), by_core, (1,)),
            ]
        )
    aligned = (width >> bit_count) % 128 == 0
    hidden_orders = ((1, (*range(2, bit_count),), 0), (0, (1, *range(3, bit_count)), 2))
    if not aligned:
        for pieces, (summed, between, traded_bit) in zip(hidden_pieces, hidden_orders):
            for k, (left, lead, right, right_lead) in enumerate(pieces):
                split = left.reshape(left.shape[:-1] + (2,) * bit_count + (width >> bit_count,))
                first = left.ndim - 1
                axes = [first + top - bit for bit in (summed, *between, traded_bit)]
                axes = tuple(range(first)) + tuple(axes) + (first + bit_count,)
                split = split.transpose(axes).reshape(left.shape)
                pieces[k] = (jnp.swapaxes(split, -1, -2), lead, right, right_lead)

    def hidden_product(index, half_rows, token, added=None, counted=False):
        chosen = after(select, token)
        if not aligned:
            return grad_product(chosen, hidden_pieces[index], width // 2, half_rows, added)
        summed, between, traded_bit = hidden_orders[index]

        def blocks(m, entry):
            found = []
            for tile in range(1 << len(between)):
                place = entry(half_rows) << summed
                for k, bit in enumerate(reversed(between)):
                    place = place + (((tile >> k) & 1) << bit)
                found += [place >> 1] if traded_bit == 0 else [place, place + (1 << traded_bit)]
            return found

        columns = (1, width >> (bit_count - (traded_bit == 0)), blocks)
        return grad_product(chosen, hidden_pieces[index], width // 2, None, added, columns, counted)

    rest_bits = range(2, bit_count)
    mixed_two = jnp.stack(
        [pick(mixed_mine, y, 1 - own_bits[4]), pick(mixed_y, 1 - own_bits[4])]
    )
    down_both = links.swap(1, down_top, state_low)
    down_pieces = [(piece, ()) for piece in (down_grad, down_y, down_top, down_both)]
    gate_traded = Traded(links, gate_low)
    gated_mine = after(gated_low, state_low).reshape(shape_out).transpose(dims_out)
    gated_mine = gated_mine.reshape(2, 2, rows_total // 4, count)
    gated_core = links.swap("core", pick(gated_mine, 1 - core))
    gated_two = jnp.stack([pick(gated_mine, core, 1 - low), pick(gated_core, 1 - low)])
    gate_sent = hidden_product(0, OTHER_Y, gated_two, None, True)
    up_sent = hidden_product(1, OTHER_X, gate_sent, None, True)
    channel_grad = after(channel_grad, mixed_two, up_sent, gate_traded.by_core, down_both)
    gate_received = links.swap(1, gate_sent, channel_grad)
    up_received = links.swap(0, up_sent, channel_grad)
    mixed_far = links.swap(top, mixed_two, channel_grad)
    out_far = links.swap(2, out_grad_low, channel_grad)
    channel_grad = after(channel_grad, up_sent)

    dealt_grad, lane_sums = recurrence_backward(
        channel_grad.reshape(block_shape), slot, offset, params, *kept
    )
    dealt_grad = after(dealt_grad, out_far)
    input_grad = trade_channels(dealt_grad.reshape(state_low.shape))
    def down_product(chosen, token, added=None):
        lefts = [(mixed_mine, (Y, TOP, chosen)), (mixed_y, (TOP, chosen))]
        lefts += [(mixed_far, (k, chosen)) for k in range(2)]
        pieces = [left + right for left, right in zip(lefts, down_pieces)]
        return grad_product(after(select, token), pieces, mixed.shape[0] // 8, None, added)

    hidden_sums = [(bit, 0) for bit in rest_bits]
    projection_sums = [(bit, 1) for bit in range(1, bit_count)]
    token = after(dealt_grad, gate_received, up_received, mixed_far)
    gate_total = hidden_product(0, Y, token, gate_received)
    gated_far = links.swap(2, gated_two, gate_total)
    token = gate_traded.trade_x(gate_total)
    gate_chain = Chain(links, [gate_total], hidden_sums, (0, "core"))
    up_total = hidden_product(1, X, token, up_received)
    up_sums = [(bit, 0) for bit in (1, *range(3, bit_count))]
    up_chain = Chain(links, [up_total], up_sums, (2, "core"))
    down_sent = down_product(OTHER_CORE, up_total)
    down_received = links.swap("core", down_sent)
    input_grad = after(input_grad, down_sent)
    input_traded = Traded(links, input_grad)
    token = input_traded.trade_x(input_grad)
    out_core = both_cores(out_grad_low, dealt_grad)
    out_both = both_cores(out_far, dealt_grad)
    out_pieces = [
        (gated_mine, (CORE, LOW), out_grad_low, ()),
        (gated_core, (LOW,), out_core, (OTHER_CORE,)),
        (gated_far, (0,), out_far, ()),
        (gated_far, (1,), out_both, (OTHER_CORE,)),
    ]
    down_total = down_product(CORE, token, down_received)
    input_total = input_traded.grad(after(select, down_total), normed_pieces)
    input_chain = Chain(links, [input_total], projection_sums, (0, "core"), True)
    down_total = after(down_total, input_chain.sent)
    down_chain = Chain(links, [down_total], [(bit, 0) for bit in (0, *range(2, top))])
    token = gate_chain.advance(down_chain.sent)
    token = up_chain.advance(token)
    input_grad = after(input_grad, token)
    normed_a_grad = gate_part + product("rt,dr->td", input_grad, w_input)
    token_norm_grad, gain_a_grad = norm_back_a(normed_a_grad)
    token_grad = middle_grad + token_norm_grad
    small = jnp.concatenate([gain_a_grad, gain_b_grad, sums])
    gate_proj_total = gate_traded.grad(after(select, token_grad), normed_pieces)
    token = input_chain.advance(gate_proj_total)
    gate_proj_total = after(gate_proj_total, token)
    gate_proj = Chain(links, [gate_proj_total], projection_sums, (0, "core"), True, small)
    out_sent = grad_product(after(select, gate_proj.sent), out_pieces, rows_total // 8, OTHER_X)
    token = down_chain.advance(out_sent)
    out_received = links.swap(0, out_sent, token)
    token = input_chain.advance(token)
    token = gate_chain.advance(token)
    token = gate_proj.advance(token)
    token = up_chain.advance(token)
    token = input_chain.advance(token)
    out_total = grad_product(after(select, token), out_pieces, rows_total // 8, X, out_received)
    out_chain = Chain(links, [out_total], up_sums)
    token = gate_proj.advance(out_total)
    chains = [gate_chain, down_chain, input_chain, out_chain, gate_proj, up_chain]
    while any(chain.sums or chain.collects for chain in chains):
        for chain in chains:
            if chain.sums or chain.collects:
                token = chain.advance(token)
    param_sums = channel_sums(lane_sums, channels, decay_logits)
    param_sums = param_sums + links.swap("core", after(param_sums, up_sent))
    totals = gate_proj.rider
    gain_size = width // (lax.axis_size("seq") * lax.axis_size("fsdp"))
    gain_start = (place * lax.axis_size("fsdp") + core) * gain_size
    return (
        output,
        token_grad,
        gate_proj.total(),
        input_chain.total(),
        out_chain.total(),
        gate_chain.total(),
        up_chain.total(),
        down_chain.total(),
        lax.dynamic_slice_in_dim(totals, gain_start, gain_size, 0),
        lax.dynamic_slice_in_dim(totals, width + gain_start, gain_size, 0),
        param_sums[:TAPS],
        param_sums[TAPS],
        param_sums[TAPS + 1 : TAPS + 3],
        param_sums[TAPS + 3 : TAPS + 5],
        param_sums[TAPS + 5],
        jnp.sqrt(totals[2 * width :] / entry_total),
    )


def solution(mesh):
    in_specs = (
        P(("seq", "fsdp"), None),
        P(("seq", "fsdp"), None),
        P("fsdp", None),
        P("fsdp", None),
        P("fsdp", None),
        P("fsdp", None),
        P("fsdp", None),
        P("fsdp", None),
        P("fsdp"),
        P("fsdp"),
        P(None, "seq"),
        P("seq"),
        P(None, "seq"),
        P(None, "seq"),
        P("seq"),
        P("fsdp", None),
        P("fsdp", None),
    )
    out_specs = (
        P(("seq", "fsdp"), None),
        P(("seq", "fsdp"), None),
        P(("seq", "fsdp"), None),
        P(("seq", "fsdp"), None),
        P(("seq", "fsdp"), None),
        P(("seq", "fsdp"), None),
        P(("seq", "fsdp"), None),
        P(("seq", "fsdp"), None),
        P(("seq", "fsdp")),
        P(("seq", "fsdp")),
        P(None, "seq"),
        P("seq"),
        P(None, "seq"),
        P(None, "seq"),
        P("seq"),
        P(),
    )
    return jax.shard_map(
        per_device, mesh=mesh, in_specs=in_specs, out_specs=out_specs, check_vma=False
    )
```
